128 devices in a mesh: seq: 64 (over y, x_hi, z, core), row: 2 (over x_lo).
Axes of the slice: x: 4 (x_hi: 2, x_lo: 2; x = x_hi * 2 + x_lo), y: 4, z: 4, core: 2. Of those that a mesh axis runs over, the one named last changes fastest.
Arguments:
- inputs: bfloat16 [2, 8192, 1024], P(None, 'seq'), may hold values from -6 to 6
- memory: bfloat16 [2, 8192, 1024], P(None, 'seq'), may hold values from -6 to 6
- cotangent: bfloat16 [2, 8192, 1024], P(None, 'seq'), may hold values from -6 to 6
- doc_lens: int32 [2, 32], replicated, may hold values from 1 to 1024, 8192 in all within a row
- counts: int32 [2, 64], replicated, may hold values from 32 to 128, as said below
- prefix_kv: bfloat16 [2, 30, 1024], P(None, None, 'row'), may hold values from -6 to 6
- self_qkv: bfloat16 [1024, 3, 1024], P(None, None, 'row'), may hold values from -0.1875 to 0.1875
- self_out: bfloat16 [1024, 1024], P('row'), may hold values from -1.5 to 1.5
- cross_q: bfloat16 [1024, 1024], P(None, 'row'), may hold values from -0.1875 to 0.1875
- cross_kv: bfloat16 [1024, 2, 1024], P(None, None, 'row'), may hold values from -0.1875 to 0.1875
- cross_out: bfloat16 [1024, 1024], P('row'), may hold values from -1.5 to 1.5
- norm_gains: float32 [3, 1024], replicated, may hold values from 0.5 to 1.5
- fc_in: bfloat16 [1024, 4096], P(None, 'row'), may hold values from -0.1875 to 0.1875
- fc_out: bfloat16 [4096, 1024], P('row'), may hold values from -0.09375 to 0.09375
- down_w: bfloat16 [1024, 512], P(None, 'row'), may hold values from -0.1875 to 0.1875
- down_b: float32 [512], P('row'), may hold values from -3 to 3
- up_w: bfloat16 [512, 1024], P('row'), may hold values from -0.0625 to 0.0625
- up_b: float32 [1024], replicated, may hold values from -0.6 to 0.6
Outputs:
- layer_out: bfloat16 [2, 8192, 1024], P(None, 'seq')
- input_grad: bfloat16 [2, 8192, 1024], P(None, 'seq')
- memory_grad: bfloat16 [2, 8192, 1024], P(None, 'seq')
- prefix_grad: float32 [2, 30, 1024], P(None, None, 'row')
- down_grad: float32 [1024, 512], P(None, 'row')
- down_bias_grad: float32 [512], P('row')
- up_grad: float32 [512, 1024], P('row')
- up_bias_grad: float32 [1024], replicated
The draws below stay inside these ranges and needn't reach their ends.
Inputs may be any that keep to these rules, and one draw needn't show every extreme that they name: `counts`: live slots stand first among the 128 slots of an index of seq; in every micro-batch one index holds 128 live slots and one a quarter of 128. `doc_lens`: the 32 lengths of a micro-batch sum to 8192; the largest is 1024.
All inputs are finite; a program needn't handle non-finite values.
Results may differ from the reference program's by a relative error of at most 0.024.
Values may be sent and summed in bfloat16 or wider, within the bound.
No kernel may reach another device: no remote copies, remote signals or barrier semaphores. Data moves between devices by JAX's collectives and lax.ppermute only.
A program may use at most 192 MiB of HBM per device.

```python
import math
import jax
import jax.numpy as jnp
import numpy as np
from jax import lax

D = 1024
H = 16
HEAD = 64
FF = 4096
A = 512
PREFIX = 30
MB = 2
DOC_MAX = 1024
TOK_DEV = 128
TOKENS = 8192
DOCS = 32
N_SEQ = 64


def draw_counts(key, part):
    key = jax.random.fold_in(key, 11)
    base_key, order_key = jax.random.split(key)
    base = jax.random.randint(base_key, (MB, N_SEQ), TOK_DEV // 4, TOK_DEV + 1)
    order = jax.vmap(lambda each_key: jax.random.permutation(each_key, N_SEQ))(jax.random.split(order_key, MB))
    position = jnp.arange(N_SEQ, dtype=jnp.int32)[None, :]
    filled = position == order[:, 0:1]
    lightest = position == order[:, 1:2]
    return jnp.where(filled, TOK_DEV, jnp.where(lightest, TOK_DEV // 4, base)).astype(jnp.int32)


def level_of(key, extent, cuts, smallest, largest):
    def one(dim, shards_of):
        draws = jax.random.uniform(jax.random.fold_in(jax.random.fold_in(key, 6), dim), (shards_of,), jnp.float32, smallest / len(cuts), largest / len(cuts))
        return jnp.repeat(jnp.exp(draws), extent[dim] // shards_of).reshape((-1,) + (1,) * (len(extent) - dim - 1))

    gain = one(*cuts[0])
    for cut in cuts[1:]:
        gain = gain * one(*cut)
    return gain


def profile(amount, total, most, skew):
    weights = [(1 << 20) // math.isqrt(rank ** skew) + 1 for rank in range(2, amount + 1)]
    rest, given = total - most - (amount - 1), [1] * (amount - 1)
    while rest > 0:
        movable = [i for i in range(amount - 1) if given[i] < most]
        whole, budget = sum([weights[i] for i in movable]), rest
        for i in movable:
            addition = min(most - given[i], max(1, budget * weights[i] // whole), rest)
            given[i] = given[i] + addition
            rest = rest - addition
    return np.array([most] + given)


def uneven(own_key, amount, total, most, lean):
    if amount == 2:
        one = jax.random.randint(own_key, (), max(1, total - most), min(most, total - 1) + 1)
        return jnp.stack([one, total - one])
    tallies = jnp.asarray(profile(amount, total, most, lean), jnp.int32)
    pairs = (amount - 1) // 2
    donor, taker = tallies[1:1 + 2 * pairs:2], tallies[2:2 + 2 * pairs:2]
    margin = jnp.minimum(donor - 1, most - taker)
    moved = jax.random.randint(jax.random.fold_in(own_key, 1), (pairs,), 0, 1 << 20) % (margin + 1)
    tallies = tallies.at[1:1 + 2 * pairs:2].set(donor - moved).at[2:2 + 2 * pairs:2].set(taker + moved)
    return tallies[jax.random.permutation(jax.random.fold_in(own_key, 2), amount)]


def gaussian(rng, dims, deviation, reach, pieces=(), kind=jnp.bfloat16):
    values = jax.random.normal(rng, dims, jnp.float32) * deviation
    if len(pieces) > 0:
        values = level_of(rng, dims, pieces, -0.22, 0.18) * values
    return jnp.clip(values, min=-reach, max=reach).astype(kind)


def setup_inputs(seed: int = 0) -> dict:
    splits = jax.random.split(jax.random.key(seed), 19)
    return {
        "inputs": gaussian(splits[0], (MB, TOKENS, D), 1.0, 6.0, ((1, 64),)),
        "memory": gaussian(splits[1], (MB, TOKENS, D), 1.0, 6.0, ((1, 64),)),
        "cotangent": gaussian(splits[2], (MB, TOKENS, D), 1.0, 6.0, ((1, 64),)),
        "doc_lens": jax.vmap(lambda own: uneven(own, DOCS, TOKENS, DOC_MAX, 2))(jax.random.split(splits[3], MB)).reshape((MB, DOCS)).astype(jnp.int32),
        "counts": draw_counts(jax.random.fold_in(splits[18], 71), 0),
        "prefix_kv": gaussian(splits[5], (2, PREFIX, D), 1.0, 6.0, ((2, 2),)),
        "self_qkv": gaussian(splits[6], (D, 3, D), D ** -0.5, 0.1875, ((2, 2),)),
        "self_out": gaussian(splits[7], (D, D), (D // 64) ** -0.5, 1.5, ((0, 2),)),
        "cross_q": gaussian(splits[8], (D, D), D ** -0.5, 0.1875, ((1, 2),)),
        "cross_kv": gaussian(splits[9], (D, 2, D), D ** -0.5, 0.1875, ((2, 2),)),
        "cross_out": gaussian(splits[10], (D, D), (D // 64) ** -0.5, 1.5, ((0, 2),)),
        "norm_gains": jnp.clip(1.0 + 0.1 * jax.random.normal(splits[11], (3, D), jnp.float32), 0.5, 1.5),
        "fc_in": gaussian(splits[12], (D, FF), D ** -0.5, 0.1875, ((1, 2),)),
        "fc_out": gaussian(splits[13], (FF, D), FF ** -0.5, 0.09375, ((0, 2),)),
        "down_w": gaussian(splits[14], (D, A), D ** -0.5, 0.1875, ((1, 2),)),
        "down_b": gaussian(splits[15], (A,), 0.5, 3.0, ((0, 2),), jnp.float32),
        "up_w": gaussian(splits[16], (A, D), (16 * A) ** -0.5, 0.0625, ((0, 2),)),
        "up_b": gaussian(splits[17], (D,), 0.1, 0.6, (), jnp.float32),
    }


@jax.custom_vjp
def low(v):
    return lax.optimization_barrier(v.astype(jnp.bfloat16)).astype(jnp.float32)

@jax.custom_vjp
def low_back(v):
    return v

def low_keep(v):
    return (low(v), None)

def low_pass(kept, grad):
    return (grad,)

def back_keep(v):
    return (v, None)

def back_low(kept, grad):
    return (low(grad),)
low.defvjp(low_keep, low_pass)
low_back.defvjp(back_keep, back_low)
HIGHEST_PRECISION = lax.Precision.HIGHEST
EPSILON = 1e-05
MASKED = -1000000000.0

def matmul(left, right):
    return jnp.dot(left, right, precision=HIGHEST_PRECISION)

def norm_rows(values, norm_gain):
    center = values - lax.optimization_barrier(jnp.mean(values, axis=-1, keepdims=True))
    spread = lax.optimization_barrier(jnp.mean(center * center, axis=-1, keepdims=True))
    return center * lax.rsqrt(spread + EPSILON) * norm_gain

def to_heads(values):
    return values.reshape(values.shape[0], H, HEAD)

def doc_of(slots, doc_ends):
    return lax.optimization_barrier(jnp.sum((doc_ends[None, :] <= slots[:, None]).astype(jnp.int32), axis=1)).astype(jnp.int32)

def attend(queries, keys, values, query_doc, key_doc, key_live, extra, causal):
    row_count = queries.shape[0]
    key_count = keys.shape[0]
    block_size = math.gcd(row_count, 512)
    block_count = row_count // block_size
    window = min(key_count, block_size + 2 * DOC_MAX)

    def each_block(block_index):
        first = (block_index * block_size).astype(jnp.int32)
        start = jnp.clip(first - DOC_MAX, 0, key_count - window).astype(jnp.int32)
        query_blk = lax.dynamic_slice_in_dim(queries, first, block_size, 0)
        doc_blk = lax.dynamic_slice_in_dim(query_doc, first, block_size, 0)
        keys_blk = lax.dynamic_slice_in_dim(keys, start, window, 0)
        values_blk = lax.dynamic_slice_in_dim(values, start, window, 0)
        key_doc_blk = lax.dynamic_slice_in_dim(key_doc, start, window, 0)
        live_blk = lax.dynamic_slice_in_dim(key_live, start, window, 0)
        query_slot = first + jnp.arange(block_size, dtype=jnp.int32)
        key_slot = start + jnp.arange(window, dtype=jnp.int32)
        scores = jnp.einsum('qhe,khe->hqk', query_blk, keys_blk, precision=HIGHEST_PRECISION)
        allowed = (doc_blk[:, None] == key_doc_blk[None, :]) & live_blk[None, :]
        if causal:
            allowed = allowed & (key_slot[None, :] <= query_slot[:, None])
        all_values = values_blk
        if extra is not None:
            extra_scores = jnp.einsum('qhe,khe->hqk', query_blk, extra[0], precision=HIGHEST_PRECISION)
            scores = jnp.concatenate([extra_scores, scores], axis=-1)
            always = jnp.zeros((block_size, extra[0].shape[0]), jnp.int32) == 0
            allowed = jnp.concatenate([always, allowed], axis=-1)
            all_values = jnp.concatenate([extra[1], values_blk], axis=0)
        scores = low_back(scores)
        scores = jnp.where(allowed[None], scores, MASKED)
        weights = jax.nn.softmax(scores, axis=-1)
        return jnp.einsum('hqk,khe->qhe', low(weights), all_values, precision=HIGHEST_PRECISION)
    result = lax.map(jax.checkpoint(each_block), jnp.arange(block_count, dtype=jnp.int32))
    return result.reshape(row_count, H * HEAD)

def layer(inputs, memory, prefix, down_w, down_b, up_w, up_b, frozen, doc_ids, live_slot):
    self_qkv, self_out, cross_q, cross_kv, cross_out, norm_gains, fc_in, fc_out = frozen
    queries = low_back(low(0.125 * matmul(inputs, self_qkv[:, 0, :])))
    keys = low_back(low(matmul(inputs, self_qkv[:, 1, :])))
    values = low_back(low(matmul(inputs, self_qkv[:, 2, :])))
    extra = (to_heads(prefix[0]), to_heads(prefix[1]))
    context = attend(to_heads(queries), to_heads(keys), to_heads(values), doc_ids, doc_ids, live_slot, extra, True)
    context = low_back(low(context))
    mixed = inputs + low_back(matmul(context, self_out))
    first_norm = norm_rows(mixed, norm_gains[0])
    first_low = low(first_norm)
    cross_queries = low_back(low(0.125 * matmul(first_low, cross_q)))
    mem_keys = low_back(low(matmul(memory, cross_kv[:, 0, :])))
    mem_values = low_back(low(matmul(memory, cross_kv[:, 1, :])))
    cross_context = attend(to_heads(cross_queries), to_heads(mem_keys), to_heads(mem_values), doc_ids, doc_ids, doc_ids >= 0, None, False)
    cross_context = low_back(low(cross_context))
    crossed = first_norm + low_back(matmul(cross_context, cross_out))
    second_norm = norm_rows(crossed, norm_gains[1])
    second_low = low(second_norm)
    hidden = low_back(matmul(second_low, fc_in))
    hidden_act = low(jax.nn.gelu(hidden, approximate=False))
    adapter_pre = low_back(matmul(second_low, down_w) + down_b)
    adapter_act = low(jax.nn.gelu(adapter_pre, approximate=False))
    branch = low_back(matmul(hidden_act, fc_out) + 4.0 * (matmul(adapter_act, up_w) + up_b))
    return norm_rows(second_norm + branch, norm_gains[2])

def reference(inputs, memory, cotangent, doc_lens, counts, prefix_kv, self_qkv, self_out, cross_q, cross_kv, cross_out, norm_gains, fc_in, fc_out, down_w, down_b, up_w, up_b):
    frozen = tuple((weight.astype(jnp.float32) for weight in (self_qkv, self_out, cross_q, cross_kv, cross_out, norm_gains, fc_in, fc_out)))
    slot_total = TOK_DEV * N_SEQ
    slot_index = jnp.arange(slot_total, dtype=jnp.int32)
    trained = (prefix_kv.astype(jnp.float32), down_w.astype(jnp.float32), down_b.astype(jnp.float32), up_w.astype(jnp.float32), up_b.astype(jnp.float32))
    totals = tuple((jnp.zeros(weight.shape, jnp.float32) for weight in trained))
    outputs = []
    input_grads = []
    memory_grads = []
    for micro_index in range(MB):
        live_slot = slot_index % TOK_DEV < jnp.repeat(counts[micro_index], TOK_DEV)
        doc_ends = jnp.cumsum(doc_lens[micro_index]).astype(jnp.int32)
        doc_ids = doc_of(slot_index, doc_ends)

        def forward(inputs_now, memory_now, prefix, weight_down, bias_down, weight_up, bias_up):
            return layer(inputs_now, memory_now, prefix, weight_down, bias_down, weight_up, bias_up, frozen, doc_ids, live_slot)
        result, pullback = jax.vjp(forward, inputs[micro_index].astype(jnp.float32), memory[micro_index].astype(jnp.float32), *trained)
        grads = pullback(cotangent[micro_index].astype(jnp.float32))
        outputs.append(result.astype(jnp.bfloat16))
        input_grads.append(grads[0].astype(jnp.bfloat16))
        memory_grads.append(grads[1].astype(jnp.bfloat16))
        totals = tuple((total_now + grad_now for total_now, grad_now in zip(totals, grads[2:])))
    return (jnp.stack(outputs), jnp.stack(input_grads), jnp.stack(memory_grads), totals[0], totals[1], totals[2], totals[3], totals[4])
```

```python
from functools import partial

import jax
import jax.numpy as jnp
from jax import lax
from jax.experimental import pallas as pl
from jax.experimental.pallas import tpu as pltpu
from jax.sharding import Mesh
from jax.sharding import PartitionSpec as P

HEAD = 64
EPSILON = 1e-05
MASKED = -1000000000.0
CHUNK = 256
BLOCK = 128
SEQ = ("y", "x_hi", "z", "core")
GROUP = ("z", "core")
WIDE_GROUP = ("z", "core", "row")
BF16 = jnp.bfloat16
F32 = jnp.float32


def dot(left, right):
    return jnp.dot(left, right, preferred_element_type=F32)


def norm_rows(values, norm_gain):
    center = values - jnp.mean(values, axis=-1, keepdims=True)
    inverse_std = lax.rsqrt(jnp.mean(center * center, axis=-1, keepdims=True) + EPSILON)
    normed = center * inverse_std
    return (normed * norm_gain, normed, inverse_std)


def norm_back(gradient, norm_gain, normed, inverse_std):
    scaled = gradient * norm_gain
    centered = scaled - jnp.mean(scaled, axis=-1, keepdims=True)
    return (centered - normed * jnp.mean(scaled * normed, axis=-1, keepdims=True)) * inverse_std


def gelu_both(pre_act):
    cdf = 0.5 * (1.0 + lax.erf(pre_act * 0.7071067811865476))
    slope = cdf + pre_act * (0.3989422804014327 * jnp.exp(-0.5 * pre_act * pre_act))
    return (pre_act * cdf, slope)


def row_total(partial_sum):
    low = partial_sum.astype(BF16)
    other = lax.ppermute(low, "row", [(0, 1), (1, 0)])
    return low.astype(F32) + other.astype(F32)


def shift_groups(value, by):
    devices = 64
    pairs = [(i, i + 8 * by) for i in range(devices) if 0 <= i + 8 * by < devices]
    return lax.ppermute(value, SEQ, pairs)


def regroup(value):
    return lax.all_to_all(value, GROUP, 0, 0)


def regroup_wide(value):
    return lax.all_to_all(value, WIDE_GROUP, 0, 0)


def flip(value, axis_name, bit):
    size = lax.axis_size(axis_name)
    return lax.ppermute(value, axis_name, [(i, i ^ bit) for i in range(size)])


def transposed(value):
    return value.astype(F32).T.astype(BF16)


def allowed_keys(limits, chunk, meta_ref, batch, live):
    keys = lax.broadcasted_iota(jnp.int32, (CHUNK, CHUNK), 0)
    low = limits[0:1, :] - chunk * CHUNK
    high = limits[1:2, :] - chunk * CHUNK
    allowed = (keys >= low) & (keys < high)
    if live:
        first = meta_ref[batch, 8 + 2 * chunk]
        second = meta_ref[batch, 9 + 2 * chunk] + BLOCK
        allowed = allowed & (keys < jnp.where(keys < BLOCK, first, second))
    return allowed


def prefix_mask(prefix_rows):
    return lax.broadcasted_iota(jnp.int32, (BLOCK, CHUNK), 0) < prefix_rows


def attend_kernel(kv_offsets, prefix_rows, copies, meta_ref, limits_ref, q_ref, *refs):
    kv_count = len(kv_offsets)
    kv_refs = refs[:kv_count]
    refs = refs[kv_count:]
    if prefix_rows:
        prefix_k_ref, prefix_vt_ref = refs[:2]
        refs = refs[2:]
    out_ref, full_ref, stats_ref, k_buf, vt_buf, qt_buf = refs
    batch, block = pl.program_id(0), pl.program_id(1)

    @pl.when(block == 0)
    def _():
        for part in range(kv_count):
            start = kv_offsets[part]
            for j in range(8):
                chunk, cols = 4 * part + j // 2, slice((j % 2) * BLOCK, (j % 2 + 1) * BLOCK)
                k_buf[chunk, cols, :] = transposed(kv_refs[part][j, start : start + HEAD, :])
                vt_buf[chunk, :, cols] = kv_refs[part][j, start + HEAD : start + 2 * HEAD, :]
        for j in range(8):
            cols = slice((j % 2) * BLOCK, (j % 2 + 1) * BLOCK)
            qt_buf[j // 2, :, cols] = q_ref[j, 0:HEAD, :]

    queries = qt_buf[block]
    limits = limits_ref[0, 0]
    if prefix_rows:
        scores = dot(prefix_k_ref[...], queries)
        scores = jnp.where(prefix_mask(prefix_rows), scores, MASKED)
        top = jnp.max(scores, axis=0, keepdims=True)
        weights = jnp.exp(scores - top)
        mass = jnp.sum(weights, axis=0, keepdims=True)
        total = dot(prefix_vt_ref[...], weights.astype(BF16))
    else:
        top = jnp.full((1, CHUNK), MASKED, F32)
        mass = jnp.zeros((1, CHUNK), F32)
        total = jnp.zeros((HEAD, CHUNK), F32)

    def step(chunk, carry):
        top, mass, total = carry
        scores = dot(k_buf[chunk], queries)
        allowed = allowed_keys(limits, chunk, meta_ref, batch, prefix_rows > 0)
        scores = jnp.where(allowed, scores, MASKED)
        new_top = jnp.maximum(top, jnp.max(scores, axis=0, keepdims=True))
        shrink = jnp.exp(top - new_top)
        weights = jnp.exp(scores - new_top)
        mass = mass * shrink + jnp.sum(weights, axis=0, keepdims=True)
        total = total * shrink + dot(vt_buf[chunk], weights.astype(BF16))
        return new_top, mass, total

    top, mass, total = lax.fori_loop(
        meta_ref[batch, block], meta_ref[batch, 4 + block], step, (top, mass, total)
    )
    inverse = 1.0 / mass
    context = total * inverse
    full_ref[0, 0] = context
    low = context.astype(BF16)
    for j in range(2):
        for copy in range(copies):
            out_ref[j * copies + copy] = low[:, j * BLOCK : (j + 1) * BLOCK]
    stats_ref[0, 0, 0:1, :] = top
    stats_ref[0, 0, 1:2, :] = inverse


def attend_back_kernel(kv_offsets, prefix_rows, copies, meta_ref, limits_ref, q_ref, *refs):
    kv_count = len(kv_offsets)
    kv_refs = refs[:kv_count]
    refs = refs[kv_count:]
    if prefix_rows:
        prefix_k_ref, prefix_kt_ref, prefix_v_ref = refs[:3]
        refs = refs[3:]
    grad_ref, full_ref, stats_ref = refs[:3]
    refs = refs[3:]
    dq_ref, dkv_refs = refs[0], refs[1 : 1 + kv_count]
    refs = refs[1 + kv_count :]
    if prefix_rows:
        dprefix_ref = refs[0]
        refs = refs[1:]
    k_buf, kt_buf, v_buf, qt_buf, gt_buf, dk_sum, dv_sum = refs
    batch, block = pl.program_id(0), pl.program_id(1)

    @pl.when(block == 0)
    def _():
        for part in range(kv_count):
            start = kv_offsets[part]
            for j in range(8):
                chunk, cols = 4 * part + j // 2, slice((j % 2) * BLOCK, (j % 2 + 1) * BLOCK)
                keys_t = kv_refs[part][j, start : start + HEAD, :]
                k_buf[chunk, cols, :] = transposed(keys_t)
                kt_buf[chunk, :, cols] = keys_t
                v_buf[chunk, cols, :] = transposed(
                    kv_refs[part][j, start + HEAD : start + 2 * HEAD, :]
                )
        for j in range(8):
            cols = slice((j % 2) * BLOCK, (j % 2 + 1) * BLOCK)
            qt_buf[j // 2, :, cols] = q_ref[j, 0:HEAD, :]
            gt_buf[j // 2, :, cols] = grad_ref[j]
        dk_sum[...] = jnp.zeros_like(dk_sum)
        dv_sum[...] = jnp.zeros_like(dv_sum)

    queries = qt_buf[block]
    grads = gt_buf[block]
    queries_r = transposed(queries)
    grads_r = transposed(grads)
    limits = limits_ref[0, 0]
    top = stats_ref[0, 0, 0:1, :]
    inverse = stats_ref[0, 0, 1:2, :]
    delta = jnp.sum(grads.astype(F32) * full_ref[0, 0], axis=0, keepdims=True)

    def score_grads(keys, values, allowed):
        scores = jnp.where(allowed, dot(keys, queries), MASKED)
        weights = jnp.exp(scores - top) * inverse
        grad_score = weights * (dot(values, grads) - delta)
        return weights.astype(BF16), grad_score.astype(BF16)

    dq = jnp.zeros((HEAD, CHUNK), F32)
    if prefix_rows:
        weights, grad_score = score_grads(
            prefix_k_ref[...], prefix_v_ref[...], prefix_mask(prefix_rows)
        )
        dq = dot(prefix_kt_ref[...], grad_score)

        @pl.when((batch == 0) & (block == 0))
        def _():
            dprefix_ref[...] = jnp.zeros_like(dprefix_ref)

        dprefix_ref[0] += dot(grad_score, queries_r)
        dprefix_ref[1] += dot(weights, grads_r)

    def step(chunk, dq):
        allowed = allowed_keys(limits, chunk, meta_ref, batch, prefix_rows > 0)
        weights, grad_score = score_grads(k_buf[chunk], v_buf[chunk], allowed)
        dk_sum[chunk] += dot(grad_score, queries_r)
        dv_sum[chunk] += dot(weights, grads_r)
        return dq + dot(kt_buf[chunk], grad_score)

    dq = lax.fori_loop(meta_ref[batch, block], meta_ref[batch, 4 + block], step, dq)
    low = dq.astype(BF16) * 0.125
    for j in range(2):
        for copy in range(copies):
            dq_ref[j * copies + copy] = low[:, j * BLOCK : (j + 1) * BLOCK]

    @pl.when(block == 3)
    def _():
        for part in range(kv_count):
            for j in range(8):
                chunk, rows = 4 * part + j // 2, slice((j % 2) * BLOCK, (j % 2 + 1) * BLOCK)
                dkv_refs[part][j, 0:HEAD, :] = dk_sum[chunk, rows, :].T.astype(BF16)
                dkv_refs[part][j, HEAD : 2 * HEAD, :] = dv_sum[chunk, rows, :].T.astype(BF16)


def by_batch(rows):
    return pl.BlockSpec((8, rows, BLOCK), lambda b, i, meta: (0, 0, b))


def whole(shape):
    return pl.BlockSpec(shape, lambda b, i, meta: (0,) * len(shape))


def per_block(rows):
    return pl.BlockSpec((1, 1, rows, CHUNK), lambda b, i, meta: (b, i, 0, 0))


def per_query(copies):
    return pl.BlockSpec((2 * copies, HEAD, BLOCK), lambda b, i, meta: (i, 0, b))


PARAMS = pltpu.CompilerParams(
    dimension_semantics=("arbitrary", "arbitrary"), vmem_limit_bytes=48 * 1024 * 1024
)


def attend(meta, limits, queries, kvs, kv_offsets, prefix, prefix_rows, copies):
    chunks = 4 * len(kvs)
    in_specs = [per_block(8), by_batch(queries.shape[1])] + [by_batch(kv.shape[1]) for kv in kvs]
    operands = [limits, queries, *kvs]
    if prefix_rows:
        in_specs += [whole((BLOCK, HEAD)), whole((HEAD, BLOCK))]
        operands += [prefix[0], prefix[1].T]
    return pl.pallas_call(
        partial(attend_kernel, kv_offsets, prefix_rows, copies),
        out_shape=(
            jax.ShapeDtypeStruct((8 * copies, HEAD, 2 * BLOCK), BF16),
            jax.ShapeDtypeStruct((2, 4, HEAD, CHUNK), F32),
            jax.ShapeDtypeStruct((2, 4, 8, CHUNK), F32),
        ),
        grid_spec=pltpu.PrefetchScalarGridSpec(
            num_scalar_prefetch=1,
            grid=(2, 4),
            in_specs=in_specs,
            out_specs=(per_query(copies), per_block(HEAD), per_block(8)),
            scratch_shapes=[
                pltpu.VMEM((chunks, CHUNK, HEAD), BF16),
                pltpu.VMEM((chunks, HEAD, CHUNK), BF16),
                pltpu.VMEM((4, HEAD, CHUNK), BF16),
            ],
        ),
        compiler_params=PARAMS,
        cost_estimate=pl.CostEstimate(flops=10**9, bytes_accessed=4 * 10**6, transcendentals=0),
    )(meta, *operands)


def attend_back(
    meta, limits, queries, kvs, kv_offsets, prefix, prefix_rows, copies, grads, full, stats
):
    chunks = 4 * len(kvs)
    in_specs = [per_block(8), by_batch(queries.shape[1])] + [by_batch(kv.shape[1]) for kv in kvs]
    operands = [limits, queries, *kvs]
    out_shape = [jax.ShapeDtypeStruct((8 * copies, HEAD, 2 * BLOCK), BF16)]
    out_specs = [per_query(copies)]
    for _ in kvs:
        out_shape.append(jax.ShapeDtypeStruct((8, 2 * HEAD, 2 * BLOCK), BF16))
        out_specs.append(by_batch(2 * HEAD))
    if prefix_rows:
        in_specs += [whole((BLOCK, HEAD)), whole((HEAD, BLOCK)), whole((BLOCK, HEAD))]
        operands += [prefix[0], prefix[0].T, prefix[1]]
        out_shape.append(jax.ShapeDtypeStruct((2, BLOCK, HEAD), F32))
        out_specs.append(whole((2, BLOCK, HEAD)))
    in_specs += [by_batch(HEAD), per_block(HEAD), per_block(8)]
    operands += [grads, full, stats]
    return pl.pallas_call(
        partial(attend_back_kernel, kv_offsets, prefix_rows, copies),
        out_shape=tuple(out_shape),
        grid_spec=pltpu.PrefetchScalarGridSpec(
            num_scalar_prefetch=1,
            grid=(2, 4),
            in_specs=in_specs,
            out_specs=tuple(out_specs),
            scratch_shapes=[
                pltpu.VMEM((chunks, CHUNK, HEAD), BF16),
                pltpu.VMEM((chunks, HEAD, CHUNK), BF16),
                pltpu.VMEM((chunks, CHUNK, HEAD), BF16),
                pltpu.VMEM((4, HEAD, CHUNK), BF16),
                pltpu.VMEM((4, HEAD, CHUNK), BF16),
                pltpu.VMEM((chunks, CHUNK, HEAD), F32),
                pltpu.VMEM((chunks, CHUNK, HEAD), F32),
            ],
        ),
        compiler_params=PARAMS,
        cost_estimate=pl.CostEstimate(flops=3 * 10**9, bytes_accessed=8 * 10**6, transcendentals=0),
    )(meta, *operands)


def positions(doc_lens, counts, group):
    docs = doc_lens.shape[1]
    upto = jnp.arange(docs)[:, None] <= jnp.arange(docs)[None, :]
    ends = jnp.sum(jnp.where(upto[None], doc_lens[:, :, None], 0), axis=1)
    slots = group * 1024 + jnp.arange(1024, dtype=jnp.int32)
    passed = ends[:, :, None] <= slots[None, None, :]
    origin = (group - 1) * 1024
    start = jnp.max(jnp.where(passed, ends[:, :, None], 0), axis=1) - origin
    stop = jnp.min(jnp.where(passed, 8192, ends[:, :, None]), axis=1) - origin
    own = jnp.broadcast_to(slots[None] - origin + 1, start.shape)

    def limits(low, high):
        both = jnp.stack([low, high], axis=1).reshape(2, 2, 4, CHUNK).transpose(0, 2, 1, 3)
        return jnp.pad(both, ((0, 0), (0, 0), (0, 6), (0, 0)))

    first = start[:, ::CHUNK] // CHUNK
    self_last = jnp.broadcast_to(jnp.arange(5, 9, dtype=jnp.int32)[None], first.shape)
    cross_last = (stop[:, CHUNK - 1 :: CHUNK] + (CHUNK - 1)) // CHUNK
    blocks = jnp.arange(16, dtype=jnp.int32) + (group - 1) * 8
    at = blocks[:, None] == jnp.arange(64, dtype=jnp.int32)[None]
    window_counts = jnp.sum(jnp.where(at[None], counts[:, None, :], 0), axis=2)
    self_meta = jnp.concatenate([first, self_last, window_counts], axis=1)
    cross_meta = jnp.concatenate([first, cross_last], axis=1)
    return (self_meta, limits(start, own), cross_meta, limits(start, stop))


def to_heads(projected):
    parts = projected.shape[1] // 512
    turned = projected.T.reshape(parts, 8, HEAD, 2 * BLOCK)
    return turned.transpose(1, 0, 2, 3).reshape(8, parts * HEAD, 2 * BLOCK)


def from_heads(value):
    parts = value.shape[1] // HEAD
    return value.reshape(8, parts, HEAD, 2 * BLOCK).transpose(1, 0, 2, 3).reshape(-1, 2 * BLOCK)


def from_wide(value):
    return value.reshape(8, 2, HEAD, 2 * BLOCK).transpose(1, 0, 2, 3).reshape(-1, 2 * BLOCK)


def tdot(left, right):
    return lax.dot_general(left, right, (((0,), (0,)), ((), ())), preferred_element_type=F32)


def dot_t(left, right):
    return lax.dot_general(left, right, (((1,), (1,)), ((), ())), preferred_element_type=F32)


def tdot_t(left, right):
    return lax.dot_general(left, right, (((0,), (1,)), ((), ())), preferred_element_type=F32)


def seq_total(grads, biases):
    width = grads.shape[1]
    extra = jnp.pad(biases, (0, 16 * width - biases.shape[0])).reshape(16, width)
    part = grads.reshape(4, 2, 4, 2, 16, width)
    for axis, bit, dim in (
        ("core", 1, 3),
        ("z", 1, 2),
        ("z", 2, 2),
        ("y", 1, 0),
        ("y", 2, 0),
        ("x_hi", 1, 1),
    ):
        size = part.shape[dim]
        mine = lax.axis_index(axis)
        if size == 4:
            pairs = part.reshape(part.shape[:dim] + (2, 2) + part.shape[dim + 1 :])
            bit_here, cut = mine % 2, dim + 1
        else:
            pairs = part
            bit_here, cut = (mine // bit) % 2, dim
        keep = lax.dynamic_index_in_dim(pairs, bit_here, cut, False)
        give = lax.dynamic_index_in_dim(pairs, 1 - bit_here, cut, False)
        shape = keep.shape
        extra_low = extra.astype(BF16)
        message = jnp.concatenate([give.astype(BF16).reshape(-1, width), extra_low], axis=0)
        got = flip(message, axis, bit)
        part = keep + got[:-16].reshape(shape).astype(F32)
        extra = extra_low.astype(F32) + got[-16:].astype(F32)
        if size == 2:
            part = part.reshape(part.shape[:dim] + (1,) + part.shape[dim:])
    mine = part.reshape(16, width).astype(BF16)
    gathered = lax.all_gather(mine, SEQ, axis=0, tiled=True)
    return gathered.astype(F32), extra.reshape(-1)[: biases.shape[0]]


def on_device(
    inputs,
    memory,
    cotangent,
    doc_lens,
    counts,
    prefix_kv,
    self_qkv,
    self_out,
    cross_q,
    cross_kv,
    cross_out,
    norm_gains,
    fc_in,
    fc_out,
    down_w,
    down_b,
    up_w,
    up_b,
):
    rows, width = (2 * BLOCK, inputs.shape[2])
    prefix_rows = prefix_kv.shape[1]
    group = lax.axis_index("y") * 2 + lax.axis_index("x_hi")
    head = lax.axis_index("z") * 2 + lax.axis_index("core")
    self_meta, self_limits, cross_meta, cross_limits = positions(doc_lens, counts, group)
    prefix = lax.dynamic_slice_in_dim(prefix_kv, head * HEAD, HEAD, 2)
    prefix = jnp.pad(prefix, ((0, 0), (0, BLOCK - prefix_rows), (0, 0)))

    self_out_full = lax.all_gather(self_out, "row", axis=0, tiled=True)
    cross_out_full = lax.all_gather(cross_out, "row", axis=0, tiled=True)
    cross_q_full = lax.all_gather(cross_q, "row", axis=1, tiled=True)

    tokens = inputs.reshape(rows, width)
    qkv_w = self_qkv.reshape(width, -1)
    scale = jnp.where(jnp.arange(qkv_w.shape[1]) < 512, 0.125, 1.0)
    projected = (dot(tokens, qkv_w) * scale).astype(BF16)
    own = regroup(to_heads(projected))
    behind = shift_groups(own[:, HEAD:, :], 1)

    kv_w = cross_kv.reshape(width, -1)
    mem_own = regroup(to_heads(dot(memory.reshape(rows, width), kv_w).astype(BF16)))
    mem_behind = shift_groups(mem_own, 1)
    mem_ahead = shift_groups(mem_own, -1)

    self_args = (self_meta, self_limits, own, (behind, own), (0, HEAD), prefix, prefix_rows)
    context, self_full, self_stats = attend(*self_args, 2)
    context = from_wide(regroup_wide(context))
    mixed = tokens.astype(F32) + tdot(context, self_out_full)
    first_norm, first_normed, first_scale = norm_rows(mixed, norm_gains[0])
    first_low = first_norm.astype(BF16)
    cross_queries = regroup(to_heads((0.125 * dot(first_low, cross_q)).astype(BF16)))

    cross_args = (
        cross_meta,
        cross_limits,
        cross_queries,
        (mem_behind, mem_own, mem_ahead),
        (0, 0, 0),
        None,
        0,
    )
    context, cross_full, cross_stats = attend(*cross_args, 2)
    context = from_wide(regroup_wide(context))
    crossed = first_norm + tdot(context, cross_out_full)
    second_norm, second_normed, second_scale = norm_rows(crossed, norm_gains[1])
    second_low = second_norm.astype(BF16)

    hidden_act, hidden_slope = gelu_both(dot(second_low, fc_in))
    adapter_act, adapter_slope = gelu_both(dot(second_low, down_w) + down_b)
    hidden_low = hidden_act.astype(BF16)
    adapter_low = adapter_act.astype(BF16)
    branch = row_total(dot(hidden_low, fc_out) + 4.0 * dot(adapter_low, up_w)) + 4.0 * up_b
    result, third_normed, third_scale = norm_rows(second_norm + branch, norm_gains[2])
    layer_out = result.astype(BF16).reshape(inputs.shape)

    grad_sum = norm_back(
        cotangent.reshape(rows, width).astype(F32), norm_gains[2], third_normed, third_scale
    )
    grad_branch = grad_sum.astype(BF16)
    grad_hidden = (dot_t(grad_branch, fc_out) * hidden_slope).astype(BF16)
    grad_adapter = (4.0 * dot_t(grad_branch, up_w) * adapter_slope).astype(BF16)
    grad_second = grad_sum + row_total(dot_t(grad_hidden, fc_in) + dot_t(grad_adapter, down_w))
    up_sum = 4.0 * tdot(grad_branch, adapter_low)
    down_sum = tdot(second_low, grad_adapter)
    up_bias_sum = 4.0 * jnp.sum(grad_branch.astype(F32), axis=0)
    down_bias_sum = jnp.sum(grad_adapter.astype(F32), axis=0)
    adapter_sums, bias_sums = seq_total(
        jnp.concatenate([down_sum, up_sum], axis=1), jnp.concatenate([down_bias_sum, up_bias_sum])
    )

    grad_crossed = norm_back(grad_second, norm_gains[1], second_normed, second_scale)
    grad_context = regroup(to_heads(dot_t(grad_crossed.astype(BF16), cross_out).astype(BF16)))
    grad_q, grad_behind, grad_own, grad_ahead = attend_back(
        *cross_args, 2, grad_context, cross_full, cross_stats
    )
    returned = shift_groups(grad_behind, -1)
    returned_too = shift_groups(grad_ahead, 1)
    grad_q = from_wide(regroup_wide(grad_q))
    grad_first = grad_crossed + tdot_t(grad_q, cross_q_full)
    grad_mixed = norm_back(grad_first, norm_gains[0], first_normed, first_scale)
    grad_context = regroup(to_heads(dot_t(grad_mixed.astype(BF16), self_out).astype(BF16)))

    grad_mem = (
        grad_own.astype(F32) + returned.astype(F32) + returned_too.astype(F32)
    ).astype(BF16)
    grad_mem = from_heads(regroup(grad_mem))
    grad_memory = row_total(tdot_t(grad_mem, kv_w)).astype(BF16).reshape(memory.shape)

    grad_q, grad_behind, grad_own, grad_prefix = attend_back(
        *self_args, 1, grad_context, self_full, self_stats
    )
    returned = shift_groups(grad_behind, -1)
    grad_kv = (grad_own.astype(F32) + returned.astype(F32)).astype(BF16)
    prefix_part = jnp.concatenate([grad_prefix[0, :32], grad_prefix[1, :32]], axis=1)
    prefix_part = prefix_part.astype(BF16).reshape(16, 2 * BLOCK)
    prefix_part = jnp.broadcast_to(prefix_part[None], (8, 16, 2 * BLOCK))
    grads = regroup(jnp.concatenate([grad_q, grad_kv, prefix_part], axis=1))
    grad_qkv = from_heads(grads[:, : 3 * HEAD])
    grad_inputs = grad_mixed + row_total(tdot_t(grad_qkv, qkv_w))
    input_grad = grad_inputs.astype(BF16).reshape(inputs.shape)

    prefix_sum = grads[:, 3 * HEAD :].astype(F32)
    for axis, bit in (("y", 1), ("y", 2), ("x_hi", 1)):
        prefix_sum = prefix_sum + flip(prefix_sum, axis, bit)
    prefix_sum = prefix_sum.reshape(8, 32, 2, HEAD)[:, :prefix_rows]
    prefix_grad = prefix_sum.transpose(2, 1, 0, 3).reshape(prefix_kv.shape)

    adapters = down_w.shape[1]
    return (
        layer_out,
        input_grad,
        grad_memory,
        prefix_grad,
        adapter_sums[:, :adapters],
        bias_sums[:adapters],
        adapter_sums[:, adapters:].T,
        bias_sums[adapters:],
    )


def solution(mesh):
    fine = Mesh(mesh.devices.reshape(4, 2, 4, 2, 2), SEQ + ("row",))
    in_specs = (
        P(None, SEQ, None),
        P(None, SEQ, None),
        P(None, SEQ, None),
        P(),
        P(),
        P(None, None, "row"),
        P(None, None, "row"),
        P("row", None),
        P(None, "row"),
        P(None, None, "row"),
        P("row", None),
        P(),
        P(None, "row"),
        P("row", None),
        P(None, "row"),
        P("row"),
        P("row", None),
        P(),
    )
    out_specs = (
        P(None, SEQ, None),
        P(None, SEQ, None),
        P(None, SEQ, None),
        P(None, None, "row"),
        P(None, "row"),
        P("row"),
        P("row", None),
        P(),
    )
    return jax.shard_map(
        on_device, mesh=fine, in_specs=in_specs, out_specs=out_specs, check_vma=False
    )
```

```python
from functools import partial

import jax
import jax.numpy as jnp
from jax import lax
from jax.experimental import pallas as pl
from jax.experimental.pallas import tpu as pltpu
from jax.sharding import Mesh
from jax.sharding import PartitionSpec as P

HEAD = 64
EPSILON = 1e-05
MASKED = -1000000000.0
CHUNK = 256
BLOCK = 128
SEQ = ("y", "x_hi", "z", "core")
GROUP = ("z", "core")
WIDE_GROUP = ("z", "core", "row")
BF16 = jnp.bfloat16
F32 = jnp.float32


def dot(left, right):
    return jnp.dot(left, right, preferred_element_type=F32)


def norm_rows(values, norm_gain):
    center = values - jnp.mean(values, axis=-1, keepdims=True)
    inverse_std = lax.rsqrt(jnp.mean(center * center, axis=-1, keepdims=True) + EPSILON)
    normed = center * inverse_std
    return (normed * norm_gain, normed, inverse_std)


def norm_back(gradient, norm_gain, normed, inverse_std):
    scaled = gradient * norm_gain
    centered = scaled - jnp.mean(scaled, axis=-1, keepdims=True)
    return (centered - normed * jnp.mean(scaled * normed, axis=-1, keepdims=True)) * inverse_std


def gelu_both(pre_act):
    cdf = 0.5 * (1.0 + lax.erf(pre_act * 0.7071067811865476))
    slope = cdf + pre_act * (0.3989422804014327 * jnp.exp(-0.5 * pre_act * pre_act))
    return (pre_act * cdf, slope)


def row_total(partial_sum):
    low = partial_sum.astype(BF16)
    other = lax.ppermute(low, "row", [(0, 1), (1, 0)])
    return low.astype(F32) + other.astype(F32)


def shift_groups(value, by):
    devices = 64
    pairs = [(i, i + 8 * by) for i in range(devices) if 0 <= i + 8 * by < devices]
    return lax.ppermute(value, SEQ, pairs)


def regroup(value):
    return lax.all_to_all(value, GROUP, 0, 0)


def regroup_wide(value):
    return lax.all_to_all(value, WIDE_GROUP, 0, 0)


def flip(value, axis_name, bit):
    size = lax.axis_size(axis_name)
    return lax.ppermute(value, axis_name, [(i, i ^ bit) for i in range(size)])


def transposed(value):
    return value.astype(F32).T.astype(BF16)


def allowed_keys(limits, chunk, meta_ref, batch, live):
    keys = lax.broadcasted_iota(jnp.int32, (CHUNK, CHUNK), 0)
    low = limits[0:1, :] - chunk * CHUNK
    high = limits[1:2, :] - chunk * CHUNK
    allowed = (keys >= low) & (keys < high)
    if live:
        first = meta_ref[batch, LIVE_AT + 2 * chunk]
        second = meta_ref[batch, LIVE_AT + 1 + 2 * chunk] + BLOCK
        allowed = allowed & (keys < jnp.where(keys < BLOCK, first, second))
    return allowed


def prefix_mask(prefix_rows):
    return lax.broadcasted_iota(jnp.int32, (BLOCK, CHUNK), 0) < prefix_rows


def half(j):
    return slice((j % 2) * BLOCK, (j % 2 + 1) * BLOCK)


def by_count(meta_ref, batch, block, range_at, counts, body):
    first = meta_ref[batch, range_at + block]
    last = meta_ref[batch, range_at + 4 + block]
    base, end = meta_ref[batch, range_at + 8], meta_ref[batch, range_at + 9]
    needed = last - first
    smaller = -1
    for count in counts:
        fits = needed <= count
        if count == counts[-1]:
            fits = needed > smaller
        elif smaller >= 0:
            fits = fits & (needed > smaller)

        @pl.when(fits)
        def _(count=count):
            body(jnp.maximum(jnp.minimum(first, end - count), base), count)

        smaller = count


def attend_kernel(
    kv_offsets, base, live, prefix_rows, resume, copies, range_at, counts, extra, meta_ref, limits_ref, q_ref, *refs
):
    refs = refs[extra:]
    kv_count = len(kv_offsets)
    kv_refs = refs[:kv_count]
    refs = refs[kv_count:]
    if prefix_rows:
        prefix_k_ref, prefix_vt_ref = refs[:2]
        refs = refs[2:]
    if resume:
        total_ref, old_ref = refs[:2]
        refs = refs[2:]
    if copies:
        out_ref = refs[0]
        refs = refs[1:]
    full_ref, stats_ref, k_buf, vt_buf, qt_buf = refs
    batch, block = pl.program_id(0), pl.program_id(1)

    @pl.when(block == 0)
    def _():
        for part in range(kv_count):
            start = kv_offsets[part]
            for j in range(8):
                chunk = 4 * part + j // 2
                k_buf[chunk, half(j), :] = transposed(kv_refs[part][j, start : start + HEAD, :])
                vt_buf[chunk, :, half(j)] = kv_refs[part][j, start + HEAD : start + 2 * HEAD, :]
        for j in range(8):
            qt_buf[j // 2, :, half(j)] = q_ref[j, 0:HEAD, :]

    queries = qt_buf[block]
    limits = limits_ref[0, 0]

    def body(first, count):
        scores = []
        for i in range(count):
            chunk = first + i
            found = dot(k_buf[chunk - base], queries)
            allowed = allowed_keys(limits, chunk, meta_ref, batch, live)
            scores.append(jnp.where(allowed, found, MASKED))
        if prefix_rows:
            found = dot(prefix_k_ref[...], queries)
            scores.append(jnp.where(prefix_mask(prefix_rows), found, MASKED))
        tops = [jnp.max(score, axis=0, keepdims=True) for score in scores]
        if resume:
            tops.append(old_ref[0, 0, 0:1, :])
        top = tops[0]
        for other in tops[1:]:
            top = jnp.maximum(top, other)
        weights = [jnp.exp(score - top) for score in scores]
        mass = sum(jnp.sum(weight, axis=0, keepdims=True) for weight in weights)
        total = sum(
            dot(vt_buf[first + i - base], weights[i].astype(BF16)) for i in range(count)
        )
        if prefix_rows:
            total = total + dot(prefix_vt_ref[...], weights[count].astype(BF16))
        if resume:
            shrink = jnp.exp(old_ref[0, 0, 0:1, :] - top)
            mass = mass + old_ref[0, 0, 1:2, :] * shrink
            total = total + total_ref[0, 0] * shrink
        if copies:
            mass = 1.0 / mass
            total = total * mass
            low = total.astype(BF16)
            for j in range(2):
                for copy in range(copies):
                    out_ref[j * copies + copy] = low[:, half(j)]
        stats_ref[0, 0, 0:1, :] = top
        stats_ref[0, 0, 1:2, :] = mass
        full_ref[0, 0] = total

    by_count(meta_ref, batch, block, range_at, counts, body)


def attend_back_kernel(
    kv_offsets, base, live, prefix_rows, resume, copies, range_at, counts, extra, meta_ref, limits_ref, q_ref, *refs
):
    refs = refs[extra:]
    kv_count = len(kv_offsets)
    kv_refs = refs[:kv_count]
    refs = refs[kv_count:]
    if prefix_rows:
        prefix_k_ref, prefix_kt_ref, prefix_v_ref = refs[:3]
        refs = refs[3:]
    if resume:
        old_ref = refs[0]
        refs = refs[1:]
    grad_ref, full_ref, stats_ref = refs[:3]
    refs = refs[3:]
    dq_ref, dkv_refs = refs[0], refs[1 : 1 + kv_count]
    refs = refs[1 + kv_count :]
    if prefix_rows:
        dprefix_ref = refs[0]
        refs = refs[1:]
    k_buf, kt_buf, v_buf, qt_buf, gt_buf, dk_sum, dv_sum = refs
    batch, block = pl.program_id(0), pl.program_id(1)

    @pl.when(block == 0)
    def _():
        for part in range(kv_count):
            start = kv_offsets[part]
            for j in range(8):
                chunk = 4 * part + j // 2
                keys_t = kv_refs[part][j, start : start + HEAD, :]
                k_buf[chunk, half(j), :] = transposed(keys_t)
                kt_buf[chunk, :, half(j)] = keys_t
                v_buf[chunk, half(j), :] = transposed(
                    kv_refs[part][j, start + HEAD : start + 2 * HEAD, :]
                )
        for j in range(8):
            qt_buf[j // 2, :, half(j)] = q_ref[j, 0:HEAD, :]
            gt_buf[j // 2, :, half(j)] = grad_ref[j]
        dk_sum[...] = jnp.zeros_like(dk_sum)
        dv_sum[...] = jnp.zeros_like(dv_sum)

    if prefix_rows:

        @pl.when((batch == 0) & (block == 0))
        def _():
            dprefix_ref[...] = jnp.zeros_like(dprefix_ref)

    queries = qt_buf[block]
    grads = gt_buf[block]
    limits = limits_ref[0, 0]

    def body(first, count):
        queries_r = transposed(queries)
        grads_r = transposed(grads)
        top = stats_ref[0, 0, 0:1, :]
        inverse = stats_ref[0, 0, 1:2, :]
        delta = jnp.sum(grads.astype(F32) * full_ref[0, 0], axis=0, keepdims=True)

        def score_grads(keys, values, allowed):
            scores = jnp.where(allowed, dot(keys, queries), MASKED)
            weights = jnp.exp(scores - top) * inverse
            grad_score = weights * (dot(values, grads) - delta)
            return weights.astype(BF16), grad_score.astype(BF16)

        dq = old_ref[0, 0] if resume else jnp.zeros((HEAD, CHUNK), F32)
        if prefix_rows:
            weights, grad_score = score_grads(
                prefix_k_ref[...], prefix_v_ref[...], prefix_mask(prefix_rows)
            )
            dq = dq + dot(prefix_kt_ref[...], grad_score)
            dprefix_ref[0] += dot(grad_score, queries_r)
            dprefix_ref[1] += dot(weights, grads_r)
        for i in range(count):
            chunk = first + i
            at = chunk - base
            allowed = allowed_keys(limits, chunk, meta_ref, batch, live)
            weights, grad_score = score_grads(k_buf[at], v_buf[at], allowed)
            dk_sum[at] += dot(grad_score, queries_r)
            dv_sum[at] += dot(weights, grads_r)
            dq = dq + dot(kt_buf[at], grad_score)
        if copies:
            low = dq.astype(BF16) * 0.125
            for j in range(2):
                for copy in range(copies):
                    dq_ref[j * copies + copy] = low[:, half(j)]
        else:
            dq_ref[0, 0] = dq

    by_count(meta_ref, batch, block, range_at, counts, body)

    @pl.when(block == 3)
    def _():
        for part in range(kv_count):
            for j in range(8):
                chunk = 4 * part + j // 2
                dkv_refs[part][j, 0:HEAD, :] = dk_sum[chunk, half(j), :].T.astype(BF16)
                dkv_refs[part][j, HEAD : 2 * HEAD, :] = dv_sum[chunk, half(j), :].T.astype(BF16)


def by_batch(rows):
    return pl.BlockSpec((8, rows, BLOCK), lambda b, i, meta: (0, 0, b))


def whole(shape):
    return pl.BlockSpec(shape, lambda b, i, meta: (0,) * len(shape))


def per_block(rows):
    return pl.BlockSpec((1, 1, rows, CHUNK), lambda b, i, meta: (b, i, 0, 0))


def per_query(copies):
    return pl.BlockSpec((2 * copies, HEAD, BLOCK), lambda b, i, meta: (i, 0, b))


def shape_of(shape, dtype):
    return jax.ShapeDtypeStruct(shape, dtype)


COST = pl.CostEstimate(flops=1000, bytes_accessed=1000, transcendentals=0)
VMEM_LIMIT = 63 * 10**6
PARAMS = pltpu.CompilerParams(
    dimension_semantics=("arbitrary", "arbitrary"), vmem_limit_bytes=VMEM_LIMIT
)


RANGES = {"own": 0, "behind": 10, "self": 20, "cross": 30}
LIVE_AT = 40
COUNTS = {"own": (1, 2, 3, 4), "behind": (0, 1, 2, 4), "self": (1, 2, 3, 4, 5, 6), "cross": (1, 2, 3, 4, 5, 6, 8, 10, 12)}


def attend(meta, limits, queries, kvs, kv_offsets, base, ranges, prefix=None, prefix_rows=0, state=None, copies=2, extra=()):
    chunks = 4 * len(kvs)
    in_specs = [per_block(8), by_batch(queries.shape[1])]
    in_specs += [pl.BlockSpec(memory_space=pl.ANY)] * len(extra)
    in_specs += [by_batch(kv.shape[1]) for kv in kvs]
    operands = [limits, queries, *extra, *kvs]
    if prefix_rows:
        in_specs += [whole((BLOCK, HEAD)), whole((HEAD, BLOCK))]
        operands += [prefix[0], prefix[1].T]
    if state is not None:
        in_specs += [per_block(HEAD), per_block(8)]
        operands += state
    out_shape = [shape_of((2, 4, HEAD, CHUNK), F32), shape_of((2, 4, 8, CHUNK), F32)]
    out_specs = [per_block(HEAD), per_block(8)]
    if copies:
        out_shape.insert(0, shape_of((8 * copies, HEAD, 2 * BLOCK), BF16))
        out_specs.insert(0, per_query(copies))
    kernel = partial(
        attend_kernel,
        kv_offsets,
        base,
        ranges != "cross",
        prefix_rows,
        state is not None,
        copies,
        RANGES[ranges],
        COUNTS[ranges],
        len(extra),
    )
    return pl.pallas_call(
        kernel,
        out_shape=tuple(out_shape),
        grid_spec=pltpu.PrefetchScalarGridSpec(
            num_scalar_prefetch=1,
            grid=(2, 4),
            in_specs=in_specs,
            out_specs=tuple(out_specs),
            scratch_shapes=[
                pltpu.VMEM((chunks, CHUNK, HEAD), BF16),
                pltpu.VMEM((chunks, HEAD, CHUNK), BF16),
                pltpu.VMEM((4, HEAD, CHUNK), BF16),
            ],
        ),
        compiler_params=PARAMS,
        cost_estimate=COST,
    )(meta, *operands)


def attend_back(
    meta,
    limits,
    queries,
    kvs,
    kv_offsets,
    base,
    ranges,
    grads,
    full,
    stats,
    prefix=None,
    prefix_rows=0,
    old=None,
    copies=2,
    extra=(),
):
    chunks = 4 * len(kvs)
    in_specs = [per_block(8), by_batch(queries.shape[1])]
    in_specs += [pl.BlockSpec(memory_space=pl.ANY)] * len(extra)
    in_specs += [by_batch(kv.shape[1]) for kv in kvs]
    operands = [limits, queries, *extra, *kvs]
    if copies:
        out_shape = [shape_of((8 * copies, HEAD, 2 * BLOCK), BF16)]
        out_specs = [per_query(copies)]
    else:
        out_shape = [shape_of((2, 4, HEAD, CHUNK), F32)]
        out_specs = [per_block(HEAD)]
    for _ in kvs:
        out_shape.append(shape_of((8, 2 * HEAD, 2 * BLOCK), BF16))
        out_specs.append(by_batch(2 * HEAD))
    if prefix_rows:
        in_specs += [whole((BLOCK, HEAD)), whole((HEAD, BLOCK)), whole((BLOCK, HEAD))]
        operands += [prefix[0], prefix[0].T, prefix[1]]
        out_shape.append(shape_of((2, BLOCK, HEAD), F32))
        out_specs.append(whole((2, BLOCK, HEAD)))
    if old is not None:
        in_specs.append(per_block(HEAD))
        operands.append(old)
    in_specs += [by_batch(HEAD), per_block(HEAD), per_block(8)]
    operands += [grads, full, stats]
    kernel = partial(
        attend_back_kernel,
        kv_offsets,
        base,
        ranges != "cross",
        prefix_rows,
        old is not None,
        copies,
        RANGES[ranges],
        COUNTS[ranges],
        len(extra),
    )
    return pl.pallas_call(
        kernel,
        out_shape=tuple(out_shape),
        grid_spec=pltpu.PrefetchScalarGridSpec(
            num_scalar_prefetch=1,
            grid=(2, 4),
            in_specs=in_specs,
            out_specs=tuple(out_specs),
            scratch_shapes=[
                pltpu.VMEM((chunks, CHUNK, HEAD), BF16),
                pltpu.VMEM((chunks, HEAD, CHUNK), BF16),
                pltpu.VMEM((chunks, CHUNK, HEAD), BF16),
                pltpu.VMEM((4, HEAD, CHUNK), BF16),
                pltpu.VMEM((4, HEAD, CHUNK), BF16),
                pltpu.VMEM((chunks, CHUNK, HEAD), F32),
                pltpu.VMEM((chunks, CHUNK, HEAD), F32),
            ],
        ),
        compiler_params=PARAMS,
        cost_estimate=COST,
    )(meta, *operands)


def dot_t(left, right):
    return lax.dot_general(left, right, (((1,), (1,)), ((), ())), preferred_element_type=F32)


def tdot(left, right):
    return lax.dot_general(left, right, (((0,), (0,)), ((), ())), preferred_element_type=F32)


def small_call(kernel, out_shape, operands, extra=()):
    specs = [pl.BlockSpec(memory_space=pltpu.VMEM)] * len(operands)
    specs += [pl.BlockSpec(memory_space=pl.ANY)] * len(extra)
    count = len(operands)
    return pl.pallas_call(
        lambda *refs: kernel(*refs[:count], *refs[count + len(extra) :]),
        out_shape=tuple(out_shape),
        in_specs=specs,
        out_specs=tuple(pl.BlockSpec(memory_space=pltpu.VMEM) for _ in out_shape),
        compiler_params=pltpu.CompilerParams(vmem_limit_bytes=VMEM_LIMIT),
        cost_estimate=COST,
    )(*operands, *extra)


def store_heads(out_ref, turned):
    for h in range(8):
        out_ref[h] = turned[h * HEAD : (h + 1) * HEAD].astype(BF16)


def project_kernel(scaled, x_ref, w_ref, *refs):
    out_ref = refs[-1]
    y = dot(x_ref[...], w_ref[0])
    if scaled:
        y = y * jnp.where(pl.program_id(0) == 0, 0.125, 1.0)
    store_heads(out_ref, y.T)


def project(tokens, weights, scaled, extra=()):
    parts = weights.shape[0]
    return pl.pallas_call(
        partial(project_kernel, scaled),
        out_shape=shape_of((8, parts * HEAD, tokens.shape[0]), BF16),
        grid=(parts,),
        in_specs=[
            pl.BlockSpec(tokens.shape, lambda i: (0, 0)),
            pl.BlockSpec((1,) + weights.shape[1:], lambda i: (i, 0, 0)),
        ]
        + [pl.BlockSpec(memory_space=pl.ANY)] * len(extra),
        out_specs=pl.BlockSpec((8, HEAD, tokens.shape[0]), lambda i: (0, i, 0)),
        compiler_params=pltpu.CompilerParams(vmem_limit_bytes=VMEM_LIMIT),
        cost_estimate=COST,
    )(tokens, weights, *extra)


def unproject_kernel(grads_ref, w_ref, *refs):
    out_ref, total = refs[-2:]
    part = pl.program_id(0)
    turned = jnp.concatenate([grads_ref[h] for h in range(8)], axis=0)
    value = dot_t(transposed(turned), w_ref[0])

    @pl.when(part == 0)
    def _():
        total[...] = value

    @pl.when(part > 0)
    def _():
        total[...] += value

    @pl.when(part == pl.num_programs(0) - 1)
    def _():
        out_ref[...] = total[...].astype(BF16)


def unproject(grads, weights, extra=()):
    parts, width, tokens = weights.shape[0], weights.shape[1], grads.shape[2]
    return pl.pallas_call(
        unproject_kernel,
        out_shape=shape_of((tokens, width), BF16),
        grid=(parts,),
        in_specs=[
            pl.BlockSpec((8, HEAD, tokens), lambda i: (0, i, 0)),
            pl.BlockSpec((1,) + weights.shape[1:], lambda i: (i, 0, 0)),
        ]
        + [pl.BlockSpec(memory_space=pl.ANY)] * len(extra),
        out_specs=pl.BlockSpec((tokens, width), lambda i: (0, 0)),
        scratch_shapes=[pltpu.VMEM((tokens, width), F32)],
        compiler_params=pltpu.CompilerParams(vmem_limit_bytes=VMEM_LIMIT),
        cost_estimate=COST,
    )(grads, weights, *extra)


def whole_weight(place_ref, own_ref, direct_ref, shared_ref, axis):
    first_row, first_core = place_ref[0, 0:1, 0:1] == 0.0, place_ref[1, 0:1, 0:1] == 0.0
    direct, shared = direct_ref[...], shared_ref[...]
    first = jnp.where(first_core, direct, shared)
    last = jnp.where(first_core, shared, direct)
    other = jnp.concatenate([first, last], axis=axis)
    own = own_ref[...]
    return jnp.where(first_row, own, other), jnp.where(first_row, other, own)


def wide_rows(value_ref, row):
    return transposed(jnp.concatenate([value_ref[2 * h + row] for h in range(8)], axis=0))


def join_kernel(has_next, place_ref, context_ref, own_ref, direct_ref, shared_ref, base_ref, gain_ref, *refs):
    if has_next:
        next_ref, normed_ref, std_ref, out_ref = refs
        base = base_ref[...].astype(F32)
    else:
        base_gain_ref, normed_ref, std_ref = refs
        base = base_ref[...] * base_gain_ref[...]
    first, last = whole_weight(place_ref, own_ref, direct_ref, shared_ref, 0)
    mixed = base + (dot(wide_rows(context_ref, 0), first) + dot(wide_rows(context_ref, 1), last))
    normed, inverse_std = norm_parts(mixed)
    normed_ref[...] = normed
    std_ref[...] = jnp.broadcast_to(inverse_std, std_ref.shape)
    if has_next:
        low = (normed * gain_ref[...]).astype(BF16)
        store_heads(out_ref, (0.125 * dot(low, next_ref[...])).T)


def norm_parts(values):
    center = values - jnp.mean(values, axis=-1, keepdims=True)
    inverse_std = lax.rsqrt(jnp.mean(center * center, axis=-1, keepdims=True) + EPSILON)
    return center * inverse_std, inverse_std


def norm_back_kernel(*refs):
    sums, lows, others = refs[0:2], refs[2:4], refs[4:6]
    gain_ref, normed_ref, std_ref, weight_ref, grad_ref, out_ref = refs[6:]
    for stream in range(2):
        at = slice(stream * BLOCK, (stream + 1) * BLOCK)
        both = lows[stream][...].astype(F32) + others[stream][...].astype(F32)
        grad_ref[at, :] = norm_back(
            sums[stream][...] + both, gain_ref[...], normed_ref[at, :], std_ref[at, 0:1]
        )
    store_heads(out_ref, dot_t(weight_ref[...], grad_ref[...].astype(BF16)))


def adapter_grads_kernel(*refs):
    second, grad_adapter, branch, adapter = refs[0:2], refs[2:4], refs[4:6], refs[6:8]
    out_ref, bias_ref = refs[8:]

    def both(pair):
        return jnp.concatenate([pair[0][...], pair[1][...]], axis=0)

    grad_adapters, branches = both(grad_adapter), both(branch)
    down = dot(transposed(both(second)), grad_adapters)
    up = 4.0 * dot(transposed(branches), both(adapter))
    half_width = down.shape[1]
    for i in range(8):
        at = slice(i * 128, (i + 1) * 128)
        out_ref[i, :, 0:half_width] = down[at].astype(BF16)
        out_ref[i, :, half_width:] = up[at].astype(BF16)
    down_bias = jnp.sum(grad_adapters.astype(F32), axis=0, keepdims=True)
    up_bias = 4.0 * jnp.sum(branches.astype(F32), axis=0, keepdims=True)
    extra = jnp.concatenate([down_bias, up_bias, jnp.zeros((1, 256), F32)], axis=1)
    pieces = [extra[:, i * 512 : (i + 1) * 512] for i in range(3)]
    bias_ref[...] = jnp.concatenate(pieces + [jnp.zeros((5, 512), F32)], axis=0)


def pack_kernel(prefix_ref, bias_ref, out_ref):
    pieces = [prefix_ref[i, 8 * j : 8 * j + 8, :] for i in range(2) for j in range(4)]
    small = jnp.concatenate([jnp.concatenate(pieces, axis=1), bias_ref[...]], axis=0).astype(BF16)
    for group in range(8):
        out_ref[group] = small


def add_kernel(parts_ref, small_ref):
    total = parts_ref[0].astype(F32)
    for group in range(1, 8):
        total = total + parts_ref[group].astype(F32)
    small = total.astype(BF16)
    small_ref[0:16, :] = small[:, 0:256]
    small_ref[16:32, :] = small[:, 256:512]


def finish_kernel(total_ref, small_ref, down_ref, up_ref, bias_ref, prefix_ref):
    half_width = down_ref.shape[1]
    for i in range(8):
        block = total_ref[i].astype(F32)
        at = slice(i * 128, (i + 1) * 128)
        down_ref[at, :] = block[:, 0:half_width]
        up_ref[:, at] = block[:, half_width:].T
    biases = [jnp.zeros((8, 256), F32)] * 2
    for i in range(2):
        for j in range(4):
            pieces = []
            for head in range(8):
                pieces.append(small_ref[head, 16 * i : 16 * i + 16, :].astype(F32)[0:8, 64 * j : 64 * j + 64])
            prefix_ref[i, 8 * j : 8 * j + 8, :] = jnp.concatenate(pieces, axis=1)
        for head in range(8):
            biases[i] = biases[i] + small_ref[head, 16 * i : 16 * i + 16, :].astype(F32)[8:16]
    bias_ref[...] = jnp.concatenate(biases, axis=1)


def join_back_kernel(
    place_ref,
    grad_q_ref,
    own_ref,
    direct_ref,
    shared_ref,
    base_ref,
    gain_ref,
    normed_ref,
    std_ref,
    weight_ref,
    grad_ref,
    out_ref,
):
    first, last = whole_weight(place_ref, own_ref, direct_ref, shared_ref, 1)
    gradient = base_ref[...] + (
        dot_t(wide_rows(grad_q_ref, 0), first) + dot_t(wide_rows(grad_q_ref, 1), last)
    )
    grad = norm_back(gradient, gain_ref[...], normed_ref[...], std_ref[:, 0:1])
    grad_ref[...] = grad
    store_heads(out_ref, dot_t(weight_ref[...], grad.astype(BF16)))


def positions(doc_lens, counts, group):
    docs = doc_lens.shape[1]
    upto = jnp.arange(docs)[:, None] <= jnp.arange(docs)[None, :]
    ends = jnp.sum(jnp.where(upto[None], doc_lens[:, :, None], 0), axis=1)
    slots = group * 1024 + jnp.arange(1024, dtype=jnp.int32)
    passed = ends[:, :, None] <= slots[None, None, :]
    origin = (group - 1) * 1024
    start = jnp.max(jnp.where(passed, ends[:, :, None], 0), axis=1) - origin
    stop = jnp.min(jnp.where(passed, 8192, ends[:, :, None]), axis=1) - origin
    own = jnp.broadcast_to(slots[None] - origin + 1, start.shape)

    def limits(low, high):
        both = jnp.stack([low, high], axis=1).reshape(2, 2, 4, CHUNK).transpose(0, 2, 1, 3)
        return jnp.pad(both, ((0, 0), (0, 0), (0, 6), (0, 0)))

    first = start[:, ::CHUNK] // CHUNK
    self_last = jnp.broadcast_to(jnp.arange(5, 9, dtype=jnp.int32)[None], first.shape)
    cross_last = (stop[:, CHUNK - 1 :: CHUNK] + (CHUNK - 1)) // CHUNK

    def columns(last, low, high):
        ends = jnp.broadcast_to(jnp.array([[low, high]], jnp.int32), (2, 2))
        return [jnp.clip(first, low, high), jnp.clip(last, low, high), ends]

    blocks = jnp.arange(16, dtype=jnp.int32) + (group - 1) * 8
    at = blocks[:, None] == jnp.arange(64, dtype=jnp.int32)[None]
    window_counts = jnp.sum(jnp.where(at[None], counts[:, None, :], 0), axis=2)
    meta = columns(self_last, 4, 8) + columns(self_last, 0, 4) + columns(self_last, 0, 8)
    meta += columns(cross_last, 0, 12) + [window_counts]
    return (jnp.concatenate(meta, axis=1), limits(start, own), limits(start, stop))


def hold(value, *earlier):
    any_space = pl.BlockSpec(memory_space=pl.ANY)
    return pl.pallas_call(
        lambda *refs: None,
        out_shape=shape_of(value.shape, value.dtype),
        in_specs=[any_space] * (1 + len(earlier)),
        out_specs=any_space,
        input_output_aliases={0: 0},
        cost_estimate=COST,
    )(value, *earlier)


def on_device(
    inputs,
    memory,
    cotangent,
    doc_lens,
    counts,
    prefix_kv,
    self_qkv,
    self_out,
    cross_q,
    cross_kv,
    cross_out,
    norm_gains,
    fc_in,
    fc_out,
    down_w,
    down_b,
    up_w,
    up_b,
):
    width = inputs.shape[2]
    rows = 2 * BLOCK
    prefix_rows = prefix_kv.shape[1]
    core, row = lax.axis_index("core"), lax.axis_index("row")
    group = lax.axis_index("y") * 2 + lax.axis_index("x_hi")
    head = lax.axis_index("z") * 2 + core
    place = jnp.broadcast_to(jnp.stack([row, core]).astype(F32)[:, None, None], (2, 1, BLOCK))
    meta, self_limits, cross_limits = positions(doc_lens, counts, group)
    prefix = lax.dynamic_slice_in_dim(prefix_kv, head * HEAD, HEAD, 2)
    prefix = jnp.pad(prefix, ((0, 0), (0, BLOCK - prefix_rows), (0, 0)))
    gains = [norm_gains[i : i + 1] for i in range(3)]
    tokens = inputs.reshape(rows, width)
    qkv_w = jnp.transpose(self_qkv, (1, 0, 2))
    kv_w = jnp.transpose(cross_kv, (1, 0, 2))

    def fetch(weight, axis, *earlier):
        size = weight.shape[axis] // 2
        mine = lax.dynamic_slice_in_dim(weight, core * size, size, axis)
        return flip(hold(mine, *earlier) if earlier else mine, "row", 1)

    def share(direct, *earlier):
        held = hold(direct, *earlier)
        return held, flip(held, "core", 1)

    projected = project(tokens, qkv_w, True)
    own = regroup(projected)
    self_out_direct = fetch(self_out, 0)
    behind = shift_groups(own[:, HEAD:, :], 1)
    mem_own = regroup(hold(project(memory.reshape(rows, width), kv_w, False, (projected,)), own))
    mem_behind = shift_groups(mem_own, 1)
    mem_ahead = shift_groups(mem_own, -1)
    self_out_halves = share(self_out_direct, mem_own)

    self_full, self_stats = attend(
        meta, self_limits, own, (own,), (HEAD,), 4, "own", prefix, prefix_rows, copies=0, extra=(mem_own,)
    )
    context, self_full, self_stats = attend(
        meta, self_limits, own, (behind,), (0,), 0, "behind", state=(self_full, self_stats)
    )
    context = regroup_wide(context)
    cross_out_direct = fetch(cross_out, 0, context)
    first_normed, first_std, queries = small_call(
        partial(join_kernel, True),
        (
            shape_of((rows, width), F32),
            shape_of((rows, BLOCK), F32),
            shape_of((8, HEAD, rows), BF16),
        ),
        (place, context, self_out, *self_out_halves, tokens, gains[0], cross_q),
    )
    queries = regroup(queries)
    cross_q_direct = fetch(cross_q, 1, queries)
    cross_args = (meta, cross_limits, queries, (mem_behind, mem_own, mem_ahead), (0, 0, 0), 0, "cross")
    context, cross_full, cross_stats = attend(*cross_args)
    cross_out_halves = share(cross_out_direct, cross_full)
    context = regroup_wide(context)
    second_normed, second_std = small_call(
        partial(join_kernel, False),
        (shape_of((rows, width), F32), shape_of((rows, BLOCK), F32)),
        (place, context, cross_out, *cross_out_halves, first_normed, gains[1], gains[0]),
        extra=(cross_q_direct,),
    )

    cross_q_halves = share(cross_q_direct, second_normed)

    streams = range(2)
    outputs, grad_sums, kept, branches = [], [], [], []
    for stream in streams:
        second_norm = second_normed[stream * BLOCK : (stream + 1) * BLOCK] * norm_gains[1]
        second_low = second_norm.astype(BF16)
        hidden_act, hidden_slope = gelu_both(dot(second_low, fc_in))
        adapter_act, adapter_slope = gelu_both(dot(second_low, down_w) + down_b)
        hidden_low = hidden_act.astype(BF16)
        adapter_low = adapter_act.astype(BF16)
        kept.append((second_low, hidden_slope, adapter_low, adapter_slope, second_norm))
        low = (dot(hidden_low, fc_out) + 4.0 * dot(adapter_low, up_w)).astype(BF16)
        branches.append((low, flip(low, "row", 1)))

    grad_adapters, grad_branches, lows, others = [], [], [], []
    for stream in streams:
        second_low, hidden_slope, adapter_low, adapter_slope, second_norm = kept[stream]
        low, other = branches[stream]
        other = hold(other, lows[-1] if stream else branches[1][0])
        branch = (low.astype(F32) + other.astype(F32)) + 4.0 * up_b
        result, normed, inverse_std = norm_rows(second_norm + branch, norm_gains[2])
        outputs.append(result.astype(BF16))
        grad_sums.append(
            norm_back(cotangent[stream].astype(F32), norm_gains[2], normed, inverse_std)
        )
        grad_branch = grad_sums[stream].astype(BF16)
        grad_hidden = (dot_t(grad_branch, fc_out) * hidden_slope).astype(BF16)
        grad_adapter = (4.0 * dot_t(grad_branch, up_w) * adapter_slope).astype(BF16)
        grad_hidden, grad_adapter = lax.optimization_barrier((grad_hidden, grad_adapter))
        low = (dot_t(grad_hidden, fc_in) + dot_t(grad_adapter, down_w)).astype(BF16)
        lows.append(low)
        others.append(flip(low, "row", 1))
        grad_adapters.append(grad_adapter)
        grad_branches.append(grad_branch)

    adapters = down_w.shape[1]
    message, bias_sums = small_call(
        adapter_grads_kernel,
        (shape_of((8, 128, 512), BF16), shape_of((8, 512), F32)),
        (kept[0][0], kept[1][0], *grad_adapters, *grad_branches, kept[0][2], kept[1][2]),
        extra=(others[0], lows[1]),
    )
    adapter_part = lax.psum_scatter(message, GROUP, scatter_dimension=0, tiled=True)

    grad_crossed, grad_context = small_call(
        norm_back_kernel,
        (shape_of((rows, width), F32), shape_of((8, HEAD, rows), BF16)),
        (
            *grad_sums,
            *lows,
            *others,
            gains[1],
            second_normed,
            second_std,
            cross_out,
        ),
        extra=(message,),
    )
    grad_context = regroup(grad_context)

    grad_q, grad_behind, grad_own, grad_ahead = attend_back(
        *cross_args, grad_context, cross_full, cross_stats
    )
    grad_q = regroup_wide(grad_q)
    adapter_parts = lax.all_gather(
        hold(adapter_part, grad_own), ("y", "x_hi"), axis=0, tiled=True
    )
    mem_parts = (
        grad_own,
        shift_groups(hold(grad_behind, grad_q), -1),
        shift_groups(hold(grad_ahead, grad_q), 1),
    )
    grad_mixed, grad_context = small_call(
        join_back_kernel,
        (shape_of((rows, width), F32), shape_of((8, HEAD, rows), BF16)),
        (
            place,
            grad_q,
            cross_q,
            *cross_q_halves,
            grad_crossed,
            gains[0],
            first_normed,
            first_std,
            self_out,
        ),
    )
    grad_context = regroup(grad_context)

    grad_mem = sum(part.astype(F32) for part in mem_parts).astype(BF16)
    grad_q, grad_behind, grad_prefix = attend_back(
        meta,
        self_limits,
        own,
        (behind,),
        (0,),
        0,
        "behind",
        grad_context,
        self_full,
        self_stats,
        prefix,
        prefix_rows,
        copies=0,
    )
    returned = shift_groups(grad_behind, -1)
    (packed,) = small_call(pack_kernel, (shape_of((8, 16, 512), BF16),), (grad_prefix, bias_sums))
    parts = lax.all_to_all(packed, ("y", "x_hi"), 0, 0)
    grad_mem = hold(grad_mem, grad_behind)
    mem_recv = regroup(grad_mem)
    grad_q, grad_own = attend_back(
        meta,
        self_limits,
        own,
        (own,),
        (HEAD,),
        4,
        "own",
        grad_context,
        self_full,
        self_stats,
        old=grad_q,
        copies=1,
        extra=(packed, grad_mem, returned),
    )
    (small_sums,) = small_call(
        add_kernel, (shape_of((32, rows), BF16),), (parts,), extra=(mem_recv,)
    )
    adapter_part = jnp.sum(hold(adapter_parts, grad_own).astype(F32), axis=0, keepdims=True)
    adapter_total = lax.all_gather(adapter_part.astype(BF16), GROUP, axis=0, tiled=True)

    grad_kv = (grad_own.astype(F32) + returned.astype(F32)).astype(BF16)
    small_sums = jnp.broadcast_to(small_sums[None], (8, 32, rows))
    message = jnp.concatenate([grad_q, grad_kv, small_sums], axis=1)
    grads = regroup(message)
    mem_low = unproject(mem_recv, kv_w, (message,))
    mem_other = flip(mem_low, "row", 1)
    low = unproject(grads, qkv_w)
    other = flip(low, "row", 1)
    grad_memory = (mem_low.astype(F32) + mem_other.astype(F32)).astype(BF16)

    down_grad, up_grad, bias_grads, prefix_grad = small_call(
        finish_kernel,
        (
            shape_of((width, adapters), F32),
            shape_of((adapters, width), F32),
            shape_of((8, 512), F32),
            shape_of((2, 32, prefix_kv.shape[2]), F32),
        ),
        (adapter_total, grads[:, 3 * HEAD :]),
        extra=(low,),
    )
    bias_grads = bias_grads.reshape(-1)
    other = hold(other, down_grad)
    input_grad = (grad_mixed + (low.astype(F32) + other.astype(F32))).astype(BF16)
    return (
        jnp.stack(outputs),
        input_grad.reshape(inputs.shape),
        grad_memory.reshape(memory.shape),
        prefix_grad[:, :prefix_rows],
        down_grad,
        bias_grads[:adapters],
        up_grad,
        bias_grads[adapters : adapters + width],
    )


def solution(mesh):
    fine = Mesh(mesh.devices.reshape(4, 2, 4, 2, 2), SEQ + ("row",))
    in_specs = (
        P(None, SEQ, None),
        P(None, SEQ, None),
        P(None, SEQ, None),
        P(),
        P(),
        P(None, None, "row"),
        P(None, None, "row"),
        P("row", None),
        P(None, "row"),
        P(None, None, "row"),
        P("row", None),
        P(),
        P(None, "row"),
        P("row", None),
        P(None, "row"),
        P("row"),
        P("row", None),
        P(),
    )
    out_specs = (
        P(None, SEQ, None),
        P(None, SEQ, None),
        P(None, SEQ, None),
        P(None, None, "row"),
        P(None, "row"),
        P("row"),
        P("row", None),
        P(),
    )
    return jax.shard_map(
        on_device, mesh=fine, in_specs=in_specs, out_specs=out_specs, check_vma=False
    )
```

```python
from functools import partial

import jax
import jax.numpy as jnp
from jax import lax
from jax.experimental import pallas as pl
from jax.experimental.pallas import tpu as pltpu
from jax.sharding import Mesh
from jax.sharding import PartitionSpec as P

HEAD = 64
EPSILON = 1e-05
MASKED = -1000000000.0
CHUNK = 256
PREFIX_ROWS = 32
BLOCK = 128
SEQ = ("y", "x_hi", "z", "core")
GROUP = ("z", "core")
WIDE_GROUP = ("z", "core", "row")
BF16 = jnp.bfloat16
F32 = jnp.float32


def dot(left, right):
    return jnp.dot(left, right, preferred_element_type=F32)


def norm_rows(values, norm_gain):
    center = values - jnp.mean(values, axis=-1, keepdims=True)
    inverse_std = lax.rsqrt(jnp.mean(center * center, axis=-1, keepdims=True) + EPSILON)
    normed = center * inverse_std
    return (normed * norm_gain, normed, inverse_std)


def norm_back(gradient, norm_gain, normed, inverse_std):
    scaled = gradient * norm_gain
    centered = scaled - jnp.mean(scaled, axis=-1, keepdims=True)
    return (centered - normed * jnp.mean(scaled * normed, axis=-1, keepdims=True)) * inverse_std


def gelu_both(pre_act):
    cdf = 0.5 * (1.0 + lax.erf(pre_act * 0.7071067811865476))
    slope = cdf + pre_act * (0.3989422804014327 * jnp.exp(-0.5 * pre_act * pre_act))
    return (pre_act * cdf, slope)


def row_total(partial_sum):
    low = partial_sum.astype(BF16)
    other = lax.ppermute(low, "row", [(0, 1), (1, 0)])
    return low.astype(F32) + other.astype(F32)


def shift_groups(value, by):
    devices = 64
    pairs = [(i, i + 8 * by) for i in range(devices) if 0 <= i + 8 * by < devices]
    return lax.ppermute(value, SEQ, pairs)


def regroup(value):
    return lax.all_to_all(value, GROUP, 0, 0)


def regroup_wide(value):
    return lax.all_to_all(value, WIDE_GROUP, 0, 0)


def flip(value, axis_name, bit):
    size = lax.axis_size(axis_name)
    return lax.ppermute(value, axis_name, [(i, i ^ bit) for i in range(size)])


def transposed(value):
    return value.astype(F32).T.astype(BF16)


def allowed_keys(limits, chunk, meta_ref, batch, live):
    keys = lax.broadcasted_iota(jnp.int32, (CHUNK, CHUNK), 0)
    low = limits[0:1, :] - chunk * CHUNK
    high = limits[1:2, :] - chunk * CHUNK
    allowed = (keys >= low) & (keys < high)
    if live:
        first = meta_ref[batch, LIVE_AT + 2 * chunk]
        second = meta_ref[batch, LIVE_AT + 1 + 2 * chunk] + BLOCK
        allowed = allowed & (keys < jnp.where(keys < BLOCK, first, second))
    return allowed


def prefix_mask(prefix_rows):
    return lax.broadcasted_iota(jnp.int32, (PREFIX_ROWS, CHUNK), 0) < prefix_rows


def half(j):
    return slice((j % 2) * BLOCK, (j % 2 + 1) * BLOCK)


def by_count(meta_ref, batches, block, range_at, counts, body):
    firsts = [meta_ref[batch, range_at + block] for batch in batches]
    needs = [meta_ref[batch, range_at + 4 + block] - first for batch, first in zip(batches, firsts)]
    base, end = meta_ref[0, range_at + 8], meta_ref[0, range_at + 9]
    needed = needs[0]
    for need in needs[1:]:
        needed = jnp.maximum(needed, need)
    smaller = -1
    for count in counts:
        fits = needed <= count
        if count == counts[-1]:
            fits = needed > smaller
        elif smaller >= 0:
            fits = fits & (needed > smaller)

        @pl.when(fits)
        def _(count=count):
            body([jnp.maximum(jnp.minimum(first, end - count), base) for first in firsts], count)

        smaller = count


def lanes(batch):
    return slice(batch * BLOCK, (batch + 1) * BLOCK)


def any_lanes(batch):
    return pl.ds(pl.multiple_of(batch * BLOCK, BLOCK), BLOCK)


def each_block(count, body):
    def step(index, carry):
        body(index)
        return carry

    lax.fori_loop(0, count, step, 0)


def attend_kernel(kv_offsets, passes, live, prefix_rows, resume, copies, extra, meta_ref, limits_ref, q_ref, *refs):
    refs = refs[extra:]
    kv_count = len(kv_offsets)
    chunks = 4 * kv_count
    kv_refs = refs[:kv_count]
    refs = refs[kv_count:]
    if prefix_rows:
        prefix_k_ref, prefix_vt_ref = refs[:2]
        refs = refs[2:]
    if resume:
        total_ref, old_ref = refs[:2]
        refs = refs[2:]
    if copies:
        out_ref = refs[0]
        refs = refs[1:]
    full_ref, stats_ref, k_buf, vt_buf, qt_buf = refs

    for batch in range(2):
        for part in range(kv_count):
            start = kv_offsets[part]
            for j in range(8):
                chunk = chunks * batch + 4 * part + j // 2
                kv = kv_refs[part][j, start : start + 2 * HEAD, lanes(batch)]
                k_buf[chunk, half(j), :] = transposed(kv[:HEAD])
                vt_buf[chunk, :, half(j)] = kv[HEAD:]
        for j in range(8):
            qt_buf[4 * batch + j // 2, :, half(j)] = q_ref[j, 0:HEAD, lanes(batch)]

    def attend_pass(part, ranges):
        base = BASES[ranges]
        prefixed = prefix_rows > 0 and part == 0
        state = (full_ref, stats_ref) if part else (total_ref, old_ref) if resume else None
        finish = copies > 0 and part == kv_count - 1

        def attend_block(batch, block, first, count):
            queries = qt_buf[4 * batch + block]
            limits = limits_ref[batch, block]
            at = chunks * batch + 4 * part + first - base
            scores = []
            for i in range(count):
                found = dot(k_buf[at + i], queries)
                allowed = allowed_keys(limits, first + i, meta_ref, batch, live)
                scores.append(jnp.where(allowed, found, MASKED))
            if prefixed:
                found = dot(prefix_k_ref[...], queries)
                scores.append(jnp.where(prefix_mask(prefix_rows), found, MASKED))
            tops = [jnp.max(score, axis=0, keepdims=True) for score in scores]
            if state:
                old_top = state[1][batch, block, 0:1, :]
                tops.append(old_top)
            top = tops[0]
            for other in tops[1:]:
                top = jnp.maximum(top, other)
            weights = [jnp.exp(score - top) for score in scores]
            mass = sum(jnp.sum(weight, axis=0, keepdims=True) for weight in weights)
            total = sum(dot(vt_buf[at + i], weights[i].astype(BF16)) for i in range(count))
            if prefixed:
                total = total + dot(prefix_vt_ref[...], weights[count].astype(BF16))
            if state:
                shrink = jnp.exp(old_top - top)
                mass = mass + state[1][batch, block, 1:2, :] * shrink
                total = total + state[0][batch, block] * shrink
            if finish:
                mass = 1.0 / mass
                total = total * mass
            return top, mass, total

        def query_block(block):
            def body(firsts, count):
                found = [attend_block(batch, block, firsts[batch], count) for batch in range(2)]
                for batch in range(2):
                    top, mass, total = found[batch]
                    if finish:
                        low = total.astype(BF16)
                        for j in range(2):
                            for copy in range(copies):
                                out_ref[(2 * block + j) * copies + copy, :, lanes(batch)] = low[:, half(j)]
                    stats_ref[batch, block, 0:1, :] = top
                    stats_ref[batch, block, 1:2, :] = mass
                    full_ref[batch, block] = total

            by_count(meta_ref, (0, 1), block, RANGES[ranges], COUNTS[ranges], body)

        each_block(4, query_block)

    for part, ranges in enumerate(passes):
        attend_pass(part, ranges)


def score_grads(keys, values, queries, grads, stats, delta, allowed):
    scores = jnp.where(allowed, dot(keys, queries), MASKED)
    weights = jnp.exp(scores - stats[0:1, :]) * stats[1:2, :]
    grad_score = weights * (dot(values, grads) - delta)
    return weights.astype(BF16), grad_score.astype(BF16)


def attend_back_kernel(
    kv_offsets, base, live, resume, copies, range_at, counts, extra, meta_ref, limits_ref, q_ref, *refs
):
    refs = refs[extra:]
    kv_count = len(kv_offsets)
    chunks = 4 * kv_count
    kv_refs = refs[:kv_count]
    refs = refs[kv_count:]
    if resume:
        old_ref = refs[0]
        refs = refs[1:]
    grad_ref, full_ref, stats_ref = refs[:3]
    refs = refs[3:]
    dq_ref, dkv_refs = refs[0], refs[1 : 1 + kv_count]
    k_buf, kt_buf, v_buf, qt_buf, gt_buf, dk_sum, dv_sum = refs[1 + kv_count :]

    for batch in range(2):
        for part in range(kv_count):
            start = kv_offsets[part]
            for j in range(8):
                chunk = chunks * batch + 4 * part + j // 2
                kv = kv_refs[part][j, start : start + 2 * HEAD, lanes(batch)]
                k_buf[chunk, half(j), :] = transposed(kv[:HEAD])
                kt_buf[chunk, :, half(j)] = kv[:HEAD]
                v_buf[chunk, half(j), :] = transposed(kv[HEAD:])
        for j in range(8):
            qt_buf[4 * batch + j // 2, :, half(j)] = q_ref[j, 0:HEAD, lanes(batch)]
            gt_buf[4 * batch + j // 2, :, half(j)] = grad_ref[j, :, lanes(batch)]
    dk_sum[...] = jnp.zeros_like(dk_sum)
    dv_sum[...] = jnp.zeros_like(dv_sum)

    def query_block(index):
        batch, block = index // 4, index % 4
        queries = qt_buf[4 * batch + block]
        grads = gt_buf[4 * batch + block]
        limits = limits_ref[batch, block]
        stats = stats_ref[batch, block]

        def body(firsts, count):
            first = firsts[0]
            dq = old_ref[batch, block] if resume else jnp.zeros((HEAD, CHUNK), F32)
            if count:
                queries_r = transposed(queries)
                grads_r = transposed(grads)
                delta = jnp.sum(grads.astype(F32) * full_ref[batch, block], axis=0, keepdims=True)
            for i in range(count):
                chunk = first + i
                at = chunks * batch + chunk - base
                allowed = allowed_keys(limits, chunk, meta_ref, batch, live)
                weights, grad_score = score_grads(
                    k_buf[at], v_buf[at], queries, grads, stats, delta, allowed
                )
                dk_sum[at] += dot(grad_score, queries_r)
                dv_sum[at] += dot(weights, grads_r)
                dq = dq + dot(kt_buf[at], grad_score)
            if copies:
                low = dq.astype(BF16) * 0.125
                for j in range(2):
                    for copy in range(copies):
                        dq_ref[(2 * block + j) * copies + copy, :, any_lanes(batch)] = low[:, half(j)]
            else:
                dq_ref[batch, block] = dq

        by_count(meta_ref, (batch,), block, range_at, counts, body)

    each_block(8, query_block)

    for batch in range(2):
        for part in range(kv_count):
            for j in range(8):
                chunk = chunks * batch + 4 * part + j // 2
                dkv_refs[part][j, 0:HEAD, lanes(batch)] = dk_sum[chunk, half(j), :].T.astype(BF16)
                dkv_refs[part][j, HEAD : 2 * HEAD, lanes(batch)] = dv_sum[chunk, half(j), :].T.astype(BF16)


def prefix_back_kernel(
    prefix_rows, q_ref, k_ref, kt_ref, v_ref, grad_ref, full_ref, stats_ref, bias_ref, dq_ref, out_ref
):
    dk = jnp.zeros((PREFIX_ROWS, HEAD), F32)
    dv = jnp.zeros((PREFIX_ROWS, HEAD), F32)
    for batch in range(2):
        for block in range(4):
            queries = jnp.concatenate(
                [q_ref[2 * block + j, 0:HEAD, lanes(batch)] for j in range(2)], axis=1
            )
            grads = jnp.concatenate([grad_ref[2 * block + j, :, lanes(batch)] for j in range(2)], axis=1)
            delta = jnp.sum(grads.astype(F32) * full_ref[batch, block], axis=0, keepdims=True)
            weights, grad_score = score_grads(
                k_ref[...],
                v_ref[...],
                queries,
                grads,
                stats_ref[batch, block],
                delta,
                prefix_mask(prefix_rows),
            )
            dq_ref[batch, block] = dot(kt_ref[...], grad_score)
            dk = dk + dot(grad_score, transposed(queries))
            dv = dv + dot(weights, transposed(grads))
    pieces = [value[8 * j : 8 * j + 8] for value in (dk, dv) for j in range(4)]
    small = jnp.concatenate([jnp.concatenate(pieces, axis=1), bias_ref[...]], axis=0).astype(BF16)
    for group in range(8):
        out_ref[group] = small


def shape_of(shape, dtype):
    return jax.ShapeDtypeStruct(shape, dtype)


COST = pl.CostEstimate(flops=1000, bytes_accessed=1000, transcendentals=0)
VMEM_LIMIT = 63 * 10**6
PARAMS = pltpu.CompilerParams(vmem_limit_bytes=VMEM_LIMIT)
IN_VMEM = pl.BlockSpec(memory_space=pltpu.VMEM)
ANYWHERE = pl.BlockSpec(memory_space=pl.ANY)

RANGES = {"own": 0, "behind": 10, "cross": 20, "cross own": 30, "cross behind": 40, "cross ahead": 50}
BASES = {"own": 4, "behind": 0, "cross": 0, "cross own": 4, "cross behind": 0, "cross ahead": 8}
LIVE_AT = 60
COUNTS = {
    "own": (1, 2, 3, 4),
    "behind": (0, 1, 2, 3, 4),
    "cross": (1, 2, 3, 4, 5, 6, 8, 10, 12),
    "cross own": (1, 2, 3, 4),
    "cross behind": (0, 1, 2, 4),
    "cross ahead": (0, 1, 2, 4),
}


def attend(meta, limits, queries, kvs, kv_offsets, passes, prefix=None, prefix_rows=0, state=None, copies=2, extra=()):
    chunks = 4 * len(kvs)
    operands = [*kvs]
    if prefix_rows:
        operands += [prefix[0], prefix[1].T]
    if state is not None:
        operands += state
    out_shape = [shape_of((2, 4, HEAD, CHUNK), F32), shape_of((2, 4, 8, CHUNK), F32)]
    if copies:
        out_shape.insert(0, shape_of((8 * copies, HEAD, 2 * BLOCK), BF16))
    kernel = partial(
        attend_kernel,
        kv_offsets,
        passes,
        not passes[0].startswith("cross"),
        prefix_rows,
        state is not None,
        copies,
        len(extra),
    )
    return pl.pallas_call(
        kernel,
        out_shape=tuple(out_shape),
        in_specs=[pl.BlockSpec(memory_space=pltpu.SMEM), IN_VMEM, IN_VMEM]
        + [ANYWHERE] * len(extra)
        + [IN_VMEM] * len(operands),
        out_specs=tuple(IN_VMEM for _ in out_shape),
        scratch_shapes=[
            pltpu.VMEM((2 * chunks, CHUNK, HEAD), BF16),
            pltpu.VMEM((2 * chunks, HEAD, CHUNK), BF16),
            pltpu.VMEM((8, HEAD, CHUNK), BF16),
        ],
        compiler_params=PARAMS,
        cost_estimate=COST,
    )(meta, limits, queries, *extra, *operands)


def attend_back(
    meta, limits, queries, kvs, kv_offsets, base, ranges, grads, full, stats, old=None, copies=2, extra=()
):
    chunks = 4 * len(kvs)
    operands = [*kvs]
    if copies:
        out_shape = [shape_of((8 * copies, HEAD, 2 * BLOCK), BF16)]
    else:
        out_shape = [shape_of((2, 4, HEAD, CHUNK), F32)]
    for _ in kvs:
        out_shape.append(shape_of((8, 2 * HEAD, 2 * BLOCK), BF16))
    if old is not None:
        operands.append(old)
    operands += [grads, full, stats]
    kernel = partial(
        attend_back_kernel,
        kv_offsets,
        base,
        ranges != "cross",
        old is not None,
        copies,
        RANGES[ranges],
        COUNTS[ranges],
        len(extra),
    )
    return pl.pallas_call(
        kernel,
        out_shape=tuple(out_shape),
        in_specs=[pl.BlockSpec(memory_space=pltpu.SMEM), IN_VMEM, IN_VMEM]
        + [ANYWHERE] * len(extra)
        + [IN_VMEM] * len(operands),
        out_specs=tuple(IN_VMEM for _ in out_shape),
        scratch_shapes=[
            pltpu.VMEM((2 * chunks, CHUNK, HEAD), BF16),
            pltpu.VMEM((2 * chunks, HEAD, CHUNK), BF16),
            pltpu.VMEM((2 * chunks, CHUNK, HEAD), BF16),
            pltpu.VMEM((8, HEAD, CHUNK), BF16),
            pltpu.VMEM((8, HEAD, CHUNK), BF16),
            pltpu.VMEM((2 * chunks, CHUNK, HEAD), F32),
            pltpu.VMEM((2 * chunks, CHUNK, HEAD), F32),
        ],
        compiler_params=PARAMS,
        cost_estimate=COST,
    )(meta, limits, queries, *extra, *operands)


def prefix_back(queries, prefix, prefix_rows, grads, full, stats, biases):
    return pl.pallas_call(
        partial(prefix_back_kernel, prefix_rows),
        out_shape=(shape_of((2, 4, HEAD, CHUNK), F32), shape_of((8, 16, 512), BF16)),
        in_specs=[IN_VMEM] * 8,
        out_specs=(IN_VMEM, IN_VMEM),
        compiler_params=PARAMS,
        cost_estimate=COST,
    )(queries, prefix[0], prefix[0].T, prefix[1], grads, full, stats, biases)


def dot_t(left, right):
    return lax.dot_general(left, right, (((1,), (1,)), ((), ())), preferred_element_type=F32)


def tdot(left, right):
    return lax.dot_general(left, right, (((0,), (0,)), ((), ())), preferred_element_type=F32)


def small_call(kernel, out_shape, operands, extra=()):
    specs = [IN_VMEM] * len(operands)
    specs += [pl.BlockSpec(memory_space=pl.ANY)] * len(extra)
    count = len(operands)
    return pl.pallas_call(
        lambda *refs: kernel(*refs[:count], *refs[count + len(extra) :]),
        out_shape=tuple(out_shape),
        in_specs=specs,
        out_specs=tuple(pl.BlockSpec(memory_space=pltpu.VMEM) for _ in out_shape),
        compiler_params=pltpu.CompilerParams(vmem_limit_bytes=VMEM_LIMIT),
        cost_estimate=COST,
    )(*operands, *extra)


def store_heads(out_ref, turned):
    for h in range(8):
        out_ref[h] = turned[h * HEAD : (h + 1) * HEAD].astype(BF16)


def project_kernel(scaled, x_ref, w_ref, *refs):
    out_ref = refs[-1]
    y = dot(x_ref[...], w_ref[0])
    if scaled:
        y = y * jnp.where(pl.program_id(0) == 0, 0.125, 1.0)
    store_heads(out_ref, y.T)


def project(tokens, weights, scaled, extra=()):
    parts = weights.shape[0]
    return pl.pallas_call(
        partial(project_kernel, scaled),
        out_shape=shape_of((8, parts * HEAD, tokens.shape[0]), BF16),
        grid=(parts,),
        in_specs=[
            pl.BlockSpec(tokens.shape, lambda i: (0, 0)),
            pl.BlockSpec((1,) + weights.shape[1:], lambda i: (i, 0, 0)),
        ]
        + [pl.BlockSpec(memory_space=pl.ANY)] * len(extra),
        out_specs=pl.BlockSpec((8, HEAD, tokens.shape[0]), lambda i: (0, i, 0)),
        compiler_params=pltpu.CompilerParams(vmem_limit_bytes=VMEM_LIMIT),
        cost_estimate=COST,
    )(tokens, weights, *extra)


def unproject_kernel(grads_ref, w_ref, *refs):
    out_ref, total = refs[-2:]
    part = pl.program_id(0)
    turned = jnp.concatenate([grads_ref[h] for h in range(8)], axis=0)
    value = dot_t(transposed(turned), w_ref[0])

    @pl.when(part == 0)
    def _():
        total[...] = value

    @pl.when(part > 0)
    def _():
        total[...] += value

    @pl.when(part == pl.num_programs(0) - 1)
    def _():
        out_ref[...] = total[...].astype(BF16)


def unproject(grads, weights, extra=()):
    parts, width, tokens = weights.shape[0], weights.shape[1], grads.shape[2]
    return pl.pallas_call(
        unproject_kernel,
        out_shape=shape_of((tokens, width), BF16),
        grid=(parts,),
        in_specs=[
            pl.BlockSpec((8, HEAD, tokens), lambda i: (0, i, 0)),
            pl.BlockSpec((1,) + weights.shape[1:], lambda i: (i, 0, 0)),
        ]
        + [pl.BlockSpec(memory_space=pl.ANY)] * len(extra),
        out_specs=pl.BlockSpec((tokens, width), lambda i: (0, 0)),
        scratch_shapes=[pltpu.VMEM((tokens, width), F32)],
        compiler_params=pltpu.CompilerParams(vmem_limit_bytes=VMEM_LIMIT),
        cost_estimate=COST,
    )(grads, weights, *extra)


def whole_weight(place_ref, own_ref, direct_ref, shared_ref, axis):
    first_row, first_core = place_ref[0, 0:1, 0:1] == 0.0, place_ref[1, 0:1, 0:1] == 0.0
    direct, shared = direct_ref[...], shared_ref[...]
    first = jnp.where(first_core, direct, shared)
    last = jnp.where(first_core, shared, direct)
    other = jnp.concatenate([first, last], axis=axis)
    own = own_ref[...]
    return jnp.where(first_row, own, other), jnp.where(first_row, other, own)


def wide_rows(value_ref, row):
    return transposed(jnp.concatenate([value_ref[2 * h + row] for h in range(8)], axis=0))


def join_kernel(has_next, place_ref, context_ref, own_ref, direct_ref, shared_ref, base_ref, gain_ref, *refs):
    if has_next:
        next_ref, normed_ref, std_ref, out_ref = refs
        base = base_ref[...].astype(F32)
    else:
        base_gain_ref, normed_ref, std_ref = refs
        base = base_ref[...] * base_gain_ref[...]
    first, last = whole_weight(place_ref, own_ref, direct_ref, shared_ref, 0)
    mixed = base + (dot(wide_rows(context_ref, 0), first) + dot(wide_rows(context_ref, 1), last))
    normed, inverse_std = norm_parts(mixed)
    normed_ref[...] = normed
    std_ref[...] = jnp.broadcast_to(inverse_std, std_ref.shape)
    if has_next:
        low = (normed * gain_ref[...]).astype(BF16)
        store_heads(out_ref, (0.125 * dot(low, next_ref[...])).T)


def norm_parts(values):
    center = values - jnp.mean(values, axis=-1, keepdims=True)
    inverse_std = lax.rsqrt(jnp.mean(center * center, axis=-1, keepdims=True) + EPSILON)
    return center * inverse_std, inverse_std


def norm_back_kernel(*refs):
    sums, lows, others = refs[0:2], refs[2:4], refs[4:6]
    gain_ref, normed_ref, std_ref, weight_ref, grad_ref, out_ref = refs[6:]
    for stream in range(2):
        at = slice(stream * BLOCK, (stream + 1) * BLOCK)
        both = lows[stream][...].astype(F32) + others[stream][...].astype(F32)
        grad_ref[at, :] = norm_back(
            sums[stream][...] + both, gain_ref[...], normed_ref[at, :], std_ref[at, 0:1]
        )
    store_heads(out_ref, dot_t(weight_ref[...], grad_ref[...].astype(BF16)))


def adapter_grads_kernel(*refs):
    second, grad_adapter, branch, adapter = refs[0:2], refs[2:4], refs[4:6], refs[6:8]
    out_ref, bias_ref = refs[8:]

    def both(pair):
        return jnp.concatenate([pair[0][...], pair[1][...]], axis=0)

    grad_adapters, branches = both(grad_adapter), both(branch)
    down = dot(transposed(both(second)), grad_adapters)
    up = 4.0 * dot(transposed(branches), both(adapter))
    half_width = down.shape[1]
    for i in range(8):
        at = slice(i * 128, (i + 1) * 128)
        out_ref[i, :, 0:half_width] = down[at].astype(BF16)
        out_ref[i, :, half_width:] = up[at].astype(BF16)
    down_bias = jnp.sum(grad_adapters.astype(F32), axis=0, keepdims=True)
    up_bias = 4.0 * jnp.sum(branches.astype(F32), axis=0, keepdims=True)
    extra = jnp.concatenate([down_bias, up_bias, jnp.zeros((1, 256), F32)], axis=1)
    pieces = [extra[:, i * 512 : (i + 1) * 512] for i in range(3)]
    bias_ref[...] = jnp.concatenate(pieces + [jnp.zeros((5, 512), F32)], axis=0)


def add_kernel(parts_ref, small_ref):
    total = parts_ref[0].astype(F32)
    for group in range(1, 8):
        total = total + parts_ref[group].astype(F32)
    small = total.astype(BF16)
    small_ref[0:16, :] = small[:, 0:256]
    small_ref[16:32, :] = small[:, 256:512]


def finish_kernel(total_ref, small_ref, down_ref, up_ref, bias_ref, prefix_ref):
    half_width = down_ref.shape[1]
    for i in range(8):
        block = total_ref[i].astype(F32)
        at = slice(i * 128, (i + 1) * 128)
        down_ref[at, :] = block[:, 0:half_width]
        up_ref[:, at] = block[:, half_width:].T
    biases = [jnp.zeros((8, 256), F32)] * 2
    for i in range(2):
        for j in range(4):
            pieces = []
            for head in range(8):
                pieces.append(small_ref[head, 16 * i : 16 * i + 16, :].astype(F32)[0:8, 64 * j : 64 * j + 64])
            prefix_ref[i, 8 * j : 8 * j + 8, :] = jnp.concatenate(pieces, axis=1)
        for head in range(8):
            biases[i] = biases[i] + small_ref[head, 16 * i : 16 * i + 16, :].astype(F32)[8:16]
    bias_ref[...] = jnp.concatenate(biases, axis=1)


def join_back_kernel(
    place_ref,
    grad_q_ref,
    own_ref,
    direct_ref,
    shared_ref,
    base_ref,
    gain_ref,
    normed_ref,
    std_ref,
    weight_ref,
    grad_ref,
    out_ref,
):
    first, last = whole_weight(place_ref, own_ref, direct_ref, shared_ref, 1)
    gradient = base_ref[...] + (
        dot_t(wide_rows(grad_q_ref, 0), first) + dot_t(wide_rows(grad_q_ref, 1), last)
    )
    grad = norm_back(gradient, gain_ref[...], normed_ref[...], std_ref[:, 0:1])
    grad_ref[...] = grad
    store_heads(out_ref, dot_t(weight_ref[...], grad.astype(BF16)))


def positions(doc_lens, counts, group):
    docs = doc_lens.shape[1]
    upto = jnp.arange(docs)[:, None] <= jnp.arange(docs)[None, :]
    ends = jnp.sum(jnp.where(upto[None], doc_lens[:, :, None], 0), axis=1)
    slots = group * 1024 + jnp.arange(1024, dtype=jnp.int32)
    passed = ends[:, :, None] <= slots[None, None, :]
    origin = (group - 1) * 1024
    start = jnp.max(jnp.where(passed, ends[:, :, None], 0), axis=1) - origin
    stop = jnp.min(jnp.where(passed, 8192, ends[:, :, None]), axis=1) - origin
    own = jnp.broadcast_to(slots[None] - origin + 1, start.shape)

    def limits(low, high):
        both = jnp.stack([low, high], axis=1).reshape(2, 2, 4, CHUNK).transpose(0, 2, 1, 3)
        return jnp.pad(both, ((0, 0), (0, 0), (0, 6), (0, 0)))

    first = start[:, ::CHUNK] // CHUNK
    self_last = jnp.broadcast_to(jnp.arange(5, 9, dtype=jnp.int32)[None], first.shape)
    cross_last = (stop[:, CHUNK - 1 :: CHUNK] + (CHUNK - 1)) // CHUNK

    def columns(last, low, high):
        ends = jnp.broadcast_to(jnp.array([[low, high]], jnp.int32), (2, 2))
        return [jnp.clip(first, low, high), jnp.clip(last, low, high), ends]

    blocks = jnp.arange(16, dtype=jnp.int32) + (group - 1) * 8
    at = blocks[:, None] == jnp.arange(64, dtype=jnp.int32)[None]
    window_counts = jnp.sum(jnp.where(at[None], counts[:, None, :], 0), axis=2)
    meta = columns(self_last, 4, 8) + columns(self_last, 0, 4) + columns(cross_last, 0, 12)
    meta += columns(cross_last, 4, 8) + columns(cross_last, 0, 4) + columns(cross_last, 8, 12)
    meta += [window_counts]
    return (jnp.concatenate(meta, axis=1), limits(start, own), limits(start, stop))


def hold(value, *earlier):
    any_space = pl.BlockSpec(memory_space=pl.ANY)
    return pl.pallas_call(
        lambda *refs: None,
        out_shape=shape_of(value.shape, value.dtype),
        in_specs=[any_space] * (1 + len(earlier)),
        out_specs=any_space,
        input_output_aliases={0: 0},
        cost_estimate=COST,
    )(value, *earlier)


def on_device(
    inputs,
    memory,
    cotangent,
    doc_lens,
    counts,
    prefix_kv,
    self_qkv,
    self_out,
    cross_q,
    cross_kv,
    cross_out,
    norm_gains,
    fc_in,
    fc_out,
    down_w,
    down_b,
    up_w,
    up_b,
):
    width = inputs.shape[2]
    rows = 2 * BLOCK
    prefix_rows = prefix_kv.shape[1]
    core, row = lax.axis_index("core"), lax.axis_index("row")
    group = lax.axis_index("y") * 2 + lax.axis_index("x_hi")
    head = lax.axis_index("z") * 2 + core
    place = jnp.broadcast_to(jnp.stack([row, core]).astype(F32)[:, None, None], (2, 1, BLOCK))
    meta, self_limits, cross_limits = positions(doc_lens, counts, group)
    prefix = lax.dynamic_slice_in_dim(prefix_kv, head * HEAD, HEAD, 2)
    prefix = jnp.pad(prefix, ((0, 0), (0, PREFIX_ROWS - prefix_rows), (0, 0)))
    gains = [norm_gains[i : i + 1] for i in range(3)]
    tokens = inputs.reshape(rows, width)
    qkv_w = jnp.transpose(self_qkv, (1, 0, 2))
    kv_w = jnp.transpose(cross_kv, (1, 0, 2))

    def share(direct, *earlier):
        held = hold(direct, *earlier)
        return held, flip(held, "core", 1)

    def fetch(weight, axis, *earlier):
        size = weight.shape[axis] // 2
        mine = lax.dynamic_slice_in_dim(weight, core * size, size, axis)
        return flip(hold(mine, *earlier) if earlier else mine, "row", 1)

    projected = project(tokens, qkv_w, True)
    own = regroup(projected)
    self_out_direct = fetch(self_out, 0)
    behind = shift_groups(own[:, HEAD:, :], 1)
    mem_projected = project(memory.reshape(rows, width), kv_w, False, (projected,))
    mem_own = regroup(hold(mem_projected, own))
    mem_behind = shift_groups(mem_own, 1)
    mem_ahead = shift_groups(mem_own, -1)
    self_out_halves = share(self_out_direct, mem_own)

    self_full, self_stats = attend(
        meta,
        self_limits,
        own,
        (own,),
        (HEAD,),
        ("own",),
        prefix,
        prefix_rows,
        copies=0,
        extra=(mem_own,),
    )
    context, self_full, self_stats = attend(
        meta, self_limits, own, (behind,), (0,), ("behind",), state=(self_full, self_stats)
    )
    context = regroup_wide(context)
    cross_out_direct = fetch(cross_out, 0, context)
    first_normed, first_std, queries = small_call(
        partial(join_kernel, True),
        (
            shape_of((rows, width), F32),
            shape_of((rows, BLOCK), F32),
            shape_of((8, HEAD, rows), BF16),
        ),
        (place, context, self_out, *self_out_halves, tokens, gains[0], cross_q),
    )
    queries = regroup(queries)
    cross_args = (meta, cross_limits, queries, (mem_behind, mem_own, mem_ahead), (0, 0, 0), 0, "cross")
    cross_full, cross_stats = attend(
        meta,
        cross_limits,
        queries,
        (mem_own,),
        (0,),
        ("cross own",),
        copies=0,
    )
    context, cross_full, cross_stats = attend(
        meta,
        cross_limits,
        queries,
        (mem_behind, mem_ahead),
        (0, 0),
        ("cross behind", "cross ahead"),
        state=(cross_full, cross_stats),
    )
    cross_out_halves = share(cross_out_direct, cross_full)
    context = regroup_wide(context)
    second_normed, second_std = small_call(
        partial(join_kernel, False),
        (shape_of((rows, width), F32), shape_of((rows, BLOCK), F32)),
        (place, context, cross_out, *cross_out_halves, first_normed, gains[1], gains[0]),
    )

    streams = range(2)
    outputs, grad_sums, kept, branches = [], [], [], []
    for stream in streams:
        second_norm = second_normed[stream * BLOCK : (stream + 1) * BLOCK] * norm_gains[1]
        second_low = second_norm.astype(BF16)
        hidden_act, hidden_slope = gelu_both(dot(second_low, fc_in))
        adapter_act, adapter_slope = gelu_both(dot(second_low, down_w) + down_b)
        hidden_low = hidden_act.astype(BF16)
        adapter_low = adapter_act.astype(BF16)
        kept.append((second_low, hidden_slope, adapter_low, adapter_slope, second_norm))
        low = (dot(hidden_low, fc_out) + 4.0 * dot(adapter_low, up_w)).astype(BF16)
        branches.append((low, flip(low, "row", 1)))

    grad_adapters, grad_branches, lows, others = [], [], [], []
    for stream in streams:
        second_low, hidden_slope, adapter_low, adapter_slope, second_norm = kept[stream]
        low, other = branches[stream]
        other = hold(other, lows[-1] if stream else branches[1][0])
        branch = (low.astype(F32) + other.astype(F32)) + 4.0 * up_b
        result, normed, inverse_std = norm_rows(second_norm + branch, norm_gains[2])
        outputs.append(result.astype(BF16))
        grad_sums.append(
            norm_back(cotangent[stream].astype(F32), norm_gains[2], normed, inverse_std)
        )
        grad_branch = grad_sums[stream].astype(BF16)
        grad_hidden = (dot_t(grad_branch, fc_out) * hidden_slope).astype(BF16)
        grad_adapter = (4.0 * dot_t(grad_branch, up_w) * adapter_slope).astype(BF16)
        grad_hidden, grad_adapter = lax.optimization_barrier((grad_hidden, grad_adapter))
        low = (dot_t(grad_hidden, fc_in) + dot_t(grad_adapter, down_w)).astype(BF16)
        lows.append(low)
        others.append(flip(low, "row", 1))
        grad_adapters.append(grad_adapter)
        grad_branches.append(grad_branch)

    adapters = down_w.shape[1]
    message, bias_sums = small_call(
        adapter_grads_kernel,
        (shape_of((8, 128, 512), BF16), shape_of((8, 512), F32)),
        (kept[0][0], kept[1][0], *grad_adapters, *grad_branches, kept[0][2], kept[1][2]),
        extra=(others[0], lows[1]),
    )
    adapter_part = lax.psum_scatter(message, GROUP, scatter_dimension=0, tiled=True)

    grad_crossed, grad_context = small_call(
        norm_back_kernel,
        (shape_of((rows, width), F32), shape_of((8, HEAD, rows), BF16)),
        (
            *grad_sums,
            *lows,
            *others,
            gains[1],
            second_normed,
            second_std,
            cross_out,
        ),
        extra=(message,),
    )
    grad_context = regroup(grad_context)

    cross_q_direct = fetch(cross_q, 1, grad_crossed)
    grad_q, grad_behind, grad_own, grad_ahead = attend_back(
        *cross_args, grad_context, cross_full, cross_stats, extra=(cross_q_direct,)
    )
    cross_q_halves = share(cross_q_direct, grad_own)
    grad_q = regroup_wide(grad_q)
    adapter_parts = lax.all_gather(
        hold(adapter_part, grad_own), ("y", "x_hi"), axis=0, tiled=True
    )
    mem_parts = (
        grad_own,
        shift_groups(hold(grad_behind, grad_q), -1),
        shift_groups(hold(grad_ahead, grad_q), 1),
    )
    grad_mixed, grad_context = small_call(
        join_back_kernel,
        (shape_of((rows, width), F32), shape_of((8, HEAD, rows), BF16)),
        (
            place,
            grad_q,
            cross_q,
            *cross_q_halves,
            grad_crossed,
            gains[0],
            first_normed,
            first_std,
            self_out,
        ),
    )
    grad_context = regroup(grad_context)

    grad_mem = sum(part.astype(F32) for part in mem_parts).astype(BF16)
    grad_q, packed = prefix_back(
        own, prefix, prefix_rows, grad_context, self_full, self_stats, bias_sums
    )
    parts = lax.all_to_all(packed, ("y", "x_hi"), 0, 0)
    grad_q, grad_behind = attend_back(
        meta,
        self_limits,
        own,
        (behind,),
        (0,),
        0,
        "behind",
        grad_context,
        self_full,
        self_stats,
        old=grad_q,
        copies=0,
    )
    returned = shift_groups(hold(grad_behind, parts), -1)
    grad_mem = hold(grad_mem, grad_behind)
    mem_recv = regroup(grad_mem)
    grad_q, grad_own = attend_back(
        meta,
        self_limits,
        own,
        (own,),
        (HEAD,),
        4,
        "own",
        grad_context,
        self_full,
        self_stats,
        old=grad_q,
        copies=1,
        extra=(grad_mem, returned),
    )
    (small_sums,) = small_call(
        add_kernel, (shape_of((32, rows), BF16),), (parts,), extra=(mem_recv,)
    )
    adapter_part = jnp.sum(hold(adapter_parts, grad_own).astype(F32), axis=0, keepdims=True)
    adapter_total = lax.all_gather(adapter_part.astype(BF16), GROUP, axis=0, tiled=True)

    grad_kv = (grad_own.astype(F32) + returned.astype(F32)).astype(BF16)
    small_sums = jnp.broadcast_to(small_sums[None], (8, 32, rows))
    message = jnp.concatenate([grad_q, grad_kv, small_sums], axis=1)
    grads = regroup(message)
    mem_low = unproject(mem_recv, kv_w, (message,))
    mem_other = flip(mem_low, "row", 1)
    low = unproject(grads, qkv_w)
    other = flip(low, "row", 1)
    grad_memory = (mem_low.astype(F32) + mem_other.astype(F32)).astype(BF16)

    down_grad, up_grad, bias_grads, prefix_grad = small_call(
        finish_kernel,
        (
            shape_of((width, adapters), F32),
            shape_of((adapters, width), F32),
            shape_of((8, 512), F32),
            shape_of((2, 32, prefix_kv.shape[2]), F32),
        ),
        (adapter_total, grads[:, 3 * HEAD :]),
        extra=(low,),
    )
    bias_grads = bias_grads.reshape(-1)
    other = hold(other, down_grad)
    input_grad = (grad_mixed + (low.astype(F32) + other.astype(F32))).astype(BF16)
    return (
        jnp.stack(outputs),
        input_grad.reshape(inputs.shape),
        grad_memory.reshape(memory.shape),
        prefix_grad[:, :prefix_rows],
        down_grad,
        bias_grads[:adapters],
        up_grad,
        bias_grads[adapters : adapters + width],
    )


def solution(mesh):
    fine = Mesh(mesh.devices.reshape(4, 2, 4, 2, 2), SEQ + ("row",))
    in_specs = (
        P(None, SEQ, None),
        P(None, SEQ, None),
        P(None, SEQ, None),
        P(),
        P(),
        P(None, None, "row"),
        P(None, None, "row"),
        P("row", None),
        P(None, "row"),
        P(None, None, "row"),
        P("row", None),
        P(),
        P(None, "row"),
        P("row", None),
        P(None, "row"),
        P("row"),
        P("row", None),
        P(),
    )
    out_specs = (
        P(None, SEQ, None),
        P(None, SEQ, None),
        P(None, SEQ, None),
        P(None, None, "row"),
        P(None, "row"),
        P("row"),
        P("row", None),
        P(),
    )
    return jax.shard_map(
        on_device, mesh=fine, in_specs=in_specs, out_specs=out_specs, check_vma=False
    )
```

```python
from functools import partial

import jax
import jax.numpy as jnp
from jax import lax
from jax.experimental import pallas as pl
from jax.experimental.pallas import tpu as pltpu
from jax.sharding import Mesh
from jax.sharding import PartitionSpec as P

HEAD = 64
EPSILON = 1e-05
MASKED = -1000000000.0
CHUNK = 256
PREFIX_ROWS = 32
BLOCK = 128
SEQ = ("y", "x_hi", "z", "core")
GROUP = ("z", "core")
WIDE_GROUP = ("z", "core", "row")
BF16 = jnp.bfloat16
F32 = jnp.float32


def dot(left, right):
    return jnp.dot(left, right, preferred_element_type=F32)


def norm_rows(values, norm_gain):
    center = values - jnp.mean(values, axis=-1, keepdims=True)
    inverse_std = lax.rsqrt(jnp.mean(center * center, axis=-1, keepdims=True) + EPSILON)
    normed = center * inverse_std
    return (normed * norm_gain, normed, inverse_std)


def norm_back(gradient, norm_gain, normed, inverse_std):
    scaled = gradient * norm_gain
    centered = scaled - jnp.mean(scaled, axis=-1, keepdims=True)
    return (centered - normed * jnp.mean(scaled * normed, axis=-1, keepdims=True)) * inverse_std


def gelu_both(pre_act):
    cdf = 0.5 * (1.0 + lax.erf(pre_act * 0.7071067811865476))
    slope = cdf + pre_act * (0.3989422804014327 * jnp.exp(-0.5 * pre_act * pre_act))
    return (pre_act * cdf, slope)


def row_total(partial_sum):
    low = partial_sum.astype(BF16)
    other = lax.ppermute(low, "row", [(0, 1), (1, 0)])
    return low.astype(F32) + other.astype(F32)


def shift_groups(value, by):
    devices = 64
    pairs = [(i, i + 8 * by) for i in range(devices) if 0 <= i + 8 * by < devices]
    return lax.ppermute(value, SEQ, pairs)


def regroup(value):
    return lax.all_to_all(value, GROUP, 0, 0)


def regroup_wide(value):
    return lax.all_to_all(value, WIDE_GROUP, 0, 0)


def flip(value, axis_name, bit):
    size = lax.axis_size(axis_name)
    return lax.ppermute(value, axis_name, [(i, i ^ bit) for i in range(size)])


def transposed(value):
    return value.astype(F32).T.astype(BF16)


def allowed_keys(limits, chunk, meta_ref, batch, live):
    keys = lax.broadcasted_iota(jnp.int32, (CHUNK, CHUNK), 0)
    low = limits[0:1, :] - chunk * CHUNK
    high = limits[1:2, :] - chunk * CHUNK
    allowed = (keys >= low) & (keys < high)
    if live:
        first = meta_ref[batch, LIVE_AT + 2 * chunk]
        second = meta_ref[batch, LIVE_AT + 1 + 2 * chunk] + BLOCK
        allowed = allowed & (keys < jnp.where(keys < BLOCK, first, second))
    return allowed


def prefix_mask(prefix_rows):
    return lax.broadcasted_iota(jnp.int32, (PREFIX_ROWS, CHUNK), 0) < prefix_rows


def half(j):
    return slice((j % 2) * BLOCK, (j % 2 + 1) * BLOCK)


def by_count(meta_ref, batches, block, range_at, counts, body):
    firsts = [meta_ref[batch, range_at + block] for batch in batches]
    needs = [meta_ref[batch, range_at + 4 + block] - first for batch, first in zip(batches, firsts)]
    base, end = meta_ref[0, range_at + 8], meta_ref[0, range_at + 9]
    needed = needs[0]
    for need in needs[1:]:
        needed = jnp.maximum(needed, need)
    smaller = -1
    for count in counts:
        fits = needed <= count
        if count == counts[-1]:
            fits = needed > smaller
        elif smaller >= 0:
            fits = fits & (needed > smaller)

        @pl.when(fits)
        def _(count=count):
            body([jnp.maximum(jnp.minimum(first, end - count), base) for first in firsts], count)

        smaller = count


def lanes(batch):
    return slice(batch * BLOCK, (batch + 1) * BLOCK)


def any_lanes(batch):
    return pl.ds(pl.multiple_of(batch * BLOCK, BLOCK), BLOCK)


def each_block(count, body):
    def step(index, carry):
        body(index)
        return carry

    lax.fori_loop(0, count, step, 0)


def attend_kernel(kv_offsets, passes, live, prefix_rows, resume, copies, extra, meta_ref, limits_ref, q_ref, *refs):
    refs = refs[extra:]
    kv_count = len(kv_offsets)
    chunks = 4 * kv_count
    kv_refs = refs[:kv_count]
    refs = refs[kv_count:]
    if prefix_rows:
        prefix_k_ref, prefix_vt_ref = refs[:2]
        refs = refs[2:]
    if resume:
        total_ref, old_ref = refs[:2]
        refs = refs[2:]
    if copies:
        out_ref = refs[0]
        refs = refs[1:]
    full_ref, stats_ref, k_buf, vt_buf, qt_buf = refs

    for batch in range(2):
        for part in range(kv_count):
            start = kv_offsets[part]
            for j in range(8):
                chunk = chunks * batch + 4 * part + j // 2
                kv = kv_refs[part][j, start : start + 2 * HEAD, lanes(batch)]
                k_buf[chunk, half(j), :] = transposed(kv[:HEAD])
                vt_buf[chunk, :, half(j)] = kv[HEAD:]
        for j in range(8):
            qt_buf[4 * batch + j // 2, :, half(j)] = q_ref[j, 0:HEAD, lanes(batch)]

    def attend_pass(part, ranges):
        base = BASES[ranges]
        prefixed = prefix_rows > 0 and part == 0
        state = (full_ref, stats_ref) if part else (total_ref, old_ref) if resume else None
        finish = copies > 0 and part == kv_count - 1

        def attend_block(batch, block, first, count):
            queries = qt_buf[4 * batch + block]
            limits = limits_ref[batch, block]
            at = chunks * batch + 4 * part + first - base
            scores = []
            for i in range(count):
                found = dot(k_buf[at + i], queries)
                allowed = allowed_keys(limits, first + i, meta_ref, batch, live)
                scores.append(jnp.where(allowed, found, MASKED))
            if prefixed:
                found = dot(prefix_k_ref[...], queries)
                scores.append(jnp.where(prefix_mask(prefix_rows), found, MASKED))
            tops = [jnp.max(score, axis=0, keepdims=True) for score in scores]
            if state:
                old_top = state[1][batch, block, 0:1, :]
                tops.append(old_top)
            top = tops[0]
            for other in tops[1:]:
                top = jnp.maximum(top, other)
            weights = [jnp.exp(score - top) for score in scores]
            mass = sum(jnp.sum(weight, axis=0, keepdims=True) for weight in weights)
            total = sum(dot(vt_buf[at + i], weights[i].astype(BF16)) for i in range(count))
            if prefixed:
                total = total + dot(prefix_vt_ref[...], weights[count].astype(BF16))
            if state:
                shrink = jnp.exp(old_top - top)
                mass = mass + state[1][batch, block, 1:2, :] * shrink
                total = total + state[0][batch, block] * shrink
            if finish:
                mass = 1.0 / mass
                total = total * mass
            return top, mass, total

        def query_block(block):
            def body(firsts, count):
                found = [attend_block(batch, block, firsts[batch], count) for batch in range(2)]
                for batch in range(2):
                    top, mass, total = found[batch]
                    if finish:
                        low = total.astype(BF16)
                        for j in range(2):
                            for copy in range(copies):
                                out_ref[(2 * block + j) * copies + copy, :, lanes(batch)] = low[:, half(j)]
                    stats_ref[batch, block, 0:1, :] = top
                    stats_ref[batch, block, 1:2, :] = mass
                    full_ref[batch, block] = total

            by_count(meta_ref, (0, 1), block, RANGES[ranges], COUNTS[ranges], body)

        each_block(4, query_block)

    for part, ranges in enumerate(passes):
        attend_pass(part, ranges)


def score_grads(keys, values, queries, grads, stats, delta, allowed):
    scores = jnp.where(allowed, dot(keys, queries), MASKED)
    weights = jnp.exp(scores - stats[0:1, :]) * stats[1:2, :]
    grad_score = weights * (dot(values, grads) - delta)
    return weights.astype(BF16), grad_score.astype(BF16)


def attend_back_kernel(
    kv_offsets, base, live, resume, copies, range_at, counts, extra, meta_ref, limits_ref, q_ref, *refs
):
    refs = refs[extra:]
    kv_count = len(kv_offsets)
    chunks = 4 * kv_count
    kv_refs = refs[:kv_count]
    refs = refs[kv_count:]
    if resume:
        old_ref = refs[0]
        refs = refs[1:]
    grad_ref, full_ref, stats_ref = refs[:3]
    refs = refs[3:]
    dq_ref, dkv_refs = refs[0], refs[1 : 1 + kv_count]
    k_buf, kt_buf, v_buf, qt_buf, gt_buf, dk_sum, dv_sum = refs[1 + kv_count :]

    for batch in range(2):
        for part in range(kv_count):
            start = kv_offsets[part]
            for j in range(8):
                chunk = chunks * batch + 4 * part + j // 2
                kv = kv_refs[part][j, start : start + 2 * HEAD, lanes(batch)]
                k_buf[chunk, half(j), :] = transposed(kv[:HEAD])
                kt_buf[chunk, :, half(j)] = kv[:HEAD]
                v_buf[chunk, half(j), :] = transposed(kv[HEAD:])
        for j in range(8):
            qt_buf[4 * batch + j // 2, :, half(j)] = q_ref[j, 0:HEAD, lanes(batch)]
            gt_buf[4 * batch + j // 2, :, half(j)] = grad_ref[j, :, lanes(batch)]
    dk_sum[...] = jnp.zeros_like(dk_sum)
    dv_sum[...] = jnp.zeros_like(dv_sum)

    def query_block(index):
        batch, block = index // 4, index % 4
        queries = qt_buf[4 * batch + block]
        grads = gt_buf[4 * batch + block]
        limits = limits_ref[batch, block]
        stats = stats_ref[batch, block]

        def body(firsts, count):
            first = firsts[0]
            dq = old_ref[batch, block] if resume else jnp.zeros((HEAD, CHUNK), F32)
            if count:
                queries_r = transposed(queries)
                grads_r = transposed(grads)
                delta = jnp.sum(grads.astype(F32) * full_ref[batch, block], axis=0, keepdims=True)
            for i in range(count):
                chunk = first + i
                at = chunks * batch + chunk - base
                allowed = allowed_keys(limits, chunk, meta_ref, batch, live)
                weights, grad_score = score_grads(
                    k_buf[at], v_buf[at], queries, grads, stats, delta, allowed
                )
                dk_sum[at] += dot(grad_score, queries_r)
                dv_sum[at] += dot(weights, grads_r)
                dq = dq + dot(kt_buf[at], grad_score)
            if copies:
                low = dq.astype(BF16) * 0.125
                for j in range(2):
                    for copy in range(copies):
                        dq_ref[(2 * block + j) * copies + copy, :, any_lanes(batch)] = low[:, half(j)]
            else:
                dq_ref[batch, block] = dq

        by_count(meta_ref, (batch,), block, range_at, counts, body)

    each_block(8, query_block)

    for batch in range(2):
        for part in range(kv_count):
            for j in range(8):
                chunk = chunks * batch + 4 * part + j // 2
                dkv_refs[part][j, 0:HEAD, lanes(batch)] = dk_sum[chunk, half(j), :].T.astype(BF16)
                dkv_refs[part][j, HEAD : 2 * HEAD, lanes(batch)] = dv_sum[chunk, half(j), :].T.astype(BF16)


def prefix_back_kernel(
    prefix_rows, q_ref, k_ref, kt_ref, v_ref, grad_ref, full_ref, stats_ref, bias_ref, dq_ref, out_ref
):
    dk = jnp.zeros((PREFIX_ROWS, HEAD), F32)
    dv = jnp.zeros((PREFIX_ROWS, HEAD), F32)
    for batch in range(2):
        for block in range(4):
            queries = jnp.concatenate(
                [q_ref[2 * block + j, 0:HEAD, lanes(batch)] for j in range(2)], axis=1
            )
            grads = jnp.concatenate([grad_ref[2 * block + j, :, lanes(batch)] for j in range(2)], axis=1)
            delta = jnp.sum(grads.astype(F32) * full_ref[batch, block], axis=0, keepdims=True)
            weights, grad_score = score_grads(
                k_ref[...],
                v_ref[...],
                queries,
                grads,
                stats_ref[batch, block],
                delta,
                prefix_mask(prefix_rows),
            )
            dq_ref[batch, block] = dot(kt_ref[...], grad_score)
            dk = dk + dot(grad_score, transposed(queries))
            dv = dv + dot(weights, transposed(grads))
    pieces = [value[8 * j : 8 * j + 8] for value in (dk, dv) for j in range(4)]
    small = jnp.concatenate([jnp.concatenate(pieces, axis=1), bias_ref[...]], axis=0).astype(BF16)
    for group in range(8):
        out_ref[group] = small


def pinned(*values):
    return [pltpu.with_memory_space_constraint(value, pltpu.VMEM) for value in values]


def shape_of(shape, dtype):
    return jax.ShapeDtypeStruct(shape, dtype)


COST = pl.CostEstimate(flops=1000, bytes_accessed=1000, transcendentals=0)
VMEM_LIMIT = 63 * 10**6
PARAMS = pltpu.CompilerParams(vmem_limit_bytes=VMEM_LIMIT)
IN_VMEM = pl.BlockSpec(memory_space=pltpu.VMEM)
ANYWHERE = pl.BlockSpec(memory_space=pl.ANY)

RANGES = {"own": 0, "behind": 10, "cross": 20, "cross own": 30, "cross behind": 40, "cross ahead": 50}
BASES = {"own": 4, "behind": 0, "cross": 0, "cross own": 4, "cross behind": 0, "cross ahead": 8}
LIVE_AT = 60
COUNTS = {
    "own": (1, 2, 3, 4),
    "behind": (0, 1, 2, 3, 4),
    "cross": (1, 2, 3, 4, 5, 6, 8, 10, 12),
    "cross own": (1, 2, 3, 4),
    "cross behind": (0, 1, 2, 4),
    "cross ahead": (0, 1, 2, 4),
}


def attend(meta, limits, queries, kvs, kv_offsets, passes, prefix=None, prefix_rows=0, state=None, copies=2, extra=()):
    chunks = 4 * len(kvs)
    operands = pinned(*kvs) if len(kvs) == 1 else [*kvs]
    if prefix_rows:
        operands += [prefix[0], prefix[1].T]
    if state is not None:
        operands += pinned(*state)
    state_shape = shape_of if copies else pltpu.VMEM
    out_shape = [state_shape((2, 4, HEAD, CHUNK), F32), state_shape((2, 4, 8, CHUNK), F32)]
    if copies:
        out_shape.insert(0, shape_of((8 * copies, HEAD, 2 * BLOCK), BF16))
    kernel = partial(
        attend_kernel,
        kv_offsets,
        passes,
        not passes[0].startswith("cross"),
        prefix_rows,
        state is not None,
        copies,
        len(extra),
    )
    return pl.pallas_call(
        kernel,
        out_shape=tuple(out_shape),
        in_specs=[pl.BlockSpec(memory_space=pltpu.SMEM), IN_VMEM, IN_VMEM]
        + [ANYWHERE] * len(extra)
        + [IN_VMEM] * len(operands),
        out_specs=tuple(IN_VMEM for _ in out_shape),
        scratch_shapes=[
            pltpu.VMEM((2 * chunks, CHUNK, HEAD), BF16),
            pltpu.VMEM((2 * chunks, HEAD, CHUNK), BF16),
            pltpu.VMEM((8, HEAD, CHUNK), BF16),
        ],
        compiler_params=PARAMS,
        cost_estimate=COST,
    )(meta, limits, *pinned(queries), *extra, *operands)


def attend_back(
    meta, limits, queries, kvs, kv_offsets, base, ranges, grads, full, stats, old=None, copies=2, extra=()
):
    chunks = 4 * len(kvs)
    operands = [*kvs]
    if copies:
        out_shape = [shape_of((8 * copies, HEAD, 2 * BLOCK), BF16)]
    else:
        out_shape = [shape_of((2, 4, HEAD, CHUNK), F32)]
    for _ in kvs:
        out_shape.append(shape_of((8, 2 * HEAD, 2 * BLOCK), BF16))
    if old is not None:
        operands.append(old)
    operands += [*pinned(grads), full, stats]
    kernel = partial(
        attend_back_kernel,
        kv_offsets,
        base,
        ranges != "cross",
        old is not None,
        copies,
        RANGES[ranges],
        COUNTS[ranges],
        len(extra),
    )
    return pl.pallas_call(
        kernel,
        out_shape=tuple(out_shape),
        in_specs=[pl.BlockSpec(memory_space=pltpu.SMEM), IN_VMEM, IN_VMEM]
        + [ANYWHERE] * len(extra)
        + [IN_VMEM] * len(operands),
        out_specs=tuple(IN_VMEM for _ in out_shape),
        scratch_shapes=[
            pltpu.VMEM((2 * chunks, CHUNK, HEAD), BF16),
            pltpu.VMEM((2 * chunks, HEAD, CHUNK), BF16),
            pltpu.VMEM((2 * chunks, CHUNK, HEAD), BF16),
            pltpu.VMEM((8, HEAD, CHUNK), BF16),
            pltpu.VMEM((8, HEAD, CHUNK), BF16),
            pltpu.VMEM((2 * chunks, CHUNK, HEAD), F32),
            pltpu.VMEM((2 * chunks, CHUNK, HEAD), F32),
        ],
        compiler_params=PARAMS,
        cost_estimate=COST,
    )(meta, limits, queries, *extra, *operands)


def prefix_back(queries, prefix, prefix_rows, grads, full, stats, biases):
    return pl.pallas_call(
        partial(prefix_back_kernel, prefix_rows),
        out_shape=(shape_of((2, 4, HEAD, CHUNK), F32), shape_of((8, 16, 512), BF16)),
        in_specs=[IN_VMEM] * 8,
        out_specs=(IN_VMEM, IN_VMEM),
        compiler_params=PARAMS,
        cost_estimate=COST,
    )(queries, prefix[0], prefix[0].T, prefix[1], *pinned(grads), full, stats, biases)


def dot_t(left, right):
    return lax.dot_general(left, right, (((1,), (1,)), ((), ())), preferred_element_type=F32)


def tdot(left, right):
    return lax.dot_general(left, right, (((0,), (0,)), ((), ())), preferred_element_type=F32)


def small_call(kernel, out_shape, operands, extra=()):
    specs = [IN_VMEM] * len(operands)
    specs += [pl.BlockSpec(memory_space=pl.ANY)] * len(extra)
    count = len(operands)
    return pl.pallas_call(
        lambda *refs: kernel(*refs[:count], *refs[count + len(extra) :]),
        out_shape=tuple(out_shape),
        in_specs=specs,
        out_specs=tuple(pl.BlockSpec(memory_space=pltpu.VMEM) for _ in out_shape),
        compiler_params=pltpu.CompilerParams(vmem_limit_bytes=VMEM_LIMIT),
        cost_estimate=COST,
    )(*operands, *extra)


def store_heads(out_ref, turned):
    for h in range(8):
        out_ref[h] = turned[h * HEAD : (h + 1) * HEAD].astype(BF16)


def project_kernel(scaled, x_ref, w_ref, *refs):
    out_ref = refs[-1]
    y = dot(x_ref[...], w_ref[0])
    if scaled:
        y = y * jnp.where(pl.program_id(0) == 0, 0.125, 1.0)
    store_heads(out_ref, y.T)


def project(tokens, weights, scaled, extra=()):
    parts = weights.shape[0]
    return pl.pallas_call(
        partial(project_kernel, scaled),
        out_shape=shape_of((8, parts * HEAD, tokens.shape[0]), BF16),
        grid=(parts,),
        in_specs=[
            pl.BlockSpec(tokens.shape, lambda i: (0, 0)),
            pl.BlockSpec((1,) + weights.shape[1:], lambda i: (i, 0, 0)),
        ]
        + [pl.BlockSpec(memory_space=pl.ANY)] * len(extra),
        out_specs=pl.BlockSpec((8, HEAD, tokens.shape[0]), lambda i: (0, i, 0)),
        compiler_params=pltpu.CompilerParams(vmem_limit_bytes=VMEM_LIMIT),
        cost_estimate=COST,
    )(tokens, weights, *extra)


def unproject_kernel(grads_ref, w_ref, *refs):
    out_ref, total = refs[-2:]
    part = pl.program_id(0)
    turned = jnp.concatenate([grads_ref[h] for h in range(8)], axis=0)
    value = dot_t(transposed(turned), w_ref[0])

    @pl.when(part == 0)
    def _():
        total[...] = value

    @pl.when(part > 0)
    def _():
        total[...] += value

    @pl.when(part == pl.num_programs(0) - 1)
    def _():
        out_ref[...] = total[...].astype(BF16)


def unproject(grads, weights, extra=()):
    parts, width, tokens = weights.shape[0], weights.shape[1], grads.shape[2]
    return pl.pallas_call(
        unproject_kernel,
        out_shape=shape_of((tokens, width), BF16),
        grid=(parts,),
        in_specs=[
            pl.BlockSpec((8, HEAD, tokens), lambda i: (0, i, 0)),
            pl.BlockSpec((1,) + weights.shape[1:], lambda i: (i, 0, 0)),
        ]
        + [pl.BlockSpec(memory_space=pl.ANY)] * len(extra),
        out_specs=pl.BlockSpec((tokens, width), lambda i: (0, 0)),
        scratch_shapes=[pltpu.VMEM((tokens, width), F32)],
        compiler_params=pltpu.CompilerParams(vmem_limit_bytes=VMEM_LIMIT),
        cost_estimate=COST,
    )(grads, weights, *extra)


def whole_weight(place_ref, own_ref, direct_ref, shared_ref, axis):
    first_row, first_core = place_ref[0, 0:1, 0:1] == 0.0, place_ref[1, 0:1, 0:1] == 0.0
    direct, shared = direct_ref[...], shared_ref[...]
    first = jnp.where(first_core, direct, shared)
    last = jnp.where(first_core, shared, direct)
    other = jnp.concatenate([first, last], axis=axis)
    own = own_ref[...]
    return jnp.where(first_row, own, other), jnp.where(first_row, other, own)


def wide_rows(value_ref, row):
    return transposed(jnp.concatenate([value_ref[2 * h + row] for h in range(8)], axis=0))


def join_kernel(has_next, place_ref, context_ref, own_ref, direct_ref, shared_ref, base_ref, gain_ref, *refs):
    if has_next:
        next_ref, normed_ref, std_ref, out_ref = refs
        base = base_ref[...].astype(F32)
    else:
        base_gain_ref, normed_ref, std_ref = refs
        base = base_ref[...] * base_gain_ref[...]
    first, last = whole_weight(place_ref, own_ref, direct_ref, shared_ref, 0)
    mixed = base + (dot(wide_rows(context_ref, 0), first) + dot(wide_rows(context_ref, 1), last))
    normed, inverse_std = norm_parts(mixed)
    normed_ref[...] = normed
    std_ref[...] = jnp.broadcast_to(inverse_std, std_ref.shape)
    if has_next:
        low = (normed * gain_ref[...]).astype(BF16)
        store_heads(out_ref, (0.125 * dot(low, next_ref[...])).T)


def norm_parts(values):
    center = values - jnp.mean(values, axis=-1, keepdims=True)
    inverse_std = lax.rsqrt(jnp.mean(center * center, axis=-1, keepdims=True) + EPSILON)
    return center * inverse_std, inverse_std


def norm_back_kernel(*refs):
    sums, lows, others = refs[0:2], refs[2:4], refs[4:6]
    gain_ref, normed_ref, std_ref, weight_ref, grad_ref, out_ref = refs[6:]
    for stream in range(2):
        at = slice(stream * BLOCK, (stream + 1) * BLOCK)
        both = lows[stream][...].astype(F32) + others[stream][...].astype(F32)
        grad_ref[at, :] = norm_back(
            sums[stream][...] + both, gain_ref[...], normed_ref[at, :], std_ref[at, 0:1]
        )
    store_heads(out_ref, dot_t(weight_ref[...], grad_ref[...].astype(BF16)))


def adapter_grads_kernel(*refs):
    second, grad_adapter, branch, adapter = refs[0:2], refs[2:4], refs[4:6], refs[6:8]
    out_ref, bias_ref = refs[8:]

    def both(pair):
        return jnp.concatenate([pair[0][...], pair[1][...]], axis=0)

    grad_adapters, branches = both(grad_adapter), both(branch)
    down = dot(transposed(both(second)), grad_adapters)
    up = 4.0 * dot(transposed(branches), both(adapter))
    half_width = down.shape[1]
    for i in range(8):
        at = slice(i * 128, (i + 1) * 128)
        out_ref[i, :, 0:half_width] = down[at].astype(BF16)
        out_ref[i, :, half_width:] = up[at].astype(BF16)
    down_bias = jnp.sum(grad_adapters.astype(F32), axis=0, keepdims=True)
    up_bias = 4.0 * jnp.sum(branches.astype(F32), axis=0, keepdims=True)
    extra = jnp.concatenate([down_bias, up_bias, jnp.zeros((1, 256), F32)], axis=1)
    pieces = [extra[:, i * 512 : (i + 1) * 512] for i in range(3)]
    bias_ref[...] = jnp.concatenate(pieces + [jnp.zeros((5, 512), F32)], axis=0)


def add_kernel(parts_ref, small_ref):
    total = parts_ref[0].astype(F32)
    for group in range(1, 8):
        total = total + parts_ref[group].astype(F32)
    small = total.astype(BF16)
    small_ref[0:16, :] = small[:, 0:256]
    small_ref[16:32, :] = small[:, 256:512]


def finish_kernel(total_ref, small_ref, down_ref, up_ref, bias_ref, prefix_ref):
    half_width = down_ref.shape[1]
    for i in range(8):
        block = total_ref[i].astype(F32)
        at = slice(i * 128, (i + 1) * 128)
        down_ref[at, :] = block[:, 0:half_width]
        up_ref[:, at] = block[:, half_width:].T
    biases = [jnp.zeros((8, 256), F32)] * 2
    for i in range(2):
        for j in range(4):
            pieces = []
            for head in range(8):
                pieces.append(small_ref[head, 16 * i : 16 * i + 16, :].astype(F32)[0:8, 64 * j : 64 * j + 64])
            prefix_ref[i, 8 * j : 8 * j + 8, :] = jnp.concatenate(pieces, axis=1)
        for head in range(8):
            biases[i] = biases[i] + small_ref[head, 16 * i : 16 * i + 16, :].astype(F32)[8:16]
    bias_ref[...] = jnp.concatenate(biases, axis=1)


def join_back_kernel(
    place_ref,
    grad_q_ref,
    own_ref,
    direct_ref,
    shared_ref,
    base_ref,
    gain_ref,
    normed_ref,
    std_ref,
    weight_ref,
    grad_ref,
    out_ref,
):
    first, last = whole_weight(place_ref, own_ref, direct_ref, shared_ref, 1)
    gradient = base_ref[...] + (
        dot_t(wide_rows(grad_q_ref, 0), first) + dot_t(wide_rows(grad_q_ref, 1), last)
    )
    grad = norm_back(gradient, gain_ref[...], normed_ref[...], std_ref[:, 0:1])
    grad_ref[...] = grad
    store_heads(out_ref, dot_t(weight_ref[...], grad.astype(BF16)))


def positions(doc_lens, counts, group):
    docs = doc_lens.shape[1]
    upto = jnp.arange(docs)[:, None] <= jnp.arange(docs)[None, :]
    ends = jnp.sum(jnp.where(upto[None], doc_lens[:, :, None], 0), axis=1)
    slots = group * 1024 + jnp.arange(1024, dtype=jnp.int32)
    passed = ends[:, :, None] <= slots[None, None, :]
    origin = (group - 1) * 1024
    start = jnp.max(jnp.where(passed, ends[:, :, None], 0), axis=1) - origin
    stop = jnp.min(jnp.where(passed, 8192, ends[:, :, None]), axis=1) - origin
    own = jnp.broadcast_to(slots[None] - origin + 1, start.shape)

    def limits(low, high):
        both = jnp.stack([low, high], axis=1).reshape(2, 2, 4, CHUNK).transpose(0, 2, 1, 3)
        return jnp.pad(both, ((0, 0), (0, 0), (0, 6), (0, 0)))

    first = start[:, ::CHUNK] // CHUNK
    self_last = jnp.broadcast_to(jnp.arange(5, 9, dtype=jnp.int32)[None], first.shape)
    cross_last = (stop[:, CHUNK - 1 :: CHUNK] + (CHUNK - 1)) // CHUNK

    def columns(last, low, high):
        ends = jnp.broadcast_to(jnp.array([[low, high]], jnp.int32), (2, 2))
        return [jnp.clip(first, low, high), jnp.clip(last, low, high), ends]

    blocks = jnp.arange(16, dtype=jnp.int32) + (group - 1) * 8
    at = blocks[:, None] == jnp.arange(64, dtype=jnp.int32)[None]
    window_counts = jnp.sum(jnp.where(at[None], counts[:, None, :], 0), axis=2)
    meta = columns(self_last, 4, 8) + columns(self_last, 0, 4) + columns(cross_last, 0, 12)
    meta += columns(cross_last, 4, 8) + columns(cross_last, 0, 4) + columns(cross_last, 8, 12)
    meta += [window_counts]
    return (jnp.concatenate(meta, axis=1), limits(start, own), limits(start, stop))


def hold(value, *earlier):
    any_space = pl.BlockSpec(memory_space=pl.ANY)
    return pl.pallas_call(
        lambda *refs: None,
        out_shape=shape_of(value.shape, value.dtype),
        in_specs=[any_space] * (1 + len(earlier)),
        out_specs=any_space,
        input_output_aliases={0: 0},
        cost_estimate=COST,
    )(value, *earlier)


def on_device(
    inputs,
    memory,
    cotangent,
    doc_lens,
    counts,
    prefix_kv,
    self_qkv,
    self_out,
    cross_q,
    cross_kv,
    cross_out,
    norm_gains,
    fc_in,
    fc_out,
    down_w,
    down_b,
    up_w,
    up_b,
):
    width = inputs.shape[2]
    rows = 2 * BLOCK
    prefix_rows = prefix_kv.shape[1]
    core, row = lax.axis_index("core"), lax.axis_index("row")
    group = lax.axis_index("y") * 2 + lax.axis_index("x_hi")
    head = lax.axis_index("z") * 2 + core
    place = jnp.broadcast_to(jnp.stack([row, core]).astype(F32)[:, None, None], (2, 1, BLOCK))
    meta, self_limits, cross_limits = positions(doc_lens, counts, group)
    prefix = lax.dynamic_slice_in_dim(prefix_kv, head * HEAD, HEAD, 2)
    prefix = jnp.pad(prefix, ((0, 0), (0, PREFIX_ROWS - prefix_rows), (0, 0)))
    gains = [norm_gains[i : i + 1] for i in range(3)]
    tokens = inputs.reshape(rows, width)
    qkv_w = jnp.transpose(self_qkv, (1, 0, 2))
    kv_w = jnp.transpose(cross_kv, (1, 0, 2))

    def share(direct, *earlier):
        held = hold(direct, *earlier)
        return held, flip(held, "core", 1)

    def fetch(weight, axis, *earlier):
        size = weight.shape[axis] // 2
        mine = lax.dynamic_slice_in_dim(weight, core * size, size, axis)
        return flip(hold(mine, *earlier) if earlier else mine, "row", 1)

    projected = project(tokens, qkv_w, True)
    own = regroup(projected)
    self_out_direct = fetch(self_out, 0)
    behind = shift_groups(own[:, HEAD:, :], 1)
    mem_projected = project(memory.reshape(rows, width), kv_w, False, (projected,))
    mem_own = regroup(hold(mem_projected, own))
    mem_behind = shift_groups(mem_own, 1)
    mem_ahead = shift_groups(mem_own, -1)
    self_out_halves = share(self_out_direct, mem_own)

    self_full, self_stats = attend(
        meta,
        self_limits,
        own,
        (own,),
        (HEAD,),
        ("own",),
        prefix,
        prefix_rows,
        copies=0,
        extra=(mem_own,),
    )
    context, self_full, self_stats = attend(
        meta, self_limits, own, (behind,), (0,), ("behind",), state=(self_full, self_stats)
    )
    context = regroup_wide(context)
    cross_out_direct = fetch(cross_out, 0, context)
    first_normed, first_std, queries = small_call(
        partial(join_kernel, True),
        (
            shape_of((rows, width), F32),
            shape_of((rows, BLOCK), F32),
            shape_of((8, HEAD, rows), BF16),
        ),
        (place, context, self_out, *self_out_halves, tokens, gains[0], cross_q),
    )
    queries = regroup(queries)
    cross_args = (meta, cross_limits, queries, (mem_behind, mem_own, mem_ahead), (0, 0, 0), 0, "cross")
    cross_full, cross_stats = attend(
        meta,
        cross_limits,
        queries,
        (mem_own,),
        (0,),
        ("cross own",),
        copies=0,
    )
    context, cross_full, cross_stats = attend(
        meta,
        cross_limits,
        queries,
        (mem_behind, mem_ahead),
        (0, 0),
        ("cross behind", "cross ahead"),
        state=(cross_full, cross_stats),
    )
    cross_out_halves = share(cross_out_direct, cross_full)
    context = regroup_wide(context)
    second_normed, second_std = small_call(
        partial(join_kernel, False),
        (shape_of((rows, width), F32), shape_of((rows, BLOCK), F32)),
        (place, context, cross_out, *cross_out_halves, first_normed, gains[1], gains[0]),
    )

    streams = range(2)
    outputs, grad_sums, kept, branches = [], [], [], []
    for stream in streams:
        second_norm = second_normed[stream * BLOCK : (stream + 1) * BLOCK] * norm_gains[1]
        second_low = second_norm.astype(BF16)
        hidden_act, hidden_slope = gelu_both(dot(second_low, fc_in))
        adapter_act, adapter_slope = gelu_both(dot(second_low, down_w) + down_b)
        hidden_low = hidden_act.astype(BF16)
        adapter_low = adapter_act.astype(BF16)
        kept.append((second_low, hidden_slope, adapter_low, adapter_slope, second_norm))
        low = (dot(hidden_low, fc_out) + 4.0 * dot(adapter_low, up_w)).astype(BF16)
        branches.append((low, flip(low, "row", 1)))

    grad_adapters, grad_branches, lows, others = [], [], [], []
    for stream in streams:
        second_low, hidden_slope, adapter_low, adapter_slope, second_norm = kept[stream]
        low, other = branches[stream]
        other = hold(other, lows[-1] if stream else branches[1][0])
        branch = (low.astype(F32) + other.astype(F32)) + 4.0 * up_b
        result, normed, inverse_std = norm_rows(second_norm + branch, norm_gains[2])
        outputs.append(result.astype(BF16))
        grad_sums.append(
            norm_back(cotangent[stream].astype(F32), norm_gains[2], normed, inverse_std)
        )
        grad_branch = grad_sums[stream].astype(BF16)
        grad_hidden = (dot_t(grad_branch, fc_out) * hidden_slope).astype(BF16)
        grad_adapter = (4.0 * dot_t(grad_branch, up_w) * adapter_slope).astype(BF16)
        grad_hidden, grad_adapter = lax.optimization_barrier((grad_hidden, grad_adapter))
        low = (dot_t(grad_hidden, fc_in) + dot_t(grad_adapter, down_w)).astype(BF16)
        lows.append(low)
        others.append(flip(low, "row", 1))
        grad_adapters.append(grad_adapter)
        grad_branches.append(grad_branch)

    adapters = down_w.shape[1]
    message, bias_sums = small_call(
        adapter_grads_kernel,
        (shape_of((8, 128, 512), BF16), shape_of((8, 512), F32)),
        (kept[0][0], kept[1][0], *grad_adapters, *grad_branches, kept[0][2], kept[1][2]),
        extra=(others[0], lows[1]),
    )
    adapter_part = lax.psum_scatter(message, GROUP, scatter_dimension=0, tiled=True)

    grad_crossed, grad_context = small_call(
        norm_back_kernel,
        (shape_of((rows, width), F32), shape_of((8, HEAD, rows), BF16)),
        (
            *grad_sums,
            *lows,
            *others,
            gains[1],
            second_normed,
            second_std,
            cross_out,
        ),
        extra=(message,),
    )
    grad_context = regroup(grad_context)

    cross_q_direct = fetch(cross_q, 1, grad_crossed)
    grad_q, grad_behind, grad_own, grad_ahead = attend_back(
        *cross_args, grad_context, cross_full, cross_stats, extra=(cross_q_direct,)
    )
    cross_q_halves = share(cross_q_direct, grad_own)
    grad_q = regroup_wide(grad_q)
    adapter_parts = lax.all_gather(
        hold(adapter_part, grad_own), ("y", "x_hi"), axis=0, tiled=True
    )
    mem_parts = (
        grad_own,
        shift_groups(hold(grad_behind, grad_q), -1),
        shift_groups(hold(grad_ahead, grad_q), 1),
    )
    grad_mixed, grad_context = small_call(
        join_back_kernel,
        (shape_of((rows, width), F32), shape_of((8, HEAD, rows), BF16)),
        (
            place,
            grad_q,
            cross_q,
            *cross_q_halves,
            grad_crossed,
            gains[0],
            first_normed,
            first_std,
            self_out,
        ),
    )
    grad_context = regroup(grad_context)

    grad_mem = sum(part.astype(F32) for part in mem_parts).astype(BF16)
    grad_q, packed = prefix_back(
        own, prefix, prefix_rows, grad_context, self_full, self_stats, bias_sums
    )
    parts = lax.all_to_all(packed, ("y", "x_hi"), 0, 0)
    grad_q, grad_behind = attend_back(
        meta,
        self_limits,
        own,
        (behind,),
        (0,),
        0,
        "behind",
        grad_context,
        self_full,
        self_stats,
        old=grad_q,
        copies=0,
    )
    adapter_part = jnp.sum(hold(adapter_parts, grad_behind).astype(F32), axis=0, keepdims=True)
    adapter_total = lax.all_gather(adapter_part.astype(BF16), GROUP, axis=0, tiled=True)
    returned = shift_groups(hold(grad_behind, parts), -1)
    grad_mem = hold(grad_mem, grad_behind)
    mem_recv = regroup(grad_mem)
    grad_q, grad_own = attend_back(
        meta,
        self_limits,
        own,
        (own,),
        (HEAD,),
        4,
        "own",
        grad_context,
        self_full,
        self_stats,
        old=grad_q,
        copies=1,
        extra=(grad_mem, returned),
    )
    (small_sums,) = small_call(
        add_kernel, (shape_of((32, rows), BF16),), (parts,), extra=(mem_recv, grad_own)
    )

    grad_kv = (grad_own.astype(F32) + returned.astype(F32)).astype(BF16)
    small_sums = jnp.broadcast_to(small_sums[None], (8, 32, rows))
    message = jnp.concatenate([grad_q, grad_kv, small_sums], axis=1)
    grads = regroup(message)
    mem_low = unproject(mem_recv, kv_w, (message,))
    mem_other = flip(mem_low, "row", 1)
    low = unproject(grads, qkv_w)
    other = flip(low, "row", 1)
    grad_memory = (mem_low.astype(F32) + mem_other.astype(F32)).astype(BF16)

    down_grad, up_grad, bias_grads, prefix_grad = small_call(
        finish_kernel,
        (
            shape_of((width, adapters), F32),
            shape_of((adapters, width), F32),
            shape_of((8, 512), F32),
            shape_of((2, 32, prefix_kv.shape[2]), F32),
        ),
        (adapter_total, grads[:, 3 * HEAD :]),
        extra=(low,),
    )
    bias_grads = bias_grads.reshape(-1)
    other = hold(other, down_grad)
    input_grad = (grad_mixed + (low.astype(F32) + other.astype(F32))).astype(BF16)
    return (
        jnp.stack(outputs),
        input_grad.reshape(inputs.shape),
        grad_memory.reshape(memory.shape),
        prefix_grad[:, :prefix_rows],
        down_grad,
        bias_grads[:adapters],
        up_grad,
        bias_grads[adapters : adapters + width],
    )


def solution(mesh):
    fine = Mesh(mesh.devices.reshape(4, 2, 4, 2, 2), SEQ + ("row",))
    in_specs = (
        P(None, SEQ, None),
        P(None, SEQ, None),
        P(None, SEQ, None),
        P(),
        P(),
        P(None, None, "row"),
        P(None, None, "row"),
        P("row", None),
        P(None, "row"),
        P(None, None, "row"),
        P("row", None),
        P(),
        P(None, "row"),
        P("row", None),
        P(None, "row"),
        P("row"),
        P("row", None),
        P(),
    )
    out_specs = (
        P(None, SEQ, None),
        P(None, SEQ, None),
        P(None, SEQ, None),
        P(None, None, "row"),
        P(None, "row"),
        P("row"),
        P("row", None),
        P(),
    )
    return jax.shard_map(
        on_device, mesh=fine, in_specs=in_specs, out_specs=out_specs, check_vma=False
    )
```

```python
from functools import partial

import jax
import jax.numpy as jnp
from jax import lax
from jax.experimental import pallas as pl
from jax.experimental.pallas import tpu as pltpu
from jax.sharding import Mesh
from jax.sharding import PartitionSpec as P

HEAD = 64
EPSILON = 1e-05
MASKED = -1000000000.0
CHUNK = 256
PREFIX_ROWS = 32
BLOCK = 128
SEQ = ("y", "x_hi", "z", "core")
GROUP = ("z", "core")
WIDE_GROUP = ("z", "core", "row")
BF16 = jnp.bfloat16
F32 = jnp.float32


def dot(left, right):
    return jnp.dot(left, right, preferred_element_type=F32)


def norm_rows(values, norm_gain):
    center = values - jnp.mean(values, axis=-1, keepdims=True)
    inverse_std = lax.rsqrt(jnp.mean(center * center, axis=-1, keepdims=True) + EPSILON)
    normed = center * inverse_std
    return (normed * norm_gain, normed, inverse_std)


def norm_back(gradient, norm_gain, normed, inverse_std):
    scaled = gradient * norm_gain
    centered = scaled - jnp.mean(scaled, axis=-1, keepdims=True)
    return (centered - normed * jnp.mean(scaled * normed, axis=-1, keepdims=True)) * inverse_std


def gelu_both(pre_act):
    cdf = 0.5 * (1.0 + lax.erf(pre_act * 0.7071067811865476))
    slope = cdf + pre_act * (0.3989422804014327 * jnp.exp(-0.5 * pre_act * pre_act))
    return (pre_act * cdf, slope)


def row_total(partial_sum):
    low = partial_sum.astype(BF16)
    other = lax.ppermute(low, "row", [(0, 1), (1, 0)])
    return low.astype(F32) + other.astype(F32)


def shift_groups(value, by):
    devices = 64
    pairs = [(i, i + 8 * by) for i in range(devices) if 0 <= i + 8 * by < devices]
    return lax.ppermute(value, SEQ, pairs)


def regroup(value):
    return lax.all_to_all(value, GROUP, 0, 0)


def regroup_wide(value):
    return lax.all_to_all(value, WIDE_GROUP, 0, 0)


def flip(value, axis_name, bit):
    size = lax.axis_size(axis_name)
    return lax.ppermute(value, axis_name, [(i, i ^ bit) for i in range(size)])


def transposed(value):
    return value.astype(F32).T.astype(BF16)


def allowed_keys(limits, chunk, meta_ref, batch, live):
    keys = lax.broadcasted_iota(jnp.int32, (CHUNK, CHUNK), 0)
    low = limits[0:1, :] - chunk * CHUNK
    high = limits[1:2, :] - chunk * CHUNK
    allowed = (keys >= low) & (keys < high)
    if live:
        first = meta_ref[batch, LIVE_AT + 2 * chunk]
        second = meta_ref[batch, LIVE_AT + 1 + 2 * chunk] + BLOCK
        allowed = allowed & (keys < jnp.where(keys < BLOCK, first, second))
    return allowed


def prefix_mask(prefix_rows):
    return lax.broadcasted_iota(jnp.int32, (PREFIX_ROWS, CHUNK), 0) < prefix_rows


def half(j):
    return slice((j % 2) * BLOCK, (j % 2 + 1) * BLOCK)


def by_count(meta_ref, batches, block, range_at, counts, body):
    firsts = [meta_ref[batch, range_at + block] for batch in batches]
    needs = [meta_ref[batch, range_at + 4 + block] - first for batch, first in zip(batches, firsts)]
    base, end = meta_ref[0, range_at + 8], meta_ref[0, range_at + 9]
    needed = needs[0]
    for need in needs[1:]:
        needed = jnp.maximum(needed, need)
    smaller = -1
    for count in counts:
        fits = needed <= count
        if count == counts[-1]:
            fits = needed > smaller
        elif smaller >= 0:
            fits = fits & (needed > smaller)

        @pl.when(fits)
        def _(count=count):
            body([jnp.maximum(jnp.minimum(first, end - count), base) for first in firsts], count)

        smaller = count


def lanes(batch):
    return slice(batch * BLOCK, (batch + 1) * BLOCK)


def any_lanes(batch):
    return pl.ds(pl.multiple_of(batch * BLOCK, BLOCK), BLOCK)


def each_block(count, body):
    def step(index, carry):
        body(index)
        return carry

    lax.fori_loop(0, count, step, 0)


def attend_kernel(kv_offsets, passes, live, prefix_rows, resume, copies, extra, meta_ref, limits_ref, q_ref, *refs):
    refs = refs[extra:]
    kv_count = len(kv_offsets)
    chunks = 4 * kv_count
    kv_refs = refs[:kv_count]
    refs = refs[kv_count:]
    if prefix_rows:
        prefix_k_ref, prefix_vt_ref = refs[:2]
        refs = refs[2:]
    if resume:
        total_ref, old_ref = refs[:2]
        refs = refs[2:]
    if copies:
        out_ref = refs[0]
        refs = refs[1:]
    full_ref, stats_ref, k_buf, vt_buf, qt_buf = refs

    for batch in range(2):
        for part in range(kv_count):
            start = kv_offsets[part]
            for j in range(8):
                chunk = chunks * batch + 4 * part + j // 2
                kv = kv_refs[part][j, start : start + 2 * HEAD, lanes(batch)]
                k_buf[chunk, half(j), :] = transposed(kv[:HEAD])
                vt_buf[chunk, :, half(j)] = kv[HEAD:]
        for j in range(8):
            qt_buf[4 * batch + j // 2, :, half(j)] = q_ref[j, 0:HEAD, lanes(batch)]

    def attend_pass(part, ranges):
        base = BASES[ranges]
        prefixed = prefix_rows > 0 and part == 0
        state = (full_ref, stats_ref) if part else (total_ref, old_ref) if resume else None
        finish = copies > 0 and part == kv_count - 1

        def attend_block(batch, block, first, count):
            queries = qt_buf[4 * batch + block]
            limits = limits_ref[batch, block]
            at = chunks * batch + 4 * part + first - base
            scores = []
            for i in range(count):
                found = dot(k_buf[at + i], queries)
                allowed = allowed_keys(limits, first + i, meta_ref, batch, live)
                scores.append(jnp.where(allowed, found, MASKED))
            if prefixed:
                found = dot(prefix_k_ref[...], queries)
                scores.append(jnp.where(prefix_mask(prefix_rows), found, MASKED))
            tops = [jnp.max(score, axis=0, keepdims=True) for score in scores]
            if state:
                old_top = state[1][batch, block, 0:1, :]
                tops.append(old_top)
            top = tops[0]
            for other in tops[1:]:
                top = jnp.maximum(top, other)
            weights = [jnp.exp(score - top) for score in scores]
            mass = sum(jnp.sum(weight, axis=0, keepdims=True) for weight in weights)
            total = sum(dot(vt_buf[at + i], weights[i].astype(BF16)) for i in range(count))
            if prefixed:
                total = total + dot(prefix_vt_ref[...], weights[count].astype(BF16))
            if state:
                shrink = jnp.exp(old_top - top)
                mass = mass + state[1][batch, block, 1:2, :] * shrink
                total = total + state[0][batch, block] * shrink
            if finish:
                mass = 1.0 / mass
                total = total * mass
            return top, mass, total

        def query_block(block):
            def body(firsts, count):
                found = [attend_block(batch, block, firsts[batch], count) for batch in range(2)]
                for batch in range(2):
                    top, mass, total = found[batch]
                    if finish:
                        low = total.astype(BF16)
                        for j in range(2):
                            for copy in range(copies):
                                out_ref[(2 * block + j) * copies + copy, :, lanes(batch)] = low[:, half(j)]
                    stats_ref[batch, block, 0:1, :] = top
                    stats_ref[batch, block, 1:2, :] = mass
                    full_ref[batch, block] = total

            by_count(meta_ref, (0, 1), block, RANGES[ranges], COUNTS[ranges], body)

        each_block(4, query_block)

    for part, ranges in enumerate(passes):
        attend_pass(part, ranges)


def score_grads(keys, values, queries, grads, stats, delta, allowed):
    scores = jnp.where(allowed, dot(keys, queries), MASKED)
    weights = jnp.exp(scores - stats[0:1, :]) * stats[1:2, :]
    grad_score = weights * (dot(values, grads) - delta)
    return weights.astype(BF16), grad_score.astype(BF16)


def attend_back_kernel(
    kv_offsets, base, live, resume, copies, message, range_at, counts, extra, meta_ref, limits_ref, q_ref, *refs
):
    refs = refs[extra:]
    kv_count = len(kv_offsets)
    chunks = 4 * kv_count
    kv_refs = refs[:kv_count]
    refs = refs[kv_count:]
    if resume:
        old_ref = refs[0]
        refs = refs[1:]
    grad_ref, full_ref, stats_ref = refs[:3]
    refs = refs[3:]
    if message:
        returned_ref, parts_ref, dq_ref = refs[:3]
    else:
        dq_ref, dkv_refs = refs[0], refs[1 : 1 + kv_count]
    k_buf, kt_buf, v_buf, qt_buf, gt_buf, dk_sum, dv_sum = refs[-7:]

    for batch in range(2):
        for part in range(kv_count):
            start = kv_offsets[part]
            for j in range(8):
                chunk = chunks * batch + 4 * part + j // 2
                kv = kv_refs[part][j, start : start + 2 * HEAD, lanes(batch)]
                k_buf[chunk, half(j), :] = transposed(kv[:HEAD])
                kt_buf[chunk, :, half(j)] = kv[:HEAD]
                v_buf[chunk, half(j), :] = transposed(kv[HEAD:])
        for j in range(8):
            qt_buf[4 * batch + j // 2, :, half(j)] = q_ref[j, 0:HEAD, lanes(batch)]
            gt_buf[4 * batch + j // 2, :, half(j)] = grad_ref[j, :, lanes(batch)]
    dk_sum[...] = jnp.zeros_like(dk_sum)
    dv_sum[...] = jnp.zeros_like(dv_sum)

    def query_block(index):
        batch, block = index // 4, index % 4
        queries = qt_buf[4 * batch + block]
        grads = gt_buf[4 * batch + block]
        limits = limits_ref[batch, block]
        stats = stats_ref[batch, block]

        def body(firsts, count):
            first = firsts[0]
            dq = old_ref[batch, block] if resume else jnp.zeros((HEAD, CHUNK), F32)
            if count:
                queries_r = transposed(queries)
                grads_r = transposed(grads)
                delta = jnp.sum(grads.astype(F32) * full_ref[batch, block], axis=0, keepdims=True)
            for i in range(count):
                chunk = first + i
                at = chunks * batch + chunk - base
                allowed = allowed_keys(limits, chunk, meta_ref, batch, live)
                weights, grad_score = score_grads(
                    k_buf[at], v_buf[at], queries, grads, stats, delta, allowed
                )
                dk_sum[at] += dot(grad_score, queries_r)
                dv_sum[at] += dot(weights, grads_r)
                dq = dq + dot(kt_buf[at], grad_score)
            if copies:
                low = dq.astype(BF16) * 0.125
                for j in range(2):
                    for copy in range(copies):
                        dq_ref[(2 * block + j) * copies + copy, 0:HEAD, any_lanes(batch)] = low[:, half(j)]
            else:
                dq_ref[batch, block] = dq

        by_count(meta_ref, (batch,), block, range_at, counts, body)

    each_block(8, query_block)

    for batch in range(2):
        for part in range(kv_count):
            for j in range(8):
                chunk = chunks * batch + 4 * part + j // 2
                for i, total in enumerate((dk_sum, dv_sum)):
                    turned = total[chunk, half(j), :].T
                    rows = slice(i * HEAD, (i + 1) * HEAD)
                    if message:
                        turned = turned + returned_ref[j, rows, lanes(batch)].astype(F32)
                        rows = slice((i + 1) * HEAD, (i + 2) * HEAD)
                        dq_ref[j, rows, lanes(batch)] = turned.astype(BF16)
                    else:
                        dkv_refs[part][j, rows, lanes(batch)] = turned.astype(BF16)
    if message:
        total = parts_ref[0].astype(F32)
        for group in range(1, 8):
            total = total + parts_ref[group].astype(F32)
        small = total.astype(BF16)
        for j in range(8):
            dq_ref[j, 3 * HEAD : 3 * HEAD + 16, :] = small[:, 0:256]
            dq_ref[j, 3 * HEAD + 16 : 3 * HEAD + 32, :] = small[:, 256:512]


def prefix_back_kernel(
    prefix_rows, q_ref, k_ref, kt_ref, v_ref, grad_ref, full_ref, stats_ref, bias_ref, dq_ref, out_ref
):
    dk = jnp.zeros((PREFIX_ROWS, HEAD), F32)
    dv = jnp.zeros((PREFIX_ROWS, HEAD), F32)
    for batch in range(2):
        for block in range(4):
            queries = jnp.concatenate(
                [q_ref[2 * block + j, 0:HEAD, lanes(batch)] for j in range(2)], axis=1
            )
            grads = jnp.concatenate([grad_ref[2 * block + j, :, lanes(batch)] for j in range(2)], axis=1)
            delta = jnp.sum(grads.astype(F32) * full_ref[batch, block], axis=0, keepdims=True)
            weights, grad_score = score_grads(
                k_ref[...],
                v_ref[...],
                queries,
                grads,
                stats_ref[batch, block],
                delta,
                prefix_mask(prefix_rows),
            )
            dq_ref[batch, block] = dot(kt_ref[...], grad_score)
            dk = dk + dot(grad_score, transposed(queries))
            dv = dv + dot(weights, transposed(grads))
    pieces = [value[8 * j : 8 * j + 8] for value in (dk, dv) for j in range(4)]
    small = jnp.concatenate([jnp.concatenate(pieces, axis=1), bias_ref[...]], axis=0).astype(BF16)
    for group in range(8):
        out_ref[group] = small


def pinned(*values):
    return [pltpu.with_memory_space_constraint(value, pltpu.VMEM) for value in values]


def shape_of(shape, dtype):
    return jax.ShapeDtypeStruct(shape, dtype)


COST = pl.CostEstimate(flops=1000, bytes_accessed=1000, transcendentals=0)
VMEM_LIMIT = 63 * 10**6
PARAMS = pltpu.CompilerParams(vmem_limit_bytes=VMEM_LIMIT)
IN_VMEM = pl.BlockSpec(memory_space=pltpu.VMEM)
ANYWHERE = pl.BlockSpec(memory_space=pl.ANY)

RANGES = {"own": 0, "behind": 10, "cross": 20, "cross own": 30, "cross behind": 40, "cross ahead": 50}
BASES = {"own": 4, "behind": 0, "cross": 0, "cross own": 4, "cross behind": 0, "cross ahead": 8}
LIVE_AT = 60
COUNTS = {
    "own": (1, 2, 3, 4),
    "behind": (0, 1, 2, 3, 4),
    "cross": (1, 2, 3, 4, 5, 6, 8, 10, 12),
    "cross own": (1, 2, 3, 4),
    "cross behind": (0, 1, 2, 4),
    "cross ahead": (0, 1, 2, 4),
}


def attend(meta, limits, queries, kvs, kv_offsets, passes, prefix=None, prefix_rows=0, state=None, copies=2, extra=()):
    chunks = 4 * len(kvs)
    operands = pinned(*kvs) if len(kvs) == 1 else [*kvs]
    if prefix_rows:
        operands += [prefix[0], prefix[1].T]
    if state is not None:
        operands += pinned(*state)
    state_shape = shape_of if copies else pltpu.VMEM
    out_shape = [state_shape((2, 4, HEAD, CHUNK), F32), state_shape((2, 4, 8, CHUNK), F32)]
    if copies:
        out_shape.insert(0, shape_of((8 * copies, HEAD, 2 * BLOCK), BF16))
    kernel = partial(
        attend_kernel,
        kv_offsets,
        passes,
        not passes[0].startswith("cross"),
        prefix_rows,
        state is not None,
        copies,
        len(extra),
    )
    return pl.pallas_call(
        kernel,
        out_shape=tuple(out_shape),
        in_specs=[pl.BlockSpec(memory_space=pltpu.SMEM), IN_VMEM, IN_VMEM]
        + [ANYWHERE] * len(extra)
        + [IN_VMEM] * len(operands),
        out_specs=tuple(IN_VMEM for _ in out_shape),
        scratch_shapes=[
            pltpu.VMEM((2 * chunks, CHUNK, HEAD), BF16),
            pltpu.VMEM((2 * chunks, HEAD, CHUNK), BF16),
            pltpu.VMEM((8, HEAD, CHUNK), BF16),
        ],
        compiler_params=PARAMS,
        cost_estimate=COST,
    )(meta, limits, *pinned(queries), *extra, *operands)


def attend_back(
    meta, limits, queries, kvs, kv_offsets, base, ranges, grads, full, stats, old=None, copies=2, extra=(), message=()
):
    chunks = 4 * len(kvs)
    operands = [*kvs]
    if copies:
        out_shape = [shape_of((8 * copies, HEAD, 2 * BLOCK), BF16)]
    else:
        out_shape = [shape_of((2, 4, HEAD, CHUNK), F32)]
    for _ in kvs:
        out_shape.append(shape_of((8, 2 * HEAD, 2 * BLOCK), BF16))
    if old is not None:
        operands.append(old)
    operands += [*pinned(grads), full, stats, *message]
    if message:
        out_shape = [shape_of((8, 3 * HEAD + 32, 2 * BLOCK), BF16)]
    kernel = partial(
        attend_back_kernel,
        kv_offsets,
        base,
        ranges != "cross",
        old is not None,
        copies,
        len(message) > 0,
        RANGES[ranges],
        COUNTS[ranges],
        len(extra),
    )
    return pl.pallas_call(
        kernel,
        out_shape=tuple(out_shape),
        in_specs=[pl.BlockSpec(memory_space=pltpu.SMEM), IN_VMEM, IN_VMEM]
        + [ANYWHERE] * len(extra)
        + [IN_VMEM] * len(operands),
        out_specs=tuple(IN_VMEM for _ in out_shape),
        scratch_shapes=[
            pltpu.VMEM((2 * chunks, CHUNK, HEAD), BF16),
            pltpu.VMEM((2 * chunks, HEAD, CHUNK), BF16),
            pltpu.VMEM((2 * chunks, CHUNK, HEAD), BF16),
            pltpu.VMEM((8, HEAD, CHUNK), BF16),
            pltpu.VMEM((8, HEAD, CHUNK), BF16),
            pltpu.VMEM((2 * chunks, CHUNK, HEAD), F32),
            pltpu.VMEM((2 * chunks, CHUNK, HEAD), F32),
        ],
        compiler_params=PARAMS,
        cost_estimate=COST,
    )(meta, limits, queries, *extra, *operands)


def prefix_back(queries, prefix, prefix_rows, grads, full, stats, biases):
    return pl.pallas_call(
        partial(prefix_back_kernel, prefix_rows),
        out_shape=(shape_of((2, 4, HEAD, CHUNK), F32), shape_of((8, 16, 512), BF16)),
        in_specs=[IN_VMEM] * 8,
        out_specs=(IN_VMEM, IN_VMEM),
        compiler_params=PARAMS,
        cost_estimate=COST,
    )(queries, prefix[0], prefix[0].T, prefix[1], *pinned(grads), full, stats, biases)


def dot_t(left, right):
    return lax.dot_general(left, right, (((1,), (1,)), ((), ())), preferred_element_type=F32)


def tdot(left, right):
    return lax.dot_general(left, right, (((0,), (0,)), ((), ())), preferred_element_type=F32)


def small_call(kernel, out_shape, operands, extra=()):
    specs = [IN_VMEM] * len(operands)
    specs += [pl.BlockSpec(memory_space=pl.ANY)] * len(extra)
    count = len(operands)
    return pl.pallas_call(
        lambda *refs: kernel(*refs[:count], *refs[count + len(extra) :]),
        out_shape=tuple(out_shape),
        in_specs=specs,
        out_specs=tuple(pl.BlockSpec(memory_space=pltpu.VMEM) for _ in out_shape),
        compiler_params=pltpu.CompilerParams(vmem_limit_bytes=VMEM_LIMIT),
        cost_estimate=COST,
    )(*operands, *extra)


def store_heads(out_ref, turned):
    for h in range(8):
        out_ref[h] = turned[h * HEAD : (h + 1) * HEAD].astype(BF16)


def project_kernel(scaled, x_ref, w_ref, *refs):
    out_ref = refs[-1]
    y = dot(x_ref[...], w_ref[0])
    if scaled:
        y = y * jnp.where(pl.program_id(0) == 0, 0.125, 1.0)
    store_heads(out_ref, y.T)


def project(tokens, weights, scaled, extra=()):
    parts = weights.shape[0]
    return pl.pallas_call(
        partial(project_kernel, scaled),
        out_shape=shape_of((8, parts * HEAD, tokens.shape[0]), BF16),
        grid=(parts,),
        in_specs=[
            pl.BlockSpec(tokens.shape, lambda i: (0, 0)),
            pl.BlockSpec((1,) + weights.shape[1:], lambda i: (i, 0, 0)),
        ]
        + [pl.BlockSpec(memory_space=pl.ANY)] * len(extra),
        out_specs=pl.BlockSpec((8, HEAD, tokens.shape[0]), lambda i: (0, i, 0)),
        compiler_params=pltpu.CompilerParams(vmem_limit_bytes=VMEM_LIMIT),
        cost_estimate=COST,
    )(tokens, weights, *extra)


def unproject_kernel(grads_ref, w_ref, *refs):
    out_ref, total = refs[-2:]
    part = pl.program_id(0)
    turned = jnp.concatenate([grads_ref[h] for h in range(8)], axis=0)
    value = dot_t(transposed(turned), w_ref[0])

    @pl.when(part == 0)
    def _():
        total[...] = value

    @pl.when(part > 0)
    def _():
        total[...] += value

    @pl.when(part == pl.num_programs(0) - 1)
    def _():
        out_ref[...] = total[...].astype(BF16)


def unproject(grads, weights, extra=()):
    parts, width, tokens = weights.shape[0], weights.shape[1], grads.shape[2]
    return pl.pallas_call(
        unproject_kernel,
        out_shape=shape_of((tokens, width), BF16),
        grid=(parts,),
        in_specs=[
            pl.BlockSpec((8, HEAD, tokens), lambda i: (0, i, 0)),
            pl.BlockSpec((1,) + weights.shape[1:], lambda i: (i, 0, 0)),
        ]
        + [pl.BlockSpec(memory_space=pl.ANY)] * len(extra),
        out_specs=pl.BlockSpec((tokens, width), lambda i: (0, 0)),
        scratch_shapes=[pltpu.VMEM((tokens, width), F32)],
        compiler_params=pltpu.CompilerParams(vmem_limit_bytes=VMEM_LIMIT),
        cost_estimate=COST,
    )(grads, weights, *extra)


def whole_weight(place_ref, own_ref, direct_ref, shared_ref, axis):
    first_row, first_core = place_ref[0, 0:1, 0:1] == 0.0, place_ref[1, 0:1, 0:1] == 0.0
    direct, shared = direct_ref[...], shared_ref[...]
    first = jnp.where(first_core, direct, shared)
    last = jnp.where(first_core, shared, direct)
    other = jnp.concatenate([first, last], axis=axis)
    own = own_ref[...]
    return jnp.where(first_row, own, other), jnp.where(first_row, other, own)


def wide_rows(value_ref, row):
    return transposed(jnp.concatenate([value_ref[2 * h + row] for h in range(8)], axis=0))


def join_kernel(has_next, place_ref, context_ref, own_ref, direct_ref, shared_ref, base_ref, gain_ref, *refs):
    if has_next:
        next_ref, normed_ref, std_ref, out_ref = refs
        base = base_ref[...].astype(F32)
    else:
        base_gain_ref, normed_ref, std_ref, low_ref = refs
        base = base_ref[...] * base_gain_ref[...]
    first, last = whole_weight(place_ref, own_ref, direct_ref, shared_ref, 0)
    mixed = base + (dot(wide_rows(context_ref, 0), first) + dot(wide_rows(context_ref, 1), last))
    normed, inverse_std = norm_parts(mixed)
    normed_ref[...] = normed
    std_ref[...] = jnp.broadcast_to(inverse_std, std_ref.shape)
    low = (normed * gain_ref[...]).astype(BF16)
    if has_next:
        store_heads(out_ref, (0.125 * dot(low, next_ref[...])).T)
    else:
        low_ref[...] = low


def norm_parts(values):
    center = values - jnp.mean(values, axis=-1, keepdims=True)
    inverse_std = lax.rsqrt(jnp.mean(center * center, axis=-1, keepdims=True) + EPSILON)
    return center * inverse_std, inverse_std


def norm_back_kernel(*refs):
    sums, lows, others = refs[0:2], refs[2:4], refs[4:6]
    gain_ref, normed_ref, std_ref, weight_ref, grad_ref, out_ref = refs[6:]
    for stream in range(2):
        at = slice(stream * BLOCK, (stream + 1) * BLOCK)
        both = lows[stream][...].astype(F32) + others[stream][...].astype(F32)
        grad_ref[at, :] = norm_back(
            sums[stream][...] + both, gain_ref[...], normed_ref[at, :], std_ref[at, 0:1]
        )
    store_heads(out_ref, dot_t(weight_ref[...], grad_ref[...].astype(BF16)))


def adapter_grads_kernel(*refs):
    second, grad_adapter, branch, adapter = refs[0:2], refs[2:4], refs[4:6], refs[6:8]
    out_ref, bias_ref = refs[8:]

    def both(pair):
        return jnp.concatenate([pair[0][...], pair[1][...]], axis=0)

    grad_adapters, branches = both(grad_adapter), both(branch)
    down = dot(transposed(both(second)), grad_adapters)
    up = 4.0 * dot(transposed(branches), both(adapter))
    half_width = down.shape[1]
    for i in range(8):
        at = slice(i * 128, (i + 1) * 128)
        out_ref[i, :, 0:half_width] = down[at].astype(BF16)
        out_ref[i, :, half_width:] = up[at].astype(BF16)
    down_bias = jnp.sum(grad_adapters.astype(F32), axis=0, keepdims=True)
    up_bias = 4.0 * jnp.sum(branches.astype(F32), axis=0, keepdims=True)
    extra = jnp.concatenate([down_bias, up_bias, jnp.zeros((1, 256), F32)], axis=1)
    pieces = [extra[:, i * 512 : (i + 1) * 512] for i in range(3)]
    bias_ref[...] = jnp.concatenate(pieces + [jnp.zeros((5, 512), F32)], axis=0)


def finish_kernel(total_ref, small_ref, down_ref, up_ref, bias_ref, prefix_ref):
    half_width = down_ref.shape[1]
    for i in range(8):
        block = total_ref[i].astype(F32)
        at = slice(i * 128, (i + 1) * 128)
        down_ref[at, :] = block[:, 0:half_width]
        up_ref[:, at] = block[:, half_width:].T
    biases = [jnp.zeros((8, 256), F32)] * 2
    for i in range(2):
        for j in range(4):
            pieces = []
            for head in range(8):
                pieces.append(small_ref[head, 16 * i : 16 * i + 16, :].astype(F32)[0:8, 64 * j : 64 * j + 64])
            prefix_ref[i, 8 * j : 8 * j + 8, :] = jnp.concatenate(pieces, axis=1)
        for head in range(8):
            biases[i] = biases[i] + small_ref[head, 16 * i : 16 * i + 16, :].astype(F32)[8:16]
    bias_ref[...] = jnp.concatenate(biases, axis=1)


def join_back_kernel(
    place_ref,
    grad_q_ref,
    own_ref,
    direct_ref,
    shared_ref,
    base_ref,
    gain_ref,
    normed_ref,
    std_ref,
    weight_ref,
    grad_ref,
    out_ref,
):
    first, last = whole_weight(place_ref, own_ref, direct_ref, shared_ref, 1)
    gradient = base_ref[...] + (
        dot_t(wide_rows(grad_q_ref, 0), first) + dot_t(wide_rows(grad_q_ref, 1), last)
    )
    grad = norm_back(gradient, gain_ref[...], normed_ref[...], std_ref[:, 0:1])
    grad_ref[...] = grad
    store_heads(out_ref, dot_t(weight_ref[...], grad.astype(BF16)))


def positions(doc_lens, counts, group):
    docs = doc_lens.shape[1]
    upto = jnp.arange(docs)[:, None] <= jnp.arange(docs)[None, :]
    ends = jnp.sum(jnp.where(upto[None], doc_lens[:, :, None], 0), axis=1)
    slots = group * 1024 + jnp.arange(1024, dtype=jnp.int32)
    passed = ends[:, :, None] <= slots[None, None, :]
    origin = (group - 1) * 1024
    start = jnp.max(jnp.where(passed, ends[:, :, None], 0), axis=1) - origin
    stop = jnp.min(jnp.where(passed, 8192, ends[:, :, None]), axis=1) - origin
    own = jnp.broadcast_to(slots[None] - origin + 1, start.shape)

    def limits(low, high):
        both = jnp.stack([low, high], axis=1).reshape(2, 2, 4, CHUNK).transpose(0, 2, 1, 3)
        return jnp.pad(both, ((0, 0), (0, 0), (0, 6), (0, 0)))

    first = start[:, ::CHUNK] // CHUNK
    self_last = jnp.broadcast_to(jnp.arange(5, 9, dtype=jnp.int32)[None], first.shape)
    cross_last = (stop[:, CHUNK - 1 :: CHUNK] + (CHUNK - 1)) // CHUNK

    def columns(last, low, high):
        ends = jnp.broadcast_to(jnp.array([[low, high]], jnp.int32), (2, 2))
        return [jnp.clip(first, low, high), jnp.clip(last, low, high), ends]

    blocks = jnp.arange(16, dtype=jnp.int32) + (group - 1) * 8
    at = blocks[:, None] == jnp.arange(64, dtype=jnp.int32)[None]
    window_counts = jnp.sum(jnp.where(at[None], counts[:, None, :], 0), axis=2)
    meta = columns(self_last, 4, 8) + columns(self_last, 0, 4) + columns(cross_last, 0, 12)
    meta += columns(cross_last, 4, 8) + columns(cross_last, 0, 4) + columns(cross_last, 8, 12)
    meta += [window_counts]
    return (jnp.concatenate(meta, axis=1), limits(start, own), limits(start, stop))


def hold(value, *earlier):
    any_space = pl.BlockSpec(memory_space=pl.ANY)
    return pl.pallas_call(
        lambda *refs: None,
        out_shape=shape_of(value.shape, value.dtype),
        in_specs=[any_space] * (1 + len(earlier)),
        out_specs=any_space,
        input_output_aliases={0: 0},
        cost_estimate=COST,
    )(value, *earlier)


def on_device(
    inputs,
    memory,
    cotangent,
    doc_lens,
    counts,
    prefix_kv,
    self_qkv,
    self_out,
    cross_q,
    cross_kv,
    cross_out,
    norm_gains,
    fc_in,
    fc_out,
    down_w,
    down_b,
    up_w,
    up_b,
):
    width = inputs.shape[2]
    rows = 2 * BLOCK
    prefix_rows = prefix_kv.shape[1]
    core, row = lax.axis_index("core"), lax.axis_index("row")
    group = lax.axis_index("y") * 2 + lax.axis_index("x_hi")
    head = lax.axis_index("z") * 2 + core
    place = jnp.broadcast_to(jnp.stack([row, core]).astype(F32)[:, None, None], (2, 1, BLOCK))
    meta, self_limits, cross_limits = positions(doc_lens, counts, group)
    prefix = lax.dynamic_slice_in_dim(prefix_kv, head * HEAD, HEAD, 2)
    prefix = jnp.pad(prefix, ((0, 0), (0, PREFIX_ROWS - prefix_rows), (0, 0)))
    gains = [norm_gains[i : i + 1] for i in range(3)]
    tokens = inputs.reshape(rows, width)
    qkv_w = jnp.transpose(self_qkv, (1, 0, 2))
    kv_w = jnp.transpose(cross_kv, (1, 0, 2))

    def share(direct, *earlier):
        held = hold(direct, *earlier)
        return held, flip(held, "core", 1)

    def fetch(weight, axis, *earlier):
        size = weight.shape[axis] // 2
        mine = lax.dynamic_slice_in_dim(weight, core * size, size, axis)
        return flip(hold(mine, *earlier) if earlier else mine, "row", 1)

    projected = project(tokens, qkv_w, True)
    own = regroup(projected)
    self_out_direct = fetch(self_out, 0)
    own_kv = own[:, HEAD:, :]
    behind = shift_groups(own_kv, 1)
    mem_projected = project(memory.reshape(rows, width), kv_w, False, (projected,))
    mem_own = regroup(hold(mem_projected, own_kv))
    mem_behind = shift_groups(mem_own, 1)
    mem_ahead = shift_groups(mem_own, -1)
    self_out_halves = share(self_out_direct, mem_own)

    self_full, self_stats = attend(
        meta,
        self_limits,
        own,
        (own,),
        (HEAD,),
        ("own",),
        prefix,
        prefix_rows,
        copies=0,
    )
    context, self_full, self_stats = attend(
        meta, self_limits, own, (behind,), (0,), ("behind",), state=(self_full, self_stats), extra=(mem_own,)
    )
    context = regroup_wide(context)
    cross_out_direct = fetch(cross_out, 0, context)
    first_normed, first_std, queries = small_call(
        partial(join_kernel, True),
        (
            shape_of((rows, width), F32),
            shape_of((rows, BLOCK), F32),
            shape_of((8, HEAD, rows), BF16),
        ),
        (place, context, self_out, *self_out_halves, tokens, gains[0], cross_q),
    )
    queries = regroup(queries)
    cross_args = (meta, cross_limits, queries, (mem_behind, mem_own, mem_ahead), (0, 0, 0), 0, "cross")
    cross_full, cross_stats = attend(
        meta,
        cross_limits,
        queries,
        (mem_own,),
        (0,),
        ("cross own",),
        copies=0,
    )
    context, cross_full, cross_stats = attend(
        meta,
        cross_limits,
        queries,
        (mem_behind, mem_ahead),
        (0, 0),
        ("cross behind", "cross ahead"),
        state=(cross_full, cross_stats),
    )
    cross_out_halves = share(cross_out_direct, cross_full)
    context = regroup_wide(context)
    second_normed, second_std, second_all = small_call(
        partial(join_kernel, False),
        (shape_of((rows, width), F32), shape_of((rows, BLOCK), F32), shape_of((rows, width), BF16)),
        (place, context, cross_out, *cross_out_halves, first_normed, gains[1], gains[0]),
    )

    streams = range(2)
    outputs, grad_sums, kept, branches = [], [], [], []
    for stream in streams:
        second_norm = second_normed[stream * BLOCK : (stream + 1) * BLOCK] * norm_gains[1]
        second_low = second_all[stream * BLOCK : (stream + 1) * BLOCK]
        hidden_act, hidden_slope = gelu_both(dot(second_low, fc_in))
        adapter_act, adapter_slope = gelu_both(dot(second_low, down_w) + down_b)
        hidden_low = hidden_act.astype(BF16)
        adapter_low = adapter_act.astype(BF16)
        kept.append((second_low, hidden_slope, adapter_low, adapter_slope, second_norm))
        low = (dot(hidden_low, fc_out) + 4.0 * dot(adapter_low, up_w)).astype(BF16)
        branches.append((low, flip(low, "row", 1)))

    grad_adapters, grad_branches, lows, others = [], [], [], []
    for stream in streams:
        second_low, hidden_slope, adapter_low, adapter_slope, second_norm = kept[stream]
        low, other = branches[stream]
        other = hold(other, lows[-1] if stream else branches[1][0])
        branch = (low.astype(F32) + other.astype(F32)) + 4.0 * up_b
        result, normed, inverse_std = norm_rows(second_norm + branch, norm_gains[2])
        outputs.append(result.astype(BF16))
        grad_sums.append(
            norm_back(cotangent[stream].astype(F32), norm_gains[2], normed, inverse_std)
        )
        grad_branch = grad_sums[stream].astype(BF16)
        grad_hidden = (dot_t(grad_branch, fc_out) * hidden_slope).astype(BF16)
        grad_adapter = (4.0 * dot_t(grad_branch, up_w) * adapter_slope).astype(BF16)
        grad_hidden, grad_adapter = lax.optimization_barrier((grad_hidden, grad_adapter))
        low = (dot_t(grad_hidden, fc_in) + dot_t(grad_adapter, down_w)).astype(BF16)
        lows.append(low)
        others.append(flip(low, "row", 1))
        grad_adapters.append(grad_adapter)
        grad_branches.append(grad_branch)

    adapters = down_w.shape[1]
    message, bias_sums = small_call(
        adapter_grads_kernel,
        (shape_of((8, 128, 512), BF16), shape_of((8, 512), F32)),
        (kept[0][0], kept[1][0], *grad_adapters, *grad_branches, kept[0][2], kept[1][2]),
        extra=(others[0], lows[1]),
    )
    adapter_part = lax.psum_scatter(message, GROUP, scatter_dimension=0, tiled=True)

    grad_crossed, grad_context = small_call(
        norm_back_kernel,
        (shape_of((rows, width), F32), shape_of((8, HEAD, rows), BF16)),
        (
            *grad_sums,
            *lows,
            *others,
            gains[1],
            second_normed,
            second_std,
            cross_out,
        ),
        extra=(message,),
    )
    grad_context = regroup(grad_context)

    cross_q_direct = fetch(cross_q, 1, grad_crossed)
    grad_q, grad_behind, grad_own, grad_ahead = attend_back(
        *cross_args, grad_context, cross_full, cross_stats, extra=(cross_q_direct,)
    )
    cross_q_halves = share(cross_q_direct, grad_own)
    grad_q = regroup_wide(grad_q)
    adapter_parts = lax.all_gather(
        hold(adapter_part, grad_own), ("y", "x_hi"), axis=0, tiled=True
    )
    mem_parts = (
        grad_own,
        shift_groups(hold(grad_behind, grad_q), -1),
        shift_groups(hold(grad_ahead, grad_q), 1),
    )
    grad_mixed, grad_context = small_call(
        join_back_kernel,
        (shape_of((rows, width), F32), shape_of((8, HEAD, rows), BF16)),
        (
            place,
            grad_q,
            cross_q,
            *cross_q_halves,
            grad_crossed,
            gains[0],
            first_normed,
            first_std,
            self_out,
        ),
    )
    grad_context = regroup(grad_context)

    grad_mem = sum(part.astype(F32) for part in mem_parts).astype(BF16)
    grad_q, packed = prefix_back(
        own, prefix, prefix_rows, grad_context, self_full, self_stats, bias_sums
    )
    parts = lax.all_to_all(packed, ("y", "x_hi"), 0, 0)
    grad_q, grad_behind = attend_back(
        meta,
        self_limits,
        own,
        (behind,),
        (0,),
        0,
        "behind",
        grad_context,
        self_full,
        self_stats,
        old=grad_q,
        copies=0,
    )
    adapter_part = jnp.sum(hold(adapter_parts, grad_behind).astype(F32), axis=0, keepdims=True)
    adapter_total = lax.all_gather(adapter_part.astype(BF16), GROUP, axis=0, tiled=True)
    returned = shift_groups(hold(grad_behind, parts), -1)
    grad_mem = hold(grad_mem, grad_behind)
    mem_recv = regroup(grad_mem)
    (message,) = attend_back(
        meta,
        self_limits,
        own,
        (own,),
        (HEAD,),
        4,
        "own",
        grad_context,
        self_full,
        self_stats,
        old=grad_q,
        copies=1,
        extra=(grad_mem,),
        message=(returned, parts),
    )
    message = hold(message, mem_recv)
    grads = regroup(message)
    mem_low = unproject(mem_recv, kv_w, (message,))
    mem_other = flip(mem_low, "row", 1)
    low = unproject(grads, qkv_w)
    other = flip(low, "row", 1)
    grad_memory = (mem_low.astype(F32) + mem_other.astype(F32)).astype(BF16)

    down_grad, up_grad, bias_grads, prefix_grad = small_call(
        finish_kernel,
        (
            shape_of((width, adapters), F32),
            shape_of((adapters, width), F32),
            shape_of((8, 512), F32),
            shape_of((2, 32, prefix_kv.shape[2]), F32),
        ),
        (adapter_total, grads[:, 3 * HEAD :]),
        extra=(low,),
    )
    bias_grads = bias_grads.reshape(-1)
    other = hold(other, down_grad)
    input_grad = (grad_mixed + (low.astype(F32) + other.astype(F32))).astype(BF16)
    return (
        jnp.stack(outputs),
        input_grad.reshape(inputs.shape),
        grad_memory.reshape(memory.shape),
        prefix_grad[:, :prefix_rows],
        down_grad,
        bias_grads[:adapters],
        up_grad,
        bias_grads[adapters : adapters + width],
    )


def solution(mesh):
    fine = Mesh(mesh.devices.reshape(4, 2, 4, 2, 2), SEQ + ("row",))
    in_specs = (
        P(None, SEQ, None),
        P(None, SEQ, None),
        P(None, SEQ, None),
        P(),
        P(),
        P(None, None, "row"),
        P(None, None, "row"),
        P("row", None),
        P(None, "row"),
        P(None, None, "row"),
        P("row", None),
        P(),
        P(None, "row"),
        P("row", None),
        P(None, "row"),
        P("row"),
        P("row", None),
        P(),
    )
    out_specs = (
        P(None, SEQ, None),
        P(None, SEQ, None),
        P(None, SEQ, None),
        P(None, None, "row"),
        P(None, "row"),
        P("row"),
        P("row", None),
        P(),
    )
    return jax.shard_map(
        on_device, mesh=fine, in_specs=in_specs, out_specs=out_specs, check_vma=False
    )
```

```python
from functools import partial

import jax
import jax.numpy as jnp
from jax import lax
from jax.experimental import pallas as pl
from jax.experimental.pallas import tpu as pltpu
from jax.sharding import Mesh
from jax.sharding import PartitionSpec as P

HEAD = 64
EPSILON = 1e-05
MASKED = -1000000000.0
CHUNK = 256
PREFIX_ROWS = 32
BLOCK = 128
SEQ = ("y", "x_hi", "z", "core")
GROUP = ("z", "core")
WIDE_GROUP = ("z", "core", "row")
BF16 = jnp.bfloat16
F32 = jnp.float32


def dot(left, right):
    return jnp.dot(left, right, preferred_element_type=F32)


def norm_rows(values, norm_gain):
    center = values - jnp.mean(values, axis=-1, keepdims=True)
    inverse_std = lax.rsqrt(jnp.mean(center * center, axis=-1, keepdims=True) + EPSILON)
    normed = center * inverse_std
    return (normed * norm_gain, normed, inverse_std)


def norm_back(gradient, norm_gain, normed, inverse_std):
    scaled = gradient * norm_gain
    centered = scaled - jnp.mean(scaled, axis=-1, keepdims=True)
    return (centered - normed * jnp.mean(scaled * normed, axis=-1, keepdims=True)) * inverse_std


def gelu_both(pre_act):
    cdf = 0.5 * (1.0 + lax.erf(pre_act * 0.7071067811865476))
    slope = cdf + pre_act * (0.3989422804014327 * jnp.exp(-0.5 * pre_act * pre_act))
    return (pre_act * cdf, slope)


def row_total(partial_sum):
    low = partial_sum.astype(BF16)
    other = lax.ppermute(low, "row", [(0, 1), (1, 0)])
    return low.astype(F32) + other.astype(F32)


def shift_groups(value, by):
    devices = 64
    pairs = [(i, i + 8 * by) for i in range(devices) if 0 <= i + 8 * by < devices]
    return lax.ppermute(value, SEQ, pairs)


def regroup(value):
    return lax.all_to_all(value, GROUP, 0, 0)


def regroup_wide(value):
    return lax.all_to_all(value, WIDE_GROUP, 0, 0)


def flip(value, axis_name, bit):
    size = lax.axis_size(axis_name)
    return lax.ppermute(value, axis_name, [(i, i ^ bit) for i in range(size)])


def transposed(value):
    return value.astype(F32).T.astype(BF16)


def allowed_keys(limits, chunk, meta_ref, batch, live):
    keys = lax.broadcasted_iota(jnp.int32, (CHUNK, CHUNK), 0)
    low = limits[0:1, :] - chunk * CHUNK
    high = limits[1:2, :] - chunk * CHUNK
    allowed = (keys >= low) & (keys < high)
    if live:
        first = meta_ref[batch, LIVE_AT + 2 * chunk]
        second = meta_ref[batch, LIVE_AT + 1 + 2 * chunk] + BLOCK
        allowed = allowed & (keys < jnp.where(keys < BLOCK, first, second))
    return allowed


def prefix_mask(prefix_rows):
    return lax.broadcasted_iota(jnp.int32, (PREFIX_ROWS, CHUNK), 0) < prefix_rows


def half(j):
    return slice((j % 2) * BLOCK, (j % 2 + 1) * BLOCK)


def by_count(meta_ref, batches, block, range_at, counts, body):
    firsts = [meta_ref[batch, range_at + block] for batch in batches]
    needs = [meta_ref[batch, range_at + 4 + block] - first for batch, first in zip(batches, firsts)]
    base, end = meta_ref[0, range_at + 8], meta_ref[0, range_at + 9]
    needed = needs[0]
    for need in needs[1:]:
        needed = jnp.maximum(needed, need)
    smaller = -1
    for count in counts:
        fits = needed <= count
        if count == counts[-1]:
            fits = needed > smaller
        elif smaller >= 0:
            fits = fits & (needed > smaller)

        @pl.when(fits)
        def _(count=count):
            body([jnp.maximum(jnp.minimum(first, end - count), base) for first in firsts], count)

        smaller = count


def lanes(batch):
    return slice(batch * BLOCK, (batch + 1) * BLOCK)


def any_lanes(batch):
    return pl.ds(pl.multiple_of(batch * BLOCK, BLOCK), BLOCK)


def each_block(count, body):
    def step(index, carry):
        body(index)
        return carry

    lax.fori_loop(0, count, step, 0)


def attend_kernel(kv_offsets, passes, live, prefix_rows, resume, copies, extra, meta_ref, limits_ref, q_ref, *refs):
    refs = refs[extra:]
    kv_count = len(kv_offsets)
    chunks = 4 * kv_count
    kv_refs = refs[:kv_count]
    refs = refs[kv_count:]
    if prefix_rows:
        prefix_k_ref, prefix_vt_ref = refs[:2]
        refs = refs[2:]
    if resume:
        total_ref, old_ref = refs[:2]
        refs = refs[2:]
    if copies:
        out_ref = refs[0]
        refs = refs[1:]
    full_ref, stats_ref, k_buf, vt_buf, qt_buf = refs

    for batch in range(2):
        for part in range(kv_count):
            start = kv_offsets[part]
            for j in range(8):
                chunk = chunks * batch + 4 * part + j // 2
                kv = kv_refs[part][j, start : start + 2 * HEAD, lanes(batch)]
                k_buf[chunk, half(j), :] = transposed(kv[:HEAD])
                vt_buf[chunk, :, half(j)] = kv[HEAD:]
        for j in range(8):
            qt_buf[4 * batch + j // 2, :, half(j)] = q_ref[j, 0:HEAD, lanes(batch)]

    def attend_pass(part, ranges):
        base = BASES[ranges]
        prefixed = prefix_rows > 0 and part == 0
        state = (full_ref, stats_ref) if part else (total_ref, old_ref) if resume else None
        finish = copies > 0 and part == kv_count - 1

        def attend_block(batch, block, first, count):
            queries = qt_buf[4 * batch + block]
            limits = limits_ref[batch, block]
            at = chunks * batch + 4 * part + first - base
            scores = []
            for i in range(count):
                found = dot(k_buf[at + i], queries)
                allowed = allowed_keys(limits, first + i, meta_ref, batch, live)
                scores.append(jnp.where(allowed, found, MASKED))
            if prefixed:
                found = dot(prefix_k_ref[...], queries)
                scores.append(jnp.where(prefix_mask(prefix_rows), found, MASKED))
            tops = [jnp.max(score, axis=0, keepdims=True) for score in scores]
            if state:
                old_top = state[1][batch, block, 0:1, :]
                tops.append(old_top)
            top = tops[0]
            for other in tops[1:]:
                top = jnp.maximum(top, other)
            weights = [jnp.exp(score - top) for score in scores]
            mass = sum(jnp.sum(weight, axis=0, keepdims=True) for weight in weights)
            total = sum(dot(vt_buf[at + i], weights[i].astype(BF16)) for i in range(count))
            if prefixed:
                total = total + dot(prefix_vt_ref[...], weights[count].astype(BF16))
            if state:
                shrink = jnp.exp(old_top - top)
                mass = mass + state[1][batch, block, 1:2, :] * shrink
                total = total + state[0][batch, block] * shrink
            if finish:
                mass = 1.0 / mass
                total = total * mass
            return top, mass, total

        def query_block(block):
            def body(firsts, count):
                found = [attend_block(batch, block, firsts[batch], count) for batch in range(2)]
                for batch in range(2):
                    top, mass, total = found[batch]
                    if finish:
                        low = total.astype(BF16)
                        for j in range(2):
                            for copy in range(copies):
                                out_ref[(2 * block + j) * copies + copy, :, lanes(batch)] = low[:, half(j)]
                    stats_ref[batch, block, 0:1, :] = top
                    stats_ref[batch, block, 1:2, :] = mass
                    full_ref[batch, block] = total

            by_count(meta_ref, (0, 1), block, RANGES[ranges], COUNTS[ranges], body)

        each_block(4, query_block)

    for part, ranges in enumerate(passes):
        attend_pass(part, ranges)


def score_grads(keys, values, queries, grads, stats, delta, allowed):
    scores = jnp.where(allowed, dot(keys, queries), MASKED)
    weights = jnp.exp(scores - stats[0:1, :]) * stats[1:2, :]
    grad_score = weights * (dot(values, grads) - delta)
    return weights.astype(BF16), grad_score.astype(BF16)


def attend_back_kernel(
    kv_offsets, base, live, resume, copies, message, range_at, counts, extra, meta_ref, limits_ref, q_ref, *refs
):
    refs = refs[extra:]
    kv_count = len(kv_offsets)
    chunks = 4 * kv_count
    kv_refs = refs[:kv_count]
    refs = refs[kv_count:]
    if resume:
        old_ref = refs[0]
        refs = refs[1:]
    grad_ref, full_ref, stats_ref = refs[:3]
    refs = refs[3:]
    if message:
        returned_ref, parts_ref, dq_ref = refs[:3]
    else:
        dq_ref, dkv_refs = refs[0], refs[1 : 1 + kv_count]
    k_buf, kt_buf, v_buf, qt_buf, gt_buf, dk_sum, dv_sum = refs[-7:]

    for batch in range(2):
        for part in range(kv_count):
            start = kv_offsets[part]
            for j in range(8):
                chunk = chunks * batch + 4 * part + j // 2
                kv = kv_refs[part][j, start : start + 2 * HEAD, lanes(batch)]
                k_buf[chunk, half(j), :] = transposed(kv[:HEAD])
                kt_buf[chunk, :, half(j)] = kv[:HEAD]
                v_buf[chunk, half(j), :] = transposed(kv[HEAD:])
        for j in range(8):
            qt_buf[4 * batch + j // 2, :, half(j)] = q_ref[j, 0:HEAD, lanes(batch)]
            gt_buf[4 * batch + j // 2, :, half(j)] = grad_ref[j, :, lanes(batch)]
    dk_sum[...] = jnp.zeros_like(dk_sum)
    dv_sum[...] = jnp.zeros_like(dv_sum)

    def query_block(index):
        batch, block = index // 4, index % 4
        queries = qt_buf[4 * batch + block]
        grads = gt_buf[4 * batch + block]
        limits = limits_ref[batch, block]
        stats = stats_ref[batch, block]

        def body(firsts, count):
            first = firsts[0]
            dq = old_ref[batch, block] if resume else jnp.zeros((HEAD, CHUNK), F32)
            if count:
                queries_r = transposed(queries)
                grads_r = transposed(grads)
                delta = jnp.sum(grads.astype(F32) * full_ref[batch, block], axis=0, keepdims=True)
            for i in range(count):
                chunk = first + i
                at = chunks * batch + chunk - base
                allowed = allowed_keys(limits, chunk, meta_ref, batch, live)
                weights, grad_score = score_grads(
                    k_buf[at], v_buf[at], queries, grads, stats, delta, allowed
                )
                dk_sum[at] += dot(grad_score, queries_r)
                dv_sum[at] += dot(weights, grads_r)
                dq = dq + dot(kt_buf[at], grad_score)
            if copies:
                low = dq.astype(BF16) * 0.125
                for j in range(2):
                    for copy in range(copies):
                        dq_ref[(2 * block + j) * copies + copy, 0:HEAD, any_lanes(batch)] = low[:, half(j)]
            else:
                dq_ref[batch, block] = dq

        by_count(meta_ref, (batch,), block, range_at, counts, body)

    each_block(8, query_block)

    for batch in range(2):
        for part in range(kv_count):
            for j in range(8):
                chunk = chunks * batch + 4 * part + j // 2
                for i, total in enumerate((dk_sum, dv_sum)):
                    turned = total[chunk, half(j), :].T
                    rows = slice(i * HEAD, (i + 1) * HEAD)
                    if message:
                        turned = turned + returned_ref[j, rows, lanes(batch)].astype(F32)
                        rows = slice((i + 1) * HEAD, (i + 2) * HEAD)
                        dq_ref[j, rows, lanes(batch)] = turned.astype(BF16)
                    else:
                        dkv_refs[part][j, rows, lanes(batch)] = turned.astype(BF16)
    if message:
        total = parts_ref[0].astype(F32)
        for group in range(1, 8):
            total = total + parts_ref[group].astype(F32)
        small = total.astype(BF16)
        for j in range(8):
            dq_ref[j, 3 * HEAD : 3 * HEAD + 16, :] = small[:, 0:256]
            dq_ref[j, 3 * HEAD + 16 : 3 * HEAD + 32, :] = small[:, 256:512]


def prefix_back_kernel(
    prefix_rows, q_ref, k_ref, kt_ref, v_ref, grad_ref, full_ref, stats_ref, bias_ref, dq_ref, out_ref
):
    dk = jnp.zeros((PREFIX_ROWS, HEAD), F32)
    dv = jnp.zeros((PREFIX_ROWS, HEAD), F32)
    for batch in range(2):
        for block in range(4):
            queries = jnp.concatenate(
                [q_ref[2 * block + j, 0:HEAD, lanes(batch)] for j in range(2)], axis=1
            )
            grads = jnp.concatenate([grad_ref[2 * block + j, :, lanes(batch)] for j in range(2)], axis=1)
            delta = jnp.sum(grads.astype(F32) * full_ref[batch, block], axis=0, keepdims=True)
            weights, grad_score = score_grads(
                k_ref[...],
                v_ref[...],
                queries,
                grads,
                stats_ref[batch, block],
                delta,
                prefix_mask(prefix_rows),
            )
            dq_ref[batch, block] = dot(kt_ref[...], grad_score)
            dk = dk + dot(grad_score, transposed(queries))
            dv = dv + dot(weights, transposed(grads))
    pieces = [value[8 * j : 8 * j + 8] for value in (dk, dv) for j in range(4)]
    small = jnp.concatenate([jnp.concatenate(pieces, axis=1), bias_ref[...]], axis=0).astype(BF16)
    for group in range(8):
        out_ref[group] = small


def pinned(*values):
    return [pltpu.with_memory_space_constraint(value, pltpu.VMEM) for value in values]


def shape_of(shape, dtype):
    return jax.ShapeDtypeStruct(shape, dtype)


COST = pl.CostEstimate(flops=1000, bytes_accessed=1000, transcendentals=0)
VMEM_LIMIT = 63 * 10**6
PARAMS = pltpu.CompilerParams(vmem_limit_bytes=VMEM_LIMIT)
IN_VMEM = pl.BlockSpec(memory_space=pltpu.VMEM)
ANYWHERE = pl.BlockSpec(memory_space=pl.ANY)

RANGES = {"own": 0, "behind": 10, "cross": 20, "cross own": 30, "cross behind": 40, "cross ahead": 50}
BASES = {"own": 4, "behind": 0, "cross": 0, "cross own": 4, "cross behind": 0, "cross ahead": 8}
LIVE_AT = 60
COUNTS = {
    "own": (1, 2, 3, 4),
    "behind": (0, 1, 2, 3, 4),
    "cross": (1, 2, 3, 4, 5, 6, 8, 10, 12),
    "cross own": (1, 2, 3, 4),
    "cross behind": (0, 1, 2, 4),
    "cross ahead": (0, 1, 2, 4),
}


def attend(meta, limits, queries, kvs, kv_offsets, passes, prefix=None, prefix_rows=0, state=None, copies=2, extra=()):
    chunks = 4 * len(kvs)
    operands = pinned(*kvs) if len(kvs) == 1 else [*kvs]
    if prefix_rows:
        operands += [prefix[0], prefix[1].T]
    if state is not None:
        operands += pinned(*state)
    state_shape = shape_of if copies else pltpu.VMEM
    out_shape = [state_shape((2, 4, HEAD, CHUNK), F32), state_shape((2, 4, 8, CHUNK), F32)]
    if copies:
        out_shape.insert(0, shape_of((8 * copies, HEAD, 2 * BLOCK), BF16))
    kernel = partial(
        attend_kernel,
        kv_offsets,
        passes,
        not passes[0].startswith("cross"),
        prefix_rows,
        state is not None,
        copies,
        len(extra),
    )
    return pl.pallas_call(
        kernel,
        out_shape=tuple(out_shape),
        in_specs=[pl.BlockSpec(memory_space=pltpu.SMEM), IN_VMEM, IN_VMEM]
        + [ANYWHERE] * len(extra)
        + [IN_VMEM] * len(operands),
        out_specs=tuple(IN_VMEM for _ in out_shape),
        scratch_shapes=[
            pltpu.VMEM((2 * chunks, CHUNK, HEAD), BF16),
            pltpu.VMEM((2 * chunks, HEAD, CHUNK), BF16),
            pltpu.VMEM((8, HEAD, CHUNK), BF16),
        ],
        compiler_params=PARAMS,
        cost_estimate=COST,
    )(meta, limits, *pinned(queries), *extra, *operands)


def attend_back(
    meta, limits, queries, kvs, kv_offsets, base, ranges, grads, full, stats, old=None, copies=2, extra=(), message=()
):
    chunks = 4 * len(kvs)
    operands = [*kvs]
    if copies:
        out_shape = [shape_of((8 * copies, HEAD, 2 * BLOCK), BF16)]
    else:
        out_shape = [shape_of((2, 4, HEAD, CHUNK), F32)]
    for _ in kvs:
        out_shape.append(shape_of((8, 2 * HEAD, 2 * BLOCK), BF16))
    if old is not None:
        operands.append(old)
    operands += [*pinned(grads), full, stats, *message]
    if message:
        out_shape = [shape_of((8, 3 * HEAD + 32, 2 * BLOCK), BF16)]
    kernel = partial(
        attend_back_kernel,
        kv_offsets,
        base,
        ranges != "cross",
        old is not None,
        copies,
        len(message) > 0,
        RANGES[ranges],
        COUNTS[ranges],
        len(extra),
    )
    return pl.pallas_call(
        kernel,
        out_shape=tuple(out_shape),
        in_specs=[pl.BlockSpec(memory_space=pltpu.SMEM), IN_VMEM, IN_VMEM]
        + [ANYWHERE] * len(extra)
        + [IN_VMEM] * len(operands),
        out_specs=tuple(IN_VMEM for _ in out_shape),
        scratch_shapes=[
            pltpu.VMEM((2 * chunks, CHUNK, HEAD), BF16),
            pltpu.VMEM((2 * chunks, HEAD, CHUNK), BF16),
            pltpu.VMEM((2 * chunks, CHUNK, HEAD), BF16),
            pltpu.VMEM((8, HEAD, CHUNK), BF16),
            pltpu.VMEM((8, HEAD, CHUNK), BF16),
            pltpu.VMEM((2 * chunks, CHUNK, HEAD), F32),
            pltpu.VMEM((2 * chunks, CHUNK, HEAD), F32),
        ],
        compiler_params=PARAMS,
        cost_estimate=COST,
    )(meta, limits, queries, *extra, *operands)


def prefix_back(queries, prefix, prefix_rows, grads, full, stats, biases):
    return pl.pallas_call(
        partial(prefix_back_kernel, prefix_rows),
        out_shape=(shape_of((2, 4, HEAD, CHUNK), F32), shape_of((8, 16, 512), BF16)),
        in_specs=[IN_VMEM] * 8,
        out_specs=(IN_VMEM, IN_VMEM),
        compiler_params=PARAMS,
        cost_estimate=COST,
    )(queries, prefix[0], prefix[0].T, prefix[1], *pinned(grads), full, stats, biases)


def dot_t(left, right):
    return lax.dot_general(left, right, (((1,), (1,)), ((), ())), preferred_element_type=F32)


def tdot(left, right):
    return lax.dot_general(left, right, (((0,), (0,)), ((), ())), preferred_element_type=F32)


def small_call(kernel, out_shape, operands, extra=()):
    specs = [IN_VMEM] * len(operands)
    specs += [pl.BlockSpec(memory_space=pl.ANY)] * len(extra)
    count = len(operands)
    return pl.pallas_call(
        lambda *refs: kernel(*refs[:count], *refs[count + len(extra) :]),
        out_shape=tuple(out_shape),
        in_specs=specs,
        out_specs=tuple(pl.BlockSpec(memory_space=pltpu.VMEM) for _ in out_shape),
        compiler_params=pltpu.CompilerParams(vmem_limit_bytes=VMEM_LIMIT),
        cost_estimate=COST,
    )(*operands, *extra)


def store_heads(out_ref, turned):
    for h in range(8):
        out_ref[h] = turned[h * HEAD : (h + 1) * HEAD].astype(BF16)


def project_kernel(scaled, x_ref, w_ref, out_ref):
    tokens = x_ref[...]
    for part in range(w_ref.shape[0]):
        y = dot(tokens, w_ref[part])
        if scaled and part == 0:
            y = y * 0.125
        turned = y.T.astype(BF16)
        for h in range(8):
            out_ref[h, part * HEAD : (part + 1) * HEAD, :] = turned[h * HEAD : (h + 1) * HEAD]


def project(tokens, weights, scaled, extra=()):
    shape = (8, weights.shape[0] * HEAD, tokens.shape[0])
    (heads,) = small_call(
        partial(project_kernel, scaled), (shape_of(shape, BF16),), (tokens, weights), extra
    )
    return heads


def unproject_kernel(grads_ref, w_ref, out_ref):
    total = None
    for part in range(w_ref.shape[0]):
        rows = slice(part * HEAD, (part + 1) * HEAD)
        turned = jnp.concatenate([grads_ref[h, rows, :] for h in range(8)], axis=0)
        value = dot_t(transposed(turned), w_ref[part])
        total = value if total is None else total + value
    out_ref[...] = total.astype(BF16)


def unproject(grads, weights, extra=()):
    shape = (grads.shape[2], weights.shape[1])
    (low,) = small_call(unproject_kernel, (shape_of(shape, BF16),), (grads, weights), extra)
    return low


def whole_weight(place_ref, own_ref, direct_ref, shared_ref, axis):
    first_row, first_core = place_ref[0, 0:1, 0:1] == 0.0, place_ref[1, 0:1, 0:1] == 0.0
    direct, shared = direct_ref[...], shared_ref[...]
    first = jnp.where(first_core, direct, shared)
    last = jnp.where(first_core, shared, direct)
    other = jnp.concatenate([first, last], axis=axis)
    own = own_ref[...]
    return jnp.where(first_row, own, other), jnp.where(first_row, other, own)


def wide_rows(value_ref, row):
    return transposed(jnp.concatenate([value_ref[2 * h + row] for h in range(8)], axis=0))


def join_kernel(has_next, place_ref, context_ref, own_ref, direct_ref, shared_ref, base_ref, gain_ref, *refs):
    if has_next:
        next_ref, normed_ref, std_ref, out_ref = refs
        base = base_ref[...].astype(F32)
    else:
        base_gain_ref, normed_ref, std_ref, low_ref = refs
        base = base_ref[...] * base_gain_ref[...]
    first, last = whole_weight(place_ref, own_ref, direct_ref, shared_ref, 0)
    mixed = base + (dot(wide_rows(context_ref, 0), first) + dot(wide_rows(context_ref, 1), last))
    normed, inverse_std = norm_parts(mixed)
    normed_ref[...] = normed
    std_ref[...] = jnp.broadcast_to(inverse_std, std_ref.shape)
    low = (normed * gain_ref[...]).astype(BF16)
    if has_next:
        store_heads(out_ref, (0.125 * dot(low, next_ref[...])).T)
    else:
        low_ref[...] = low


def norm_parts(values):
    center = values - jnp.mean(values, axis=-1, keepdims=True)
    inverse_std = lax.rsqrt(jnp.mean(center * center, axis=-1, keepdims=True) + EPSILON)
    return center * inverse_std, inverse_std


def norm_back_kernel(*refs):
    sums, lows, others = refs[0:2], refs[2:4], refs[4:6]
    gain_ref, normed_ref, std_ref, weight_ref, grad_ref, out_ref = refs[6:]
    for stream in range(2):
        at = slice(stream * BLOCK, (stream + 1) * BLOCK)
        both = lows[stream][...].astype(F32) + others[stream][...].astype(F32)
        grad_ref[at, :] = norm_back(
            sums[stream][...] + both, gain_ref[...], normed_ref[at, :], std_ref[at, 0:1]
        )
    store_heads(out_ref, dot_t(weight_ref[...], grad_ref[...].astype(BF16)))


def adapter_grads_kernel(*refs):
    second, grad_adapter, branch, adapter = refs[0:2], refs[2:4], refs[4:6], refs[6:8]
    out_ref, bias_ref = refs[8:]

    def both(pair):
        return jnp.concatenate([pair[0][...], pair[1][...]], axis=0)

    grad_adapters, branches = both(grad_adapter), both(branch)
    down = dot(transposed(both(second)), grad_adapters)
    up = 4.0 * dot(transposed(branches), both(adapter))
    half_width = down.shape[1]
    for i in range(8):
        at = slice(i * 128, (i + 1) * 128)
        out_ref[i, :, 0:half_width] = down[at].astype(BF16)
        out_ref[i, :, half_width:] = up[at].astype(BF16)
    down_bias = jnp.sum(grad_adapters.astype(F32), axis=0, keepdims=True)
    up_bias = 4.0 * jnp.sum(branches.astype(F32), axis=0, keepdims=True)
    extra = jnp.concatenate([down_bias, up_bias, jnp.zeros((1, 256), F32)], axis=1)
    pieces = [extra[:, i * 512 : (i + 1) * 512] for i in range(3)]
    bias_ref[...] = jnp.concatenate(pieces + [jnp.zeros((5, 512), F32)], axis=0)


def finish_kernel(total_ref, small_ref, down_ref, up_ref, bias_ref, prefix_ref):
    half_width = down_ref.shape[1]
    for i in range(8):
        block = total_ref[i].astype(F32)
        at = slice(i * 128, (i + 1) * 128)
        down_ref[at, :] = block[:, 0:half_width]
        up_ref[:, at] = block[:, half_width:].T
    biases = [jnp.zeros((8, 256), F32)] * 2
    for i in range(2):
        for j in range(4):
            pieces = []
            for head in range(8):
                pieces.append(small_ref[head, 16 * i : 16 * i + 16, :].astype(F32)[0:8, 64 * j : 64 * j + 64])
            prefix_ref[i, 8 * j : 8 * j + 8, :] = jnp.concatenate(pieces, axis=1)
        for head in range(8):
            biases[i] = biases[i] + small_ref[head, 16 * i : 16 * i + 16, :].astype(F32)[8:16]
    bias_ref[...] = jnp.concatenate(biases, axis=1)


def join_back_kernel(
    place_ref,
    grad_q_ref,
    own_ref,
    direct_ref,
    shared_ref,
    base_ref,
    gain_ref,
    normed_ref,
    std_ref,
    weight_ref,
    grad_ref,
    out_ref,
):
    first, last = whole_weight(place_ref, own_ref, direct_ref, shared_ref, 1)
    gradient = base_ref[...] + (
        dot_t(wide_rows(grad_q_ref, 0), first) + dot_t(wide_rows(grad_q_ref, 1), last)
    )
    grad = norm_back(gradient, gain_ref[...], normed_ref[...], std_ref[:, 0:1])
    grad_ref[...] = grad
    store_heads(out_ref, dot_t(weight_ref[...], grad.astype(BF16)))


def positions(doc_lens, counts, group):
    docs = doc_lens.shape[1]
    upto = jnp.arange(docs)[:, None] <= jnp.arange(docs)[None, :]
    ends = jnp.sum(jnp.where(upto[None], doc_lens[:, :, None], 0), axis=1)
    slots = group * 1024 + jnp.arange(1024, dtype=jnp.int32)
    passed = ends[:, :, None] <= slots[None, None, :]
    origin = (group - 1) * 1024
    start = jnp.max(jnp.where(passed, ends[:, :, None], 0), axis=1) - origin
    stop = jnp.min(jnp.where(passed, 8192, ends[:, :, None]), axis=1) - origin
    own = jnp.broadcast_to(slots[None] - origin + 1, start.shape)

    def limits(low, high):
        both = jnp.stack([low, high], axis=1).reshape(2, 2, 4, CHUNK).transpose(0, 2, 1, 3)
        return jnp.pad(both, ((0, 0), (0, 0), (0, 6), (0, 0)))

    first = start[:, ::CHUNK] // CHUNK
    self_last = jnp.broadcast_to(jnp.arange(5, 9, dtype=jnp.int32)[None], first.shape)
    cross_last = (stop[:, CHUNK - 1 :: CHUNK] + (CHUNK - 1)) // CHUNK

    def columns(last, low, high):
        ends = jnp.broadcast_to(jnp.array([[low, high]], jnp.int32), (2, 2))
        return [jnp.clip(first, low, high), jnp.clip(last, low, high), ends]

    blocks = jnp.arange(16, dtype=jnp.int32) + (group - 1) * 8
    at = blocks[:, None] == jnp.arange(64, dtype=jnp.int32)[None]
    window_counts = jnp.sum(jnp.where(at[None], counts[:, None, :], 0), axis=2)
    meta = columns(self_last, 4, 8) + columns(self_last, 0, 4) + columns(cross_last, 0, 12)
    meta += columns(cross_last, 4, 8) + columns(cross_last, 0, 4) + columns(cross_last, 8, 12)
    meta += [window_counts]
    return (jnp.concatenate(meta, axis=1), limits(start, own), limits(start, stop))


def hold(value, *earlier):
    any_space = pl.BlockSpec(memory_space=pl.ANY)
    return pl.pallas_call(
        lambda *refs: None,
        out_shape=shape_of(value.shape, value.dtype),
        in_specs=[any_space] * (1 + len(earlier)),
        out_specs=any_space,
        input_output_aliases={0: 0},
        cost_estimate=COST,
    )(value, *earlier)


def on_device(
    inputs,
    memory,
    cotangent,
    doc_lens,
    counts,
    prefix_kv,
    self_qkv,
    self_out,
    cross_q,
    cross_kv,
    cross_out,
    norm_gains,
    fc_in,
    fc_out,
    down_w,
    down_b,
    up_w,
    up_b,
):
    width = inputs.shape[2]
    rows = 2 * BLOCK
    prefix_rows = prefix_kv.shape[1]
    core, row = lax.axis_index("core"), lax.axis_index("row")
    group = lax.axis_index("y") * 2 + lax.axis_index("x_hi")
    head = lax.axis_index("z") * 2 + core
    place = jnp.broadcast_to(jnp.stack([row, core]).astype(F32)[:, None, None], (2, 1, BLOCK))
    meta, self_limits, cross_limits = positions(doc_lens, counts, group)
    prefix = lax.dynamic_slice_in_dim(prefix_kv, head * HEAD, HEAD, 2)
    prefix = jnp.pad(prefix, ((0, 0), (0, PREFIX_ROWS - prefix_rows), (0, 0)))
    gains = [norm_gains[i : i + 1] for i in range(3)]
    tokens = inputs.reshape(rows, width)
    qkv_w = jnp.transpose(self_qkv, (1, 0, 2))
    kv_w = jnp.transpose(cross_kv, (1, 0, 2))

    def share(direct, *earlier):
        held = hold(direct, *earlier)
        return held, flip(held, "core", 1)

    def fetch(weight, axis, *earlier):
        size = weight.shape[axis] // 2
        mine = lax.dynamic_slice_in_dim(weight, core * size, size, axis)
        return flip(hold(mine, *earlier) if earlier else mine, "row", 1)

    projected = project(tokens, qkv_w, True)
    own = regroup(projected)
    self_out_direct = fetch(self_out, 0)
    own_kv = own[:, HEAD:, :]
    behind = shift_groups(own_kv, 1)
    mem_projected = project(memory.reshape(rows, width), kv_w, False, (projected,))
    mem_own = regroup(hold(mem_projected, own_kv))
    mem_behind = shift_groups(mem_own, 1)
    mem_ahead = shift_groups(mem_own, -1)
    self_out_halves = share(self_out_direct, mem_own)

    self_full, self_stats = attend(
        meta,
        self_limits,
        own,
        (own,),
        (HEAD,),
        ("own",),
        prefix,
        prefix_rows,
        copies=0,
    )
    context, self_full, self_stats = attend(
        meta, self_limits, own, (behind,), (0,), ("behind",), state=(self_full, self_stats), extra=(mem_own,)
    )
    context = regroup_wide(context)
    cross_out_direct = fetch(cross_out, 0, context)
    first_normed, first_std, queries = small_call(
        partial(join_kernel, True),
        (
            shape_of((rows, width), F32),
            shape_of((rows, BLOCK), F32),
            shape_of((8, HEAD, rows), BF16),
        ),
        (place, context, self_out, *self_out_halves, tokens, gains[0], cross_q),
    )
    queries = regroup(queries)
    cross_args = (meta, cross_limits, queries, (mem_behind, mem_own, mem_ahead), (0, 0, 0), 0, "cross")
    cross_full, cross_stats = attend(
        meta,
        cross_limits,
        queries,
        (mem_own,),
        (0,),
        ("cross own",),
        copies=0,
    )
    context, cross_full, cross_stats = attend(
        meta,
        cross_limits,
        queries,
        (mem_behind, mem_ahead),
        (0, 0),
        ("cross behind", "cross ahead"),
        state=(cross_full, cross_stats),
    )
    cross_out_halves = share(cross_out_direct, cross_full)
    context = regroup_wide(context)
    second_normed, second_std, second_all = small_call(
        partial(join_kernel, False),
        (shape_of((rows, width), F32), shape_of((rows, BLOCK), F32), shape_of((rows, width), BF16)),
        (place, context, cross_out, *cross_out_halves, first_normed, gains[1], gains[0]),
    )

    streams = range(2)
    outputs, grad_sums, kept, branches = [], [], [], []
    for stream in streams:
        second_norm = second_normed[stream * BLOCK : (stream + 1) * BLOCK] * norm_gains[1]
        second_low = second_all[stream * BLOCK : (stream + 1) * BLOCK]
        hidden_act, hidden_slope = gelu_both(dot(second_low, fc_in))
        adapter_act, adapter_slope = gelu_both(dot(second_low, down_w) + down_b)
        hidden_low = hidden_act.astype(BF16)
        adapter_low = adapter_act.astype(BF16)
        kept.append((second_low, hidden_slope, adapter_low, adapter_slope, second_norm))
        low = (dot(hidden_low, fc_out) + 4.0 * dot(adapter_low, up_w)).astype(BF16)
        branches.append((low, flip(low, "row", 1)))

    grad_adapters, grad_branches, lows, others = [], [], [], []
    for stream in streams:
        second_low, hidden_slope, adapter_low, adapter_slope, second_norm = kept[stream]
        low, other = branches[stream]
        other = hold(other, lows[-1] if stream else branches[1][0])
        branch = (low.astype(F32) + other.astype(F32)) + 4.0 * up_b
        result, normed, inverse_std = norm_rows(second_norm + branch, norm_gains[2])
        outputs.append(result.astype(BF16))
        grad_sums.append(
            norm_back(cotangent[stream].astype(F32), norm_gains[2], normed, inverse_std)
        )
        grad_branch = grad_sums[stream].astype(BF16)
        grad_hidden = (dot_t(grad_branch, fc_out) * hidden_slope).astype(BF16)
        grad_adapter = (4.0 * dot_t(grad_branch, up_w) * adapter_slope).astype(BF16)
        grad_hidden, grad_adapter = lax.optimization_barrier((grad_hidden, grad_adapter))
        low = (dot_t(grad_hidden, fc_in) + dot_t(grad_adapter, down_w)).astype(BF16)
        lows.append(low)
        others.append(flip(low, "row", 1))
        grad_adapters.append(grad_adapter)
        grad_branches.append(grad_branch)

    adapters = down_w.shape[1]
    message, bias_sums = small_call(
        adapter_grads_kernel,
        (shape_of((8, 128, 512), BF16), shape_of((8, 512), F32)),
        (kept[0][0], kept[1][0], *grad_adapters, *grad_branches, kept[0][2], kept[1][2]),
        extra=(others[0], lows[1]),
    )
    adapter_part = lax.psum_scatter(message, GROUP, scatter_dimension=0, tiled=True)

    grad_crossed, grad_context = small_call(
        norm_back_kernel,
        (shape_of((rows, width), F32), shape_of((8, HEAD, rows), BF16)),
        (
            *grad_sums,
            *lows,
            *others,
            gains[1],
            second_normed,
            second_std,
            cross_out,
        ),
        extra=(message,),
    )
    grad_context = regroup(grad_context)

    cross_q_direct = fetch(cross_q, 1, grad_crossed)
    grad_q, grad_behind, grad_own, grad_ahead = attend_back(
        *cross_args, grad_context, cross_full, cross_stats, extra=(cross_q_direct,)
    )
    cross_q_halves = share(cross_q_direct, grad_own)
    grad_q = regroup_wide(grad_q)
    adapter_parts = lax.all_gather(
        hold(adapter_part, grad_own), ("y", "x_hi"), axis=0, tiled=True
    )
    mem_parts = (
        grad_own,
        shift_groups(hold(grad_behind, grad_q), -1),
        shift_groups(hold(grad_ahead, grad_q), 1),
    )
    grad_mixed, grad_context = small_call(
        join_back_kernel,
        (shape_of((rows, width), F32), shape_of((8, HEAD, rows), BF16)),
        (
            place,
            grad_q,
            cross_q,
            *cross_q_halves,
            grad_crossed,
            gains[0],
            first_normed,
            first_std,
            self_out,
        ),
    )
    grad_context = regroup(grad_context)

    grad_mem = sum(part.astype(F32) for part in mem_parts).astype(BF16)
    grad_q, packed = prefix_back(
        own, prefix, prefix_rows, grad_context, self_full, self_stats, bias_sums
    )
    parts = lax.all_to_all(packed, ("y", "x_hi"), 0, 0)
    grad_q, grad_behind = attend_back(
        meta,
        self_limits,
        own,
        (behind,),
        (0,),
        0,
        "behind",
        grad_context,
        self_full,
        self_stats,
        old=grad_q,
        copies=0,
    )
    adapter_part = jnp.sum(hold(adapter_parts, grad_behind).astype(F32), axis=0, keepdims=True)
    adapter_total = lax.all_gather(adapter_part.astype(BF16), GROUP, axis=0, tiled=True)
    returned = shift_groups(hold(grad_behind, parts), -1)
    grad_mem = hold(grad_mem, grad_behind)
    mem_recv = regroup(grad_mem)
    (message,) = attend_back(
        meta,
        self_limits,
        own,
        (own,),
        (HEAD,),
        4,
        "own",
        grad_context,
        self_full,
        self_stats,
        old=grad_q,
        copies=1,
        extra=(grad_mem,),
        message=(returned, parts),
    )
    message = hold(message, mem_recv)
    grads = regroup(message)
    mem_low = unproject(mem_recv, kv_w, (message,))
    mem_other = flip(mem_low, "row", 1)
    low = unproject(grads, qkv_w)
    other = flip(low, "row", 1)
    grad_memory = (mem_low.astype(F32) + mem_other.astype(F32)).astype(BF16)

    down_grad, up_grad, bias_grads, prefix_grad = small_call(
        finish_kernel,
        (
            shape_of((width, adapters), F32),
            shape_of((adapters, width), F32),
            shape_of((8, 512), F32),
            shape_of((2, 32, prefix_kv.shape[2]), F32),
        ),
        (adapter_total, grads[:, 3 * HEAD :]),
        extra=(low,),
    )
    bias_grads = bias_grads.reshape(-1)
    other = hold(other, down_grad)
    input_grad = (grad_mixed + (low.astype(F32) + other.astype(F32))).astype(BF16)
    return (
        jnp.stack(outputs),
        input_grad.reshape(inputs.shape),
        grad_memory.reshape(memory.shape),
        prefix_grad[:, :prefix_rows],
        down_grad,
        bias_grads[:adapters],
        up_grad,
        bias_grads[adapters : adapters + width],
    )


def solution(mesh):
    fine = Mesh(mesh.devices.reshape(4, 2, 4, 2, 2), SEQ + ("row",))
    in_specs = (
        P(None, SEQ, None),
        P(None, SEQ, None),
        P(None, SEQ, None),
        P(),
        P(),
        P(None, None, "row"),
        P(None, None, "row"),
        P("row", None),
        P(None, "row"),
        P(None, None, "row"),
        P("row", None),
        P(),
        P(None, "row"),
        P("row", None),
        P(None, "row"),
        P("row"),
        P("row", None),
        P(),
    )
    out_specs = (
        P(None, SEQ, None),
        P(None, SEQ, None),
        P(None, SEQ, None),
        P(None, None, "row"),
        P(None, "row"),
        P("row"),
        P("row", None),
        P(),
    )
    return jax.shard_map(
        on_device, mesh=fine, in_specs=in_specs, out_specs=out_specs, check_vma=False
    )
```

```python
from functools import partial

import jax
import jax.numpy as jnp
from jax import lax
from jax.experimental import pallas as pl
from jax.experimental.pallas import tpu as pltpu
from jax.sharding import Mesh
from jax.sharding import PartitionSpec as P

HEAD = 64
EPSILON = 1e-05
MASKED = -1000000000.0
CHUNK = 256
PREFIX_ROWS = 32
BLOCK = 128
SEQ = ("y", "x_hi", "z", "core")
GROUP = ("z", "core")
WIDE_GROUP = ("z", "core", "row")
BF16 = jnp.bfloat16
F32 = jnp.float32


def dot(left, right):
    return jnp.dot(left, right, preferred_element_type=F32)


def norm_rows(values, norm_gain):
    center = values - jnp.mean(values, axis=-1, keepdims=True)
    inverse_std = lax.rsqrt(jnp.mean(center * center, axis=-1, keepdims=True) + EPSILON)
    normed = center * inverse_std
    return (normed * norm_gain, normed, inverse_std)


def norm_back(gradient, norm_gain, normed, inverse_std):
    scaled = gradient * norm_gain
    centered = scaled - jnp.mean(scaled, axis=-1, keepdims=True)
    return (centered - normed * jnp.mean(scaled * normed, axis=-1, keepdims=True)) * inverse_std


def gelu_both(pre_act):
    cdf = 0.5 * (1.0 + lax.erf(pre_act * 0.7071067811865476))
    slope = cdf + pre_act * (0.3989422804014327 * jnp.exp(-0.5 * pre_act * pre_act))
    return (pre_act * cdf, slope)


def row_total(partial_sum):
    low = partial_sum.astype(BF16)
    other = lax.ppermute(low, "row", [(0, 1), (1, 0)])
    return low.astype(F32) + other.astype(F32)


def shift_groups(value, by):
    devices = 64
    pairs = [(i, i + 8 * by) for i in range(devices) if 0 <= i + 8 * by < devices]
    return lax.ppermute(value, SEQ, pairs)


def regroup(value):
    return lax.all_to_all(value, GROUP, 0, 0)


def regroup_wide(value):
    return lax.all_to_all(value, WIDE_GROUP, 0, 0)


def flip(value, axis_name, bit):
    size = lax.axis_size(axis_name)
    return lax.ppermute(value, axis_name, [(i, i ^ bit) for i in range(size)])


def transposed(value):
    return value.astype(F32).T.astype(BF16)


def allowed_keys(limits, chunk, meta_ref, batch, live):
    keys = lax.broadcasted_iota(jnp.int32, (CHUNK, CHUNK), 0)
    low = limits[0:1, :] - chunk * CHUNK
    high = limits[1:2, :] - chunk * CHUNK
    allowed = (keys >= low) & (keys < high)
    if live:
        first = meta_ref[batch, LIVE_AT + 2 * chunk]
        second = meta_ref[batch, LIVE_AT + 1 + 2 * chunk] + BLOCK
        allowed = allowed & (keys < jnp.where(keys < BLOCK, first, second))
    return allowed


def prefix_mask(prefix_rows):
    return lax.broadcasted_iota(jnp.int32, (PREFIX_ROWS, CHUNK), 0) < prefix_rows


def half(j):
    return slice((j % 2) * BLOCK, (j % 2 + 1) * BLOCK)


def by_count(meta_ref, batches, block, range_at, counts, body):
    firsts = [meta_ref[batch, range_at + block] for batch in batches]
    needs = [meta_ref[batch, range_at + 4 + block] - first for batch, first in zip(batches, firsts)]
    base, end = meta_ref[0, range_at + 8], meta_ref[0, range_at + 9]
    needed = needs[0]
    for need in needs[1:]:
        needed = jnp.maximum(needed, need)
    smaller = -1
    for count in counts:
        fits = needed <= count
        if count == counts[-1]:
            fits = needed > smaller
        elif smaller >= 0:
            fits = fits & (needed > smaller)

        @pl.when(fits)
        def _(count=count):
            body([jnp.maximum(jnp.minimum(first, end - count), base) for first in firsts], count)

        smaller = count


def lanes(batch):
    return slice(batch * BLOCK, (batch + 1) * BLOCK)


def any_lanes(batch):
    return pl.ds(pl.multiple_of(batch * BLOCK, BLOCK), BLOCK)


def each_block(count, body):
    def step(index, carry):
        body(index)
        return carry

    lax.fori_loop(0, count, step, 0)


def attend_kernel(kv_offsets, passes, live, prefix_rows, resume, copies, extra, meta_ref, limits_ref, q_ref, *refs):
    refs = refs[extra:]
    kv_count = len(kv_offsets)
    chunks = 4 * kv_count
    kv_refs = refs[:kv_count]
    refs = refs[kv_count:]
    if prefix_rows:
        prefix_k_ref, prefix_vt_ref = refs[:2]
        refs = refs[2:]
    if resume:
        total_ref, old_ref = refs[:2]
        refs = refs[2:]
    if copies:
        out_ref = refs[0]
        refs = refs[1:]
    full_ref, stats_ref, k_buf, vt_buf, qt_buf = refs

    for batch in range(2):
        for part in range(kv_count):
            start = kv_offsets[part]
            for j in range(8):
                chunk = chunks * batch + 4 * part + j // 2
                kv = kv_refs[part][j, start : start + 2 * HEAD, lanes(batch)]
                k_buf[chunk, half(j), :] = transposed(kv[:HEAD])
                vt_buf[chunk, :, half(j)] = kv[HEAD:]
        for j in range(8):
            qt_buf[4 * batch + j // 2, :, half(j)] = q_ref[j, 0:HEAD, lanes(batch)]

    def attend_pass(part, ranges):
        base = BASES[ranges]
        prefixed = prefix_rows > 0 and part == 0
        state = (full_ref, stats_ref) if part else (total_ref, old_ref) if resume else None
        finish = copies > 0 and part == kv_count - 1

        def attend_block(batch, block, first, count):
            queries = qt_buf[4 * batch + block]
            limits = limits_ref[batch, block]
            at = chunks * batch + 4 * part + first - base
            scores = []
            for i in range(count):
                found = dot(k_buf[at + i], queries)
                allowed = allowed_keys(limits, first + i, meta_ref, batch, live)
                scores.append(jnp.where(allowed, found, MASKED))
            if prefixed:
                found = dot(prefix_k_ref[...], queries)
                scores.append(jnp.where(prefix_mask(prefix_rows), found, MASKED))
            tops = [jnp.max(score, axis=0, keepdims=True) for score in scores]
            if state:
                old_top = state[1][batch, block, 0:1, :]
                tops.append(old_top)
            top = tops[0]
            for other in tops[1:]:
                top = jnp.maximum(top, other)
            weights = [jnp.exp(score - top) for score in scores]
            mass = sum(jnp.sum(weight, axis=0, keepdims=True) for weight in weights)
            total = sum(dot(vt_buf[at + i], weights[i].astype(BF16)) for i in range(count))
            if prefixed:
                total = total + dot(prefix_vt_ref[...], weights[count].astype(BF16))
            if state:
                shrink = jnp.exp(old_top - top)
                mass = mass + state[1][batch, block, 1:2, :] * shrink
                total = total + state[0][batch, block] * shrink
            if finish:
                mass = 1.0 / mass
                total = total * mass
            return top, mass, total

        def query_block(block):
            def body(firsts, count):
                found = [attend_block(batch, block, firsts[batch], count) for batch in range(2)]
                for batch in range(2):
                    top, mass, total = found[batch]
                    if finish:
                        low = total.astype(BF16)
                        for j in range(2):
                            for copy in range(copies):
                                out_ref[(2 * block + j) * copies + copy, :, lanes(batch)] = low[:, half(j)]
                    stats_ref[batch, block, 0:1, :] = top
                    stats_ref[batch, block, 1:2, :] = mass
                    full_ref[batch, block] = total

            by_count(meta_ref, (0, 1), block, RANGES[ranges], COUNTS[ranges], body)

        each_block(4, query_block)

    for part, ranges in enumerate(passes):
        attend_pass(part, ranges)


def score_grads(keys, values, queries, grads, stats, delta, allowed):
    scores = jnp.where(allowed, dot(keys, queries), MASKED)
    weights = jnp.exp(scores - stats[0:1, :]) * stats[1:2, :]
    grad_score = weights * (dot(values, grads) - delta)
    return weights.astype(BF16), grad_score.astype(BF16)


def attend_back_kernel(
    kv_offsets, base, live, resume, copies, message, range_at, counts, extra, meta_ref, limits_ref, q_ref, *refs
):
    refs = refs[extra:]
    kv_count = len(kv_offsets)
    chunks = 4 * kv_count
    kv_refs = refs[:kv_count]
    refs = refs[kv_count:]
    if resume:
        old_ref = refs[0]
        refs = refs[1:]
    grad_ref, full_ref, stats_ref = refs[:3]
    refs = refs[3:]
    if message:
        returned_ref, parts_ref, dq_ref = refs[:3]
    else:
        dq_ref, dkv_refs = refs[0], refs[1 : 1 + kv_count]
    k_buf, kt_buf, v_buf, qt_buf, gt_buf, dk_sum, dv_sum = refs[-7:]

    for batch in range(2):
        for part in range(kv_count):
            start = kv_offsets[part]
            for j in range(8):
                chunk = chunks * batch + 4 * part + j // 2
                kv = kv_refs[part][j, start : start + 2 * HEAD, lanes(batch)]
                k_buf[chunk, half(j), :] = transposed(kv[:HEAD])
                kt_buf[chunk, :, half(j)] = kv[:HEAD]
                v_buf[chunk, half(j), :] = transposed(kv[HEAD:])
        for j in range(8):
            qt_buf[4 * batch + j // 2, :, half(j)] = q_ref[j, 0:HEAD, lanes(batch)]
            gt_buf[4 * batch + j // 2, :, half(j)] = grad_ref[j, :, lanes(batch)]
    dk_sum[...] = jnp.zeros_like(dk_sum)
    dv_sum[...] = jnp.zeros_like(dv_sum)

    def query_block(index):
        batch, block = index // 4, index % 4
        queries = qt_buf[4 * batch + block]
        grads = gt_buf[4 * batch + block]
        limits = limits_ref[batch, block]
        stats = stats_ref[batch, block]

        def body(firsts, count):
            first = firsts[0]
            dq = old_ref[batch, block] if resume else jnp.zeros((HEAD, CHUNK), F32)
            if count:
                queries_r = transposed(queries)
                grads_r = transposed(grads)
                delta = jnp.sum(grads.astype(F32) * full_ref[batch, block], axis=0, keepdims=True)
            for i in range(count):
                chunk = first + i
                at = chunks * batch + chunk - base
                allowed = allowed_keys(limits, chunk, meta_ref, batch, live)
                weights, grad_score = score_grads(
                    k_buf[at], v_buf[at], queries, grads, stats, delta, allowed
                )
                dk_sum[at] += dot(grad_score, queries_r)
                dv_sum[at] += dot(weights, grads_r)
                dq = dq + dot(kt_buf[at], grad_score)
            if copies:
                low = dq.astype(BF16) * 0.125
                for j in range(2):
                    for copy in range(copies):
                        dq_ref[(2 * block + j) * copies + copy, 0:HEAD, any_lanes(batch)] = low[:, half(j)]
            else:
                dq_ref[batch, block] = dq

        by_count(meta_ref, (batch,), block, range_at, counts, body)

    each_block(8, query_block)

    for batch in range(2):
        for part in range(kv_count):
            for j in range(8):
                chunk = chunks * batch + 4 * part + j // 2
                for i, total in enumerate((dk_sum, dv_sum)):
                    turned = total[chunk, half(j), :].T
                    rows = slice(i * HEAD, (i + 1) * HEAD)
                    if message:
                        turned = turned + returned_ref[j, rows, lanes(batch)].astype(F32)
                        rows = slice((i + 1) * HEAD, (i + 2) * HEAD)
                        dq_ref[j, rows, lanes(batch)] = turned.astype(BF16)
                    else:
                        dkv_refs[part][j, rows, lanes(batch)] = turned.astype(BF16)
    if message:
        total = parts_ref[0].astype(F32)
        for group in range(1, 8):
            total = total + parts_ref[group].astype(F32)
        small = total.astype(BF16)
        for j in range(8):
            dq_ref[j, 3 * HEAD : 3 * HEAD + 16, :] = small[:, 0:256]
            dq_ref[j, 3 * HEAD + 16 : 3 * HEAD + 32, :] = small[:, 256:512]


def prefix_back_kernel(
    prefix_rows, q_ref, k_ref, kt_ref, v_ref, grad_ref, full_ref, stats_ref, bias_ref, dq_ref, out_ref
):
    dk = jnp.zeros((PREFIX_ROWS, HEAD), F32)
    dv = jnp.zeros((PREFIX_ROWS, HEAD), F32)
    for batch in range(2):
        for block in range(4):
            queries = jnp.concatenate(
                [q_ref[2 * block + j, 0:HEAD, lanes(batch)] for j in range(2)], axis=1
            )
            grads = jnp.concatenate([grad_ref[2 * block + j, :, lanes(batch)] for j in range(2)], axis=1)
            delta = jnp.sum(grads.astype(F32) * full_ref[batch, block], axis=0, keepdims=True)
            weights, grad_score = score_grads(
                k_ref[...],
                v_ref[...],
                queries,
                grads,
                stats_ref[batch, block],
                delta,
                prefix_mask(prefix_rows),
            )
            dq_ref[batch, block] = dot(kt_ref[...], grad_score)
            dk = dk + dot(grad_score, transposed(queries))
            dv = dv + dot(weights, transposed(grads))
    pieces = [value[8 * j : 8 * j + 8] for value in (dk, dv) for j in range(4)]
    small = jnp.concatenate([jnp.concatenate(pieces, axis=1), bias_ref[...]], axis=0).astype(BF16)
    for group in range(8):
        out_ref[group] = small


def pinned(*values):
    return [pltpu.with_memory_space_constraint(value, pltpu.VMEM) for value in values]


def shape_of(shape, dtype):
    return jax.ShapeDtypeStruct(shape, dtype)


COST = pl.CostEstimate(flops=1000, bytes_accessed=1000, transcendentals=0)
VMEM_LIMIT = 63 * 10**6
PARAMS = pltpu.CompilerParams(vmem_limit_bytes=VMEM_LIMIT)
IN_VMEM = pl.BlockSpec(memory_space=pltpu.VMEM)
ANYWHERE = pl.BlockSpec(memory_space=pl.ANY)

RANGES = {"own": 0, "behind": 10, "cross": 20, "cross own": 30, "cross behind": 40, "cross ahead": 50}
BASES = {"own": 4, "behind": 0, "cross": 0, "cross own": 4, "cross behind": 0, "cross ahead": 8}
LIVE_AT = 60
COUNTS = {
    "own": (1, 2, 3, 4),
    "behind": (0, 1, 2, 3, 4),
    "cross": (1, 2, 3, 4, 5, 6, 8, 10, 12),
    "cross own": (1, 2, 3, 4),
    "cross behind": (0, 1, 2, 4),
    "cross ahead": (0, 1, 2, 4),
}


def attend(meta, limits, queries, kvs, kv_offsets, passes, prefix=None, prefix_rows=0, state=None, copies=2, extra=()):
    chunks = 4 * len(kvs)
    operands = pinned(*kvs) if len(kvs) == 1 else [*kvs]
    if prefix_rows:
        operands += [prefix[0], prefix[1].T]
    if state is not None:
        operands += pinned(*state)
    state_shape = shape_of if copies else pltpu.VMEM
    out_shape = [state_shape((2, 4, HEAD, CHUNK), F32), state_shape((2, 4, 8, CHUNK), F32)]
    if copies:
        out_shape.insert(0, shape_of((8 * copies, HEAD, 2 * BLOCK), BF16))
    kernel = partial(
        attend_kernel,
        kv_offsets,
        passes,
        not passes[0].startswith("cross"),
        prefix_rows,
        state is not None,
        copies,
        len(extra),
    )
    return pl.pallas_call(
        kernel,
        out_shape=tuple(out_shape),
        in_specs=[pl.BlockSpec(memory_space=pltpu.SMEM), IN_VMEM, IN_VMEM]
        + [ANYWHERE] * len(extra)
        + [IN_VMEM] * len(operands),
        out_specs=tuple(IN_VMEM for _ in out_shape),
        scratch_shapes=[
            pltpu.VMEM((2 * chunks, CHUNK, HEAD), BF16),
            pltpu.VMEM((2 * chunks, HEAD, CHUNK), BF16),
            pltpu.VMEM((8, HEAD, CHUNK), BF16),
        ],
        compiler_params=PARAMS,
        cost_estimate=COST,
    )(meta, limits, *pinned(queries), *extra, *operands)


def attend_back(
    meta, limits, queries, kvs, kv_offsets, base, ranges, grads, full, stats, old=None, copies=2, extra=(), message=()
):
    chunks = 4 * len(kvs)
    operands = [*kvs]
    if copies:
        out_shape = [shape_of((8 * copies, HEAD, 2 * BLOCK), BF16)]
    else:
        out_shape = [shape_of((2, 4, HEAD, CHUNK), F32)]
    for _ in kvs:
        out_shape.append(shape_of((8, 2 * HEAD, 2 * BLOCK), BF16))
    if old is not None:
        operands.append(old)
    operands += [*pinned(grads), full, stats, *message]
    if message:
        out_shape = [shape_of((8, 3 * HEAD + 32, 2 * BLOCK), BF16)]
    kernel = partial(
        attend_back_kernel,
        kv_offsets,
        base,
        ranges != "cross",
        old is not None,
        copies,
        len(message) > 0,
        RANGES[ranges],
        COUNTS[ranges],
        len(extra),
    )
    return pl.pallas_call(
        kernel,
        out_shape=tuple(out_shape),
        in_specs=[pl.BlockSpec(memory_space=pltpu.SMEM), IN_VMEM, IN_VMEM]
        + [ANYWHERE] * len(extra)
        + [IN_VMEM] * len(operands),
        out_specs=tuple(IN_VMEM for _ in out_shape),
        scratch_shapes=[
            pltpu.VMEM((2 * chunks, CHUNK, HEAD), BF16),
            pltpu.VMEM((2 * chunks, HEAD, CHUNK), BF16),
            pltpu.VMEM((2 * chunks, CHUNK, HEAD), BF16),
            pltpu.VMEM((8, HEAD, CHUNK), BF16),
            pltpu.VMEM((8, HEAD, CHUNK), BF16),
            pltpu.VMEM((2 * chunks, CHUNK, HEAD), F32),
            pltpu.VMEM((2 * chunks, CHUNK, HEAD), F32),
        ],
        compiler_params=PARAMS,
        cost_estimate=COST,
    )(meta, limits, queries, *extra, *operands)


def prefix_back(queries, prefix, prefix_rows, grads, full, stats, biases):
    return pl.pallas_call(
        partial(prefix_back_kernel, prefix_rows),
        out_shape=(shape_of((2, 4, HEAD, CHUNK), F32), shape_of((8, 16, 512), BF16)),
        in_specs=[IN_VMEM] * 8,
        out_specs=(IN_VMEM, IN_VMEM),
        compiler_params=PARAMS,
        cost_estimate=COST,
    )(queries, prefix[0], prefix[0].T, prefix[1], *pinned(grads), full, stats, biases)


def dot_t(left, right):
    return lax.dot_general(left, right, (((1,), (1,)), ((), ())), preferred_element_type=F32)


def tdot(left, right):
    return lax.dot_general(left, right, (((0,), (0,)), ((), ())), preferred_element_type=F32)


def small_call(kernel, out_shape, operands, extra=()):
    specs = [IN_VMEM] * len(operands)
    specs += [pl.BlockSpec(memory_space=pl.ANY)] * len(extra)
    count = len(operands)
    return pl.pallas_call(
        lambda *refs: kernel(*refs[:count], *refs[count + len(extra) :]),
        out_shape=tuple(out_shape),
        in_specs=specs,
        out_specs=tuple(pl.BlockSpec(memory_space=pltpu.VMEM) for _ in out_shape),
        compiler_params=pltpu.CompilerParams(vmem_limit_bytes=VMEM_LIMIT),
        cost_estimate=COST,
    )(*operands, *extra)


def store_heads(out_ref, turned):
    for h in range(8):
        out_ref[h] = turned[h * HEAD : (h + 1) * HEAD].astype(BF16)


def project_kernel(scaled, x_ref, w_ref, out_ref):
    tokens = x_ref[...]
    for part in range(w_ref.shape[0]):
        y = dot(tokens, w_ref[part])
        if scaled and part == 0:
            y = y * 0.125
        turned = y.T.astype(BF16)
        for h in range(8):
            out_ref[h, part * HEAD : (part + 1) * HEAD, :] = turned[h * HEAD : (h + 1) * HEAD]


def project(tokens, weights, scaled, extra=()):
    shape = (8, weights.shape[0] * HEAD, tokens.shape[0])
    (heads,) = small_call(
        partial(project_kernel, scaled), (shape_of(shape, BF16),), (tokens, weights), extra
    )
    return heads


def unproject_kernel(grads_ref, w_ref, out_ref):
    total = None
    for part in range(w_ref.shape[0]):
        rows = slice(part * HEAD, (part + 1) * HEAD)
        turned = jnp.concatenate([grads_ref[h, rows, :] for h in range(8)], axis=0)
        value = dot_t(transposed(turned), w_ref[part])
        total = value if total is None else total + value
    out_ref[...] = total.astype(BF16)


def unproject(grads, weights, extra=()):
    shape = (grads.shape[2], weights.shape[1])
    operands = (*pinned(grads), weights)
    (low,) = small_call(unproject_kernel, (shape_of(shape, BF16),), operands, extra)
    return low


def whole_weight(place_ref, own_ref, direct_ref, shared_ref, axis):
    first_row, first_core = place_ref[0, 0:1, 0:1] == 0.0, place_ref[1, 0:1, 0:1] == 0.0
    direct, shared = direct_ref[...], shared_ref[...]
    first = jnp.where(first_core, direct, shared)
    last = jnp.where(first_core, shared, direct)
    other = jnp.concatenate([first, last], axis=axis)
    own = own_ref[...]
    return jnp.where(first_row, own, other), jnp.where(first_row, other, own)


def wide_rows(value_ref, row):
    return transposed(jnp.concatenate([value_ref[2 * h + row] for h in range(8)], axis=0))


def join_kernel(has_next, place_ref, context_ref, own_ref, direct_ref, shared_ref, base_ref, gain_ref, *refs):
    if has_next:
        next_ref, normed_ref, std_ref, out_ref = refs
        base = base_ref[...].astype(F32)
    else:
        base_gain_ref, normed_ref, std_ref, low_ref = refs
        base = base_ref[...] * base_gain_ref[...]
    first, last = whole_weight(place_ref, own_ref, direct_ref, shared_ref, 0)
    mixed = base + (dot(wide_rows(context_ref, 0), first) + dot(wide_rows(context_ref, 1), last))
    normed, inverse_std = norm_parts(mixed)
    normed_ref[...] = normed
    std_ref[...] = jnp.broadcast_to(inverse_std, std_ref.shape)
    low = (normed * gain_ref[...]).astype(BF16)
    if has_next:
        store_heads(out_ref, (0.125 * dot(low, next_ref[...])).T)
    else:
        low_ref[...] = low


def norm_parts(values):
    center = values - jnp.mean(values, axis=-1, keepdims=True)
    inverse_std = lax.rsqrt(jnp.mean(center * center, axis=-1, keepdims=True) + EPSILON)
    return center * inverse_std, inverse_std


def norm_back_kernel(*refs):
    sums, lows, others = refs[0:2], refs[2:4], refs[4:6]
    gain_ref, normed_ref, std_ref, weight_ref, grad_ref, out_ref = refs[6:]
    for stream in range(2):
        at = slice(stream * BLOCK, (stream + 1) * BLOCK)
        both = lows[stream][...].astype(F32) + others[stream][...].astype(F32)
        grad_ref[at, :] = norm_back(
            sums[stream][...] + both, gain_ref[...], normed_ref[at, :], std_ref[at, 0:1]
        )
    store_heads(out_ref, dot_t(weight_ref[...], grad_ref[...].astype(BF16)))


def adapter_grads_kernel(*refs):
    second, grad_adapter, branch, adapter = refs[0:2], refs[2:4], refs[4:6], refs[6:8]
    out_ref, bias_ref = refs[8:]

    def both(pair):
        return jnp.concatenate([pair[0][...], pair[1][...]], axis=0)

    grad_adapters, branches = both(grad_adapter), both(branch)
    down = dot(transposed(both(second)), grad_adapters)
    up = 4.0 * dot(transposed(branches), both(adapter))
    half_width = down.shape[1]
    for i in range(8):
        at = slice(i * 128, (i + 1) * 128)
        out_ref[i, :, 0:half_width] = down[at].astype(BF16)
        out_ref[i, :, half_width:] = up[at].astype(BF16)
    down_bias = jnp.sum(grad_adapters.astype(F32), axis=0, keepdims=True)
    up_bias = 4.0 * jnp.sum(branches.astype(F32), axis=0, keepdims=True)
    extra = jnp.concatenate([down_bias, up_bias, jnp.zeros((1, 256), F32)], axis=1)
    pieces = [extra[:, i * 512 : (i + 1) * 512] for i in range(3)]
    bias_ref[...] = jnp.concatenate(pieces + [jnp.zeros((5, 512), F32)], axis=0)


def finish_kernel(total_ref, small_ref, down_ref, up_ref, bias_ref, prefix_ref):
    half_width = down_ref.shape[1]
    for i in range(8):
        block = total_ref[i].astype(F32)
        at = slice(i * 128, (i + 1) * 128)
        down_ref[at, :] = block[:, 0:half_width]
        up_ref[:, at] = block[:, half_width:].T
    biases = [jnp.zeros((8, 256), F32)] * 2
    for i in range(2):
        for j in range(4):
            pieces = []
            for head in range(8):
                pieces.append(small_ref[head, 16 * i : 16 * i + 16, :].astype(F32)[0:8, 64 * j : 64 * j + 64])
            prefix_ref[i, 8 * j : 8 * j + 8, :] = jnp.concatenate(pieces, axis=1)
        for head in range(8):
            biases[i] = biases[i] + small_ref[head, 16 * i : 16 * i + 16, :].astype(F32)[8:16]
    bias_ref[...] = jnp.concatenate(biases, axis=1)


def join_back_kernel(
    place_ref,
    grad_q_ref,
    own_ref,
    direct_ref,
    shared_ref,
    base_ref,
    gain_ref,
    normed_ref,
    std_ref,
    weight_ref,
    grad_ref,
    out_ref,
):
    first, last = whole_weight(place_ref, own_ref, direct_ref, shared_ref, 1)
    gradient = base_ref[...] + (
        dot_t(wide_rows(grad_q_ref, 0), first) + dot_t(wide_rows(grad_q_ref, 1), last)
    )
    grad = norm_back(gradient, gain_ref[...], normed_ref[...], std_ref[:, 0:1])
    grad_ref[...] = grad
    store_heads(out_ref, dot_t(weight_ref[...], grad.astype(BF16)))


def positions(doc_lens, counts, group):
    docs = doc_lens.shape[1]
    upto = jnp.arange(docs)[:, None] <= jnp.arange(docs)[None, :]
    ends = jnp.sum(jnp.where(upto[None], doc_lens[:, :, None], 0), axis=1)
    slots = group * 1024 + jnp.arange(1024, dtype=jnp.int32)
    passed = ends[:, :, None] <= slots[None, None, :]
    origin = (group - 1) * 1024
    start = jnp.max(jnp.where(passed, ends[:, :, None], 0), axis=1) - origin
    stop = jnp.min(jnp.where(passed, 8192, ends[:, :, None]), axis=1) - origin
    own = jnp.broadcast_to(slots[None] - origin + 1, start.shape)

    def limits(low, high):
        both = jnp.stack([low, high], axis=1).reshape(2, 2, 4, CHUNK).transpose(0, 2, 1, 3)
        return jnp.pad(both, ((0, 0), (0, 0), (0, 6), (0, 0)))

    first = start[:, ::CHUNK] // CHUNK
    self_last = jnp.broadcast_to(jnp.arange(5, 9, dtype=jnp.int32)[None], first.shape)
    cross_last = (stop[:, CHUNK - 1 :: CHUNK] + (CHUNK - 1)) // CHUNK

    def columns(last, low, high):
        ends = jnp.broadcast_to(jnp.array([[low, high]], jnp.int32), (2, 2))
        return [jnp.clip(first, low, high), jnp.clip(last, low, high), ends]

    blocks = jnp.arange(16, dtype=jnp.int32) + (group - 1) * 8
    at = blocks[:, None] == jnp.arange(64, dtype=jnp.int32)[None]
    window_counts = jnp.sum(jnp.where(at[None], counts[:, None, :], 0), axis=2)
    meta = columns(self_last, 4, 8) + columns(self_last, 0, 4) + columns(cross_last, 0, 12)
    meta += columns(cross_last, 4, 8) + columns(cross_last, 0, 4) + columns(cross_last, 8, 12)
    meta += [window_counts]
    return (jnp.concatenate(meta, axis=1), limits(start, own), limits(start, stop))


def hold(value, *earlier):
    any_space = pl.BlockSpec(memory_space=pl.ANY)
    return pl.pallas_call(
        lambda *refs: None,
        out_shape=shape_of(value.shape, value.dtype),
        in_specs=[any_space] * (1 + len(earlier)),
        out_specs=any_space,
        input_output_aliases={0: 0},
        cost_estimate=COST,
    )(value, *earlier)


def on_device(
    inputs,
    memory,
    cotangent,
    doc_lens,
    counts,
    prefix_kv,
    self_qkv,
    self_out,
    cross_q,
    cross_kv,
    cross_out,
    norm_gains,
    fc_in,
    fc_out,
    down_w,
    down_b,
    up_w,
    up_b,
):
    width = inputs.shape[2]
    rows = 2 * BLOCK
    prefix_rows = prefix_kv.shape[1]
    core, row = lax.axis_index("core"), lax.axis_index("row")
    group = lax.axis_index("y") * 2 + lax.axis_index("x_hi")
    head = lax.axis_index("z") * 2 + core
    place = jnp.broadcast_to(jnp.stack([row, core]).astype(F32)[:, None, None], (2, 1, BLOCK))
    meta, self_limits, cross_limits = positions(doc_lens, counts, group)
    prefix = lax.dynamic_slice_in_dim(prefix_kv, head * HEAD, HEAD, 2)
    prefix = jnp.pad(prefix, ((0, 0), (0, PREFIX_ROWS - prefix_rows), (0, 0)))
    gains = [norm_gains[i : i + 1] for i in range(3)]
    tokens = inputs.reshape(rows, width)
    qkv_w = jnp.transpose(self_qkv, (1, 0, 2))
    kv_w = jnp.transpose(cross_kv, (1, 0, 2))

    def share(direct, *earlier):
        held = hold(direct, *earlier)
        return held, flip(held, "core", 1)

    def fetch(weight, axis, *earlier):
        size = weight.shape[axis] // 2
        mine = lax.dynamic_slice_in_dim(weight, core * size, size, axis)
        return flip(hold(mine, *earlier) if earlier else mine, "row", 1)

    projected = project(tokens, qkv_w, True)
    own = regroup(projected)
    self_out_direct = fetch(self_out, 0)
    own_kv = own[:, HEAD:, :]
    behind = shift_groups(own_kv, 1)
    mem_projected = project(memory.reshape(rows, width), kv_w, False, (projected,))
    mem_own = regroup(hold(mem_projected, own_kv))
    mem_behind = shift_groups(mem_own, 1)
    mem_ahead = shift_groups(mem_own, -1)
    self_out_halves = share(self_out_direct, mem_own)

    self_full, self_stats = attend(
        meta,
        self_limits,
        own,
        (own,),
        (HEAD,),
        ("own",),
        prefix,
        prefix_rows,
        copies=0,
    )
    context, self_full, self_stats = attend(
        meta, self_limits, own, (behind,), (0,), ("behind",), state=(self_full, self_stats), extra=(mem_own,)
    )
    context = regroup_wide(context)
    cross_out_direct = fetch(cross_out, 0, context)
    first_normed, first_std, queries = small_call(
        partial(join_kernel, True),
        (
            shape_of((rows, width), F32),
            shape_of((rows, BLOCK), F32),
            shape_of((8, HEAD, rows), BF16),
        ),
        (place, context, self_out, *self_out_halves, tokens, gains[0], cross_q),
    )
    queries = regroup(queries)
    cross_args = (meta, cross_limits, queries, (mem_behind, mem_own, mem_ahead), (0, 0, 0), 0, "cross")
    cross_full, cross_stats = attend(
        meta,
        cross_limits,
        queries,
        (mem_own,),
        (0,),
        ("cross own",),
        copies=0,
    )
    context, cross_full, cross_stats = attend(
        meta,
        cross_limits,
        queries,
        (mem_behind, mem_ahead),
        (0, 0),
        ("cross behind", "cross ahead"),
        state=(cross_full, cross_stats),
    )
    cross_out_halves = share(cross_out_direct, cross_full)
    context = regroup_wide(context)
    second_normed, second_std, second_all = small_call(
        partial(join_kernel, False),
        (shape_of((rows, width), F32), shape_of((rows, BLOCK), F32), shape_of((rows, width), BF16)),
        (place, context, cross_out, *cross_out_halves, first_normed, gains[1], gains[0]),
    )

    streams = range(2)
    outputs, grad_sums, kept, branches = [], [], [], []
    for stream in streams:
        second_norm = second_normed[stream * BLOCK : (stream + 1) * BLOCK] * norm_gains[1]
        second_low = second_all[stream * BLOCK : (stream + 1) * BLOCK]
        hidden_act, hidden_slope = gelu_both(dot(second_low, fc_in))
        adapter_act, adapter_slope = gelu_both(dot(second_low, down_w) + down_b)
        hidden_low = hidden_act.astype(BF16)
        adapter_low = adapter_act.astype(BF16)
        kept.append((second_low, hidden_slope, adapter_low, adapter_slope, second_norm))
        low = (dot(hidden_low, fc_out) + 4.0 * dot(adapter_low, up_w)).astype(BF16)
        branches.append((low, flip(low, "row", 1)))

    grad_adapters, grad_branches, lows, others = [], [], [], []
    for stream in streams:
        second_low, hidden_slope, adapter_low, adapter_slope, second_norm = kept[stream]
        low, other = branches[stream]
        other = hold(other, lows[-1] if stream else branches[1][0])
        branch = (low.astype(F32) + other.astype(F32)) + 4.0 * up_b
        result, normed, inverse_std = norm_rows(second_norm + branch, norm_gains[2])
        outputs.append(result.astype(BF16))
        grad_sums.append(
            norm_back(cotangent[stream].astype(F32), norm_gains[2], normed, inverse_std)
        )
        grad_branch = grad_sums[stream].astype(BF16)
        grad_hidden = (dot_t(grad_branch, fc_out) * hidden_slope).astype(BF16)
        grad_adapter = (4.0 * dot_t(grad_branch, up_w) * adapter_slope).astype(BF16)
        grad_hidden, grad_adapter = lax.optimization_barrier((grad_hidden, grad_adapter))
        low = (dot_t(grad_hidden, fc_in) + dot_t(grad_adapter, down_w)).astype(BF16)
        lows.append(low)
        others.append(flip(low, "row", 1))
        grad_adapters.append(grad_adapter)
        grad_branches.append(grad_branch)

    adapters = down_w.shape[1]
    message, bias_sums = small_call(
        adapter_grads_kernel,
        (shape_of((8, 128, 512), BF16), shape_of((8, 512), F32)),
        (kept[0][0], kept[1][0], *grad_adapters, *grad_branches, kept[0][2], kept[1][2]),
        extra=(others[0], lows[1]),
    )
    adapter_part = lax.psum_scatter(message, GROUP, scatter_dimension=0, tiled=True)

    grad_crossed, grad_context = small_call(
        norm_back_kernel,
        (shape_of((rows, width), F32), shape_of((8, HEAD, rows), BF16)),
        (
            *grad_sums,
            *lows,
            *others,
            gains[1],
            second_normed,
            second_std,
            cross_out,
        ),
        extra=(message,),
    )
    grad_context = regroup(grad_context)

    cross_q_direct = fetch(cross_q, 1, grad_crossed)
    grad_q, grad_behind, grad_own, grad_ahead = attend_back(
        *cross_args, grad_context, cross_full, cross_stats, extra=(cross_q_direct,)
    )
    cross_q_halves = share(cross_q_direct, grad_own)
    grad_q = regroup_wide(grad_q)
    adapter_parts = lax.all_gather(
        hold(adapter_part, grad_own), ("y", "x_hi"), axis=0, tiled=True
    )
    mem_parts = (
        grad_own,
        shift_groups(hold(grad_behind, grad_q), -1),
        shift_groups(hold(grad_ahead, grad_q), 1),
    )
    grad_mixed, grad_context = small_call(
        join_back_kernel,
        (shape_of((rows, width), F32), shape_of((8, HEAD, rows), BF16)),
        (
            place,
            grad_q,
            cross_q,
            *cross_q_halves,
            grad_crossed,
            gains[0],
            first_normed,
            first_std,
            self_out,
        ),
    )
    grad_context = regroup(grad_context)

    grad_mem = sum(part.astype(F32) for part in mem_parts).astype(BF16)
    grad_q, packed = prefix_back(
        own, prefix, prefix_rows, grad_context, self_full, self_stats, bias_sums
    )
    parts = lax.all_to_all(packed, ("y", "x_hi"), 0, 0)
    grad_q, grad_behind = attend_back(
        meta,
        self_limits,
        own,
        (behind,),
        (0,),
        0,
        "behind",
        grad_context,
        self_full,
        self_stats,
        old=grad_q,
        copies=0,
    )
    adapter_part = jnp.sum(hold(adapter_parts, grad_behind).astype(F32), axis=0, keepdims=True)
    adapter_total = lax.all_gather(adapter_part.astype(BF16), GROUP, axis=0, tiled=True)
    returned = shift_groups(hold(grad_behind, parts), -1)
    grad_mem = hold(grad_mem, grad_behind)
    mem_recv = regroup(grad_mem)
    (message,) = attend_back(
        meta,
        self_limits,
        own,
        (own,),
        (HEAD,),
        4,
        "own",
        grad_context,
        self_full,
        self_stats,
        old=grad_q,
        copies=1,
        extra=(grad_mem,),
        message=(returned, parts),
    )
    message = hold(message, mem_recv)
    grads = regroup(message)
    mem_low = unproject(mem_recv, kv_w, (message,))
    mem_other = flip(mem_low, "row", 1)
    low = unproject(grads, qkv_w)
    other = flip(low, "row", 1)
    grad_memory = (mem_low.astype(F32) + mem_other.astype(F32)).astype(BF16)

    down_grad, up_grad, bias_grads, prefix_grad = small_call(
        finish_kernel,
        (
            shape_of((width, adapters), F32),
            shape_of((adapters, width), F32),
            shape_of((8, 512), F32),
            shape_of((2, 32, prefix_kv.shape[2]), F32),
        ),
        (adapter_total, grads[:, 3 * HEAD :]),
        extra=(low,),
    )
    bias_grads = bias_grads.reshape(-1)
    other = hold(other, down_grad)
    input_grad = (grad_mixed + (low.astype(F32) + other.astype(F32))).astype(BF16)
    return (
        jnp.stack(outputs),
        input_grad.reshape(inputs.shape),
        grad_memory.reshape(memory.shape),
        prefix_grad[:, :prefix_rows],
        down_grad,
        bias_grads[:adapters],
        up_grad,
        bias_grads[adapters : adapters + width],
    )


def solution(mesh):
    fine = Mesh(mesh.devices.reshape(4, 2, 4, 2, 2), SEQ + ("row",))
    in_specs = (
        P(None, SEQ, None),
        P(None, SEQ, None),
        P(None, SEQ, None),
        P(),
        P(),
        P(None, None, "row"),
        P(None, None, "row"),
        P("row", None),
        P(None, "row"),
        P(None, None, "row"),
        P("row", None),
        P(),
        P(None, "row"),
        P("row", None),
        P(None, "row"),
        P("row"),
        P("row", None),
        P(),
    )
    out_specs = (
        P(None, SEQ, None),
        P(None, SEQ, None),
        P(None, SEQ, None),
        P(None, None, "row"),
        P(None, "row"),
        P("row"),
        P("row", None),
        P(),
    )
    return jax.shard_map(
        on_device, mesh=fine, in_specs=in_specs, out_specs=out_specs, check_vma=False
    )
```
